32 devices in a mesh: img: 8 (over z, y), tile: 4 (over x, core).
Axes of the slice: x: 2, y: 2, z: 4, core: 2. Of those that a mesh axis runs over, the one named last changes fastest.
Arguments:
- patches: bfloat16 [8, 1024, 768], P('img', 'tile'), may hold values from -6 to 6
- labels: int32 [8, 1024, 256], P('img', 'tile'), may hold values from 0 to 149
- heights: int32 [8], P('img'), may hold values from 49 to 64, as said below
- cls_emb: bfloat16 [150, 768], P(None, 'img'), may hold values from -6 to 6
- gain_one: bfloat16 [768], P('img'), may hold values from 0.099609375 to 1.8984375
- w_qkv: bfloat16 [768, 2304], P('img'), may hold values from -0.21875 to 0.21875
- w_out: bfloat16 [768, 768], P('img'), may hold values from -6 to 6
- gain_two: bfloat16 [768], P('img'), may hold values from 0.099609375 to 1.8984375
- w_in: bfloat16 [768, 3072], P('img'), may hold values from -0.21875 to 0.21875
- w_back: bfloat16 [3072, 768], P('img'), may hold values from -0.109375 to 0.109375
- head_gain: bfloat16 [150], replicated, may hold values from 1.5 to 4
Outputs:
- masks: bfloat16 [8, 150, 1024, 256], P('img', None, 'tile')
- patch_grad: float32 [8, 1024, 768], P('img', 'tile')
- cls_grad: float32 [150, 768], P(None, 'img')
- gain_one_grad: float32 [768], P('img')
- w_qkv_grad: float32 [768, 2304], P('img')
- w_out_grad: float32 [768, 768], P('img')
- gain_two_grad: float32 [768], P('img')
- w_in_grad: float32 [768, 3072], P('img')
- w_back_grad: float32 [3072, 768], P('img')
- head_gain_grad: float32 [150], replicated
The draws below stay inside these ranges and needn't reach their ends.
Inputs may be any that keep to these rules, and one draw needn't show every extreme that they name: `heights`: every image has more than 48 patch rows; in every draw some image has all 64.
All inputs are finite; a program needn't handle non-finite values.
Results may differ from the reference program's by a relative error of at most 0.018.
Values may be sent and summed in bfloat16 or wider, within the bound.
A program may use at most 192 MiB of HBM per device.

```python
import math
import jax
import jax.numpy as jnp
from jax import lax

D = 768
HEADS = 12
HDIM = 64
FF = 3072
NCLS = 150
WP = 16
TROWS = 16
UP = 16
HMAX = 64
PATCHES = 1024
HPIX = 1024
WPIX = 256
IMAGES = 8


def draw_heights(key, part):
    key = jax.random.fold_in(key, 7)
    first_key, second_key = jax.random.split(key)
    drawn = jax.random.randint(first_key, (IMAGES,), 3 * TROWS + 1, HMAX + 1)
    chosen = jax.random.randint(second_key, (), 0, IMAGES)
    return jnp.where(jnp.arange(IMAGES) == chosen, HMAX, drawn).astype(jnp.int32)


def place_ends(values, own_key, low, high):
    longest = values.shape.index(max(values.shape))
    spots = []
    for shift in (0, 1):
        where = [jax.random.randint(jax.random.fold_in(own_key, axis), (), 0, length) for axis, length in enumerate(values.shape)]
        where[longest] = (where[longest] + shift) % values.shape[longest]
        spots.append(tuple(where))
    return values.at[spots[0]].set(low).at[spots[1]].set(high)


def shard_levels(key, dims, pieces, least, high):
    loudness = 1.0
    for dim, blocks in pieces:
        steps = jax.random.uniform(jax.random.fold_in(jax.random.fold_in(key, 6), dim), (blocks,), jnp.float32, least / len(pieces), high / len(pieces))
        loudness = loudness * jnp.repeat(jnp.exp(steps), dims[dim] // blocks).reshape((-1,) + (1,) * (len(dims) - 1 - dim))
    return loudness


def normal_values(key, dims, scale, bound, shards=(), held_as=jnp.bfloat16):
    level = shard_levels(key, dims, shards, -0.22, 0.18) if shards else 1.0
    values = jax.random.normal(key, dims, jnp.float32) * scale * level
    return jnp.minimum(jnp.maximum(values, -bound), bound).astype(held_as)


def setup_inputs(seed: int = 0) -> dict:
    splits = jax.random.split(jax.random.key(seed), 12)
    patches = normal_values(splits[0], (IMAGES, PATCHES, D), 1.0, 6.0, ((0, 8), (1, 4)))
    labels = place_ends(jax.random.randint(splits[1], (IMAGES, HPIX, WPIX), 0, NCLS), jax.random.fold_in(splits[1], 1), 0, NCLS - 1).astype(jnp.int32)
    heights = draw_heights(jax.random.fold_in(splits[11], 71), 0)
    cls_emb = normal_values(splits[3], (NCLS, D), 1.0, 6.0, ((1, 8),))
    gain_one = jnp.clip(1.0 + 0.18 * jax.random.normal(splits[4], (D,), jnp.float32), 0.099609375, 1.8984375).astype(jnp.bfloat16)
    w_qkv = normal_values(splits[5], (D, 3 * D), D ** -0.5, 0.21875, ((0, 8),))
    w_out = normal_values(splits[6], (D, D), (max(1, D // (PATCHES + NCLS))) ** -0.5, 6.0, ((0, 8),))
    gain_two = jnp.clip(1.0 + 0.18 * jax.random.normal(splits[7], (D,), jnp.float32), 0.099609375, 1.8984375).astype(jnp.bfloat16)
    w_in = normal_values(splits[8], (D, FF), D ** -0.5, 0.21875, ((0, 8),))
    w_back = normal_values(splits[9], (FF, D), FF ** -0.5, 0.109375, ((0, 8),))
    head_gain = jnp.clip(jnp.exp(jax.random.uniform(splits[10], (NCLS,), jnp.float32, math.log(1.5), math.log(4.0))), 1.5, 4.0).astype(jnp.bfloat16)
    return {"patches": patches, "labels": labels, "heights": heights, "cls_emb": cls_emb, "gain_one": gain_one, "w_qkv": w_qkv, "w_out": w_out, "gain_two": gain_two, "w_in": w_in, "w_back": w_back, "head_gain": head_gain}


@jax.custom_vjp
def low(v):
    return lax.optimization_barrier(v.astype(jnp.bfloat16)).astype(jnp.float32)

@jax.custom_vjp
def low_back(v):
    return v

def low_keep(v):
    return (low(v), None)

def low_pass(kept, grad):
    return (grad,)

def back_keep(v):
    return (v, None)

def back_low(kept, grad):
    return (low(grad),)
low.defvjp(low_keep, low_pass)
low_back.defvjp(back_keep, back_low)

def matmul(left, right):
    return jnp.dot(left, right, precision=lax.Precision.HIGHEST, preferred_element_type=jnp.float32)

def layer_norm(value, gain):
    centre = lax.optimization_barrier(jnp.mean(value, axis=-1, keepdims=True))
    centred = value - centre
    spread = lax.optimization_barrier(jnp.mean(centred * centred, axis=-1, keepdims=True))
    return centred * lax.rsqrt(spread + 1e-05) * gain

def unit_rows(value):
    return value * lax.rsqrt(lax.optimization_barrier(jnp.sum(value * value, axis=-1, keepdims=True)) + 1e-06)

def tent_table(pixels, cells):
    place = (jnp.arange(pixels).astype(jnp.float32) + 0.5) / UP - 0.5
    place = jnp.clip(place, 0.0, cells - 1.0)
    grid_cells = jnp.arange(cells).astype(jnp.float32)
    return jnp.maximum(0.0, 1.0 - jnp.abs(place[:, None] - grid_cells[None, :]))

def upsample_grid(grid):
    return jnp.einsum('ph,hwc,qw->cpq', tent_table(HPIX, HMAX), grid, tent_table(WPIX, WP), precision=lax.Precision.HIGHEST)

def image_pass(parameters, image_rows, height, label_grid):
    cls_rows, gain_first, w_joint, w_project, gain_second, w_expand, w_reduce, gain_head = parameters
    tokens = jnp.concatenate([image_rows, cls_rows], axis=0)
    row_count = tokens.shape[0]
    h_one = low(layer_norm(tokens, gain_first))
    joint = low(low_back(matmul(h_one, w_joint)))
    queries = joint[:, :D].reshape(row_count, HEADS, HDIM)
    keys_all = joint[:, D:2 * D].reshape(row_count, HEADS, HDIM)
    values_all = joint[:, 2 * D:].reshape(row_count, HEADS, HDIM)
    positions = jnp.arange(row_count)
    key_valid = (positions // WP < height) | (positions >= PATCHES)
    scores = jnp.einsum('qhd,khd->hqk', queries, keys_all, precision=lax.Precision.HIGHEST) * HDIM ** (-0.5)
    scores = low_back(jnp.where(key_valid[None, None, :], scores, -1e+30))
    probability = low(jax.nn.softmax(scores, axis=-1))
    mixed = jnp.einsum('hqk,khd->qhd', probability, values_all, precision=lax.Precision.HIGHEST)
    mixed = low(low_back(mixed.reshape(row_count, D)))
    after_attn = tokens + low_back(matmul(mixed, w_project))
    h_two = low(layer_norm(after_attn, gain_second))
    pre_act = low_back(matmul(h_two, w_expand))
    activation = low(jax.nn.gelu(pre_act))
    final_rows = after_attn + low_back(matmul(activation, w_reduce))
    patch_unit = low(unit_rows(final_rows[:PATCHES]))
    class_unit = low(unit_rows(final_rows[PATCHES:]))
    logits = low_back(matmul(patch_unit, class_unit.T))
    normed = low(low_back(layer_norm(logits, gain_head)))
    grid = normed.reshape(HMAX, WP, NCLS)
    upsampled = upsample_grid(grid)
    largest = lax.optimization_barrier(jnp.max(upsampled, axis=0, keepdims=True))
    log_total = largest[0] + jnp.log(lax.optimization_barrier(jnp.sum(jnp.exp(upsampled - largest), axis=0)))
    class_ids = jnp.arange(NCLS)[:, None, None]
    picked = lax.optimization_barrier(jnp.sum(jnp.where(label_grid[None] == class_ids, upsampled, 0.0), axis=0))
    row_valid = (jnp.arange(HPIX) < height * UP)[:, None]
    loss_sum = jnp.sum(jnp.where(row_valid, log_total - picked, 0.0)) / (UP * UP)
    return (loss_sum, grid)

def reference(patches, labels, heights, cls_emb, gain_one, w_qkv, w_out, gain_two, w_in, w_back, head_gain):
    parameters = tuple((item.astype(jnp.float32) for item in (cls_emb, gain_one, w_qkv, w_out, gain_two, w_in, w_back, head_gain)))
    images = patches.astype(jnp.float32)

    def total_loss(images, parameters):

        def per_image(bundle):
            image_rows, height, label_grid = bundle
            return image_pass(parameters, image_rows, height, label_grid)
        losses, grids = lax.map(jax.checkpoint(per_image), (images, heights, labels))
        return (jnp.sum(losses), grids)
    loss_value, pullback, grids = jax.vjp(total_loss, images, parameters, has_aux=True)
    image_grad, grads = pullback(jnp.ones_like(loss_value))

    def mask_of(grid):
        return upsample_grid(grid).astype(jnp.bfloat16)
    masks = lax.map(mask_of, grids)
    return (masks, image_grad, grads[0], grads[1], grads[2], grads[3], grads[4], grads[5], grads[6], grads[7])
```

```python
import functools

import jax
import jax.numpy as jnp
import numpy as np
from jax import lax
from jax.experimental import pallas as pl
from jax.experimental.pallas import tpu as pltpu
from jax.sharding import PartitionSpec as P

HEADS = 12
WP = 16
UP = 16
BAND = 32
BAND_CELLS = 4
GROUP = 8


def padded_2(x, sides, width):
    for axis, dim in sides:
        devices, length = (lax.axis_size(axis), x.shape[dim])
        up = [(i, (i + 1) % devices) for i in range(devices - 1)]
        down = [(j, i) for i, j in up]
        last = lax.slice_in_dim(x, length - width, length, axis=dim)
        initial = lax.slice_in_dim(x, 0, width, axis=dim)
        before = lax.ppermute(last, axis, up)
        after = lax.ppermute(initial, axis, down)
        x = jnp.concatenate([before, x, after], axis=dim)
    return x


def product(left, right):
    return jnp.dot(left, right, preferred_element_type=jnp.float32)


def times_transposed(left, right):
    return lax.dot_general(
        left, right, (((1,), (1,)), ((), ())), preferred_element_type=jnp.float32
    )


def transposed_times(left, right):
    return lax.dot_general(
        left, right, (((0,), (0,)), ((), ())), preferred_element_type=jnp.float32
    )


def layer_norm(value, gain):
    centre = jnp.mean(value, axis=-1, keepdims=True)
    centred = value - centre
    spread = jnp.mean(centred * centred, axis=-1, keepdims=True)
    return centred * lax.rsqrt(spread + 1e-05) * gain


def unit_rows(value):
    return value * lax.rsqrt(jnp.sum(value * value, axis=-1, keepdims=True) + 1e-06)


def tent(pixels, cells, first):
    place = (np.arange(pixels) + 0.5) / UP - 0.5 - first
    return np.maximum(0.0, 1.0 - np.abs(place[:, None] - np.arange(cells)[None, :]))


def band_tables():
    across = (np.clip((np.arange(WP * UP) + 0.5) / UP - 0.5, 0, WP - 1))[None, :]
    across = np.maximum(0.0, 1.0 - np.abs(across - np.arange(WP)[:, None]))
    down = tent(BAND, BAND_CELLS, -1)
    up = np.zeros((GROUP, BAND, 2, BAND_CELLS, GROUP), np.float32)
    back = np.zeros((BAND_CELLS, GROUP, GROUP, BAND), np.float32)
    for c in range(GROUP):
        up[c, :, :, :, c] = down[:, None, :]
        back[:, c, c, :] = down.T
    up = up.reshape(GROUP * BAND, 2 * BAND_CELLS * GROUP)
    back = back.reshape(BAND_CELLS * GROUP, GROUP * BAND)
    return [jnp.asarray(t, jnp.bfloat16) for t in (across, up, back)]


def two_parts(value):
    high = value.astype(jnp.bfloat16)
    return high, (value - high.astype(jnp.float32)).astype(jnp.bfloat16)


def upsample_kernel(
    classes, bands, cell_ref, label_ref, across_ref, up_ref, back_ref, mask_ref, sum_ref,
    wide, wide_grad, powers,
):
    band = pl.program_id(0)
    groups = -(-classes // GROUP)
    tail = classes - GROUP * (groups - 1)
    rows = cell_ref.shape[0] // WP
    pixels = label_ref.shape[1]

    @pl.when(band == 0)
    def _():
        for r in range(rows):
            wide[r] = lax.dot_general(
                cell_ref[WP * r : WP * (r + 1), :], across_ref[...], (((0,), (0,)), ((), ())),
                preferred_element_type=jnp.float32,
            )
        wide_grad[...] = jnp.zeros_like(wide_grad)

    step = BAND // UP

    def forward(g, total, count):
        part = wide[pl.ds(step * band, BAND_CELLS), pl.ds(GROUP * g, GROUP), :]
        both = jnp.concatenate(two_parts(part.reshape(BAND_CELLS * GROUP, pixels)), axis=0)
        upsampled = product(up_ref[: count * BAND, :], both).reshape(count, BAND, pixels)
        mask_ref[pl.ds(GROUP * g, count)] = upsampled.astype(jnp.bfloat16)
        power = jnp.exp(upsampled)
        powers[pl.ds(GROUP * g, count)] = power
        return total + jnp.sum(power, axis=0)

    total = jnp.zeros((BAND, pixels), jnp.float32)
    for g in range(groups):
        total = forward(g, total, GROUP if g < groups - 1 else tail)
    label = label_ref[...]
    share = 1.0 / (UP * UP)
    inverse = jnp.where(label >= 0, share, 0.0) / total

    def backward(g, count):
        parts = []
        for c in range(count):
            target = jnp.where(label == GROUP * g + c, share, 0.0)
            parts.append((powers[GROUP * g + c] * inverse - target).astype(jnp.bfloat16))
        summed = product(back_ref[:, : count * BAND], jnp.concatenate(parts, axis=0))
        wide_grad[pl.ds(step * band, BAND_CELLS), pl.ds(GROUP * g, GROUP), :] += summed.reshape(
            BAND_CELLS, GROUP, pixels
        )

    for g in range(groups):
        backward(g, GROUP if g < groups - 1 else tail)

    @pl.when(band == bands - 1)
    def _():
        for r in range(rows):
            high, low = two_parts(wide_grad[r])
            sum_ref[WP * r : WP * (r + 1), :] = times_transposed(
                across_ref[...], high
            ) + times_transposed(across_ref[...], low)


def upsampled_loss(cells, label_grid, classes):
    rows, lanes = cells.shape[0] // WP, cells.shape[1]
    tile_pixels, wide_pixels = label_grid.shape
    tables = band_tables()
    bands = tile_pixels // BAND

    def whole(shape):
        return pl.BlockSpec(shape, lambda i: (0,) * len(shape))

    return pl.pallas_call(
        functools.partial(upsample_kernel, classes, bands),
        grid=(bands,),
        out_shape=(
            jax.ShapeDtypeStruct((classes, tile_pixels, wide_pixels), jnp.bfloat16),
            jax.ShapeDtypeStruct(cells.shape, jnp.float32),
        ),
        in_specs=[whole(cells.shape), pl.BlockSpec((BAND, wide_pixels), lambda i: (i, 0))]
        + [whole(t.shape) for t in tables],
        out_specs=(
            pl.BlockSpec((classes, BAND, wide_pixels), lambda i: (0, i, 0)),
            whole(cells.shape),
        ),
        scratch_shapes=[
            pltpu.VMEM((rows, lanes, wide_pixels), jnp.float32),
            pltpu.VMEM((rows, lanes, wide_pixels), jnp.float32),
            pltpu.VMEM((lanes, BAND, wide_pixels), jnp.float32),
        ],
        compiler_params=pltpu.CompilerParams(vmem_limit_bytes=56 << 20),
        name="upsampled_loss",
    )(cells, label_grid, *tables)


def forward_block(tokens, weights, key_valid):
    w_joint, w_project, w_expand, w_reduce, gain_first, gain_second = weights
    row_count, features = tokens.shape
    head_size = features // HEADS
    h_one = layer_norm(tokens, gain_first).astype(jnp.bfloat16)
    joint = product(h_one, w_joint).astype(jnp.bfloat16)
    pairs = lax.all_gather(joint[:, features:], "tile", axis=0, tiled=True)
    queries = joint[:, :features].reshape(row_count, HEADS, head_size)
    keys_all = pairs[:, :features].reshape(-1, HEADS, head_size)
    values_all = pairs[:, features:].reshape(-1, HEADS, head_size)
    scores = jnp.einsum(
        "qhd,khd->hqk", queries, keys_all, preferred_element_type=jnp.float32
    ) * head_size ** (-0.5)
    scores = jnp.where(key_valid[None, None, :], scores, -1e30)
    largest = jnp.max(scores, axis=-1, keepdims=True)
    powers = jnp.exp(scores - largest)
    probability = powers / jnp.sum(powers, axis=-1, keepdims=True)
    prob_low = probability.astype(jnp.bfloat16)
    mixed = jnp.einsum("hqk,khd->qhd", prob_low, values_all, preferred_element_type=jnp.float32)
    mixed = mixed.reshape(row_count, features).astype(jnp.bfloat16)
    after_attn = tokens + product(mixed, w_project)
    h_two = layer_norm(after_attn, gain_second).astype(jnp.bfloat16)
    pre_act = product(h_two, w_expand)
    activation = jax.nn.gelu(pre_act).astype(jnp.bfloat16)
    final_rows = after_attn + product(activation, w_reduce)
    stored = (
        h_one,
        queries,
        keys_all,
        values_all,
        probability,
        prob_low,
        mixed,
        after_attn,
        h_two,
        pre_act,
        activation,
    )
    return (final_rows, stored)


def shards(
    patches, labels, heights, cls_emb, gain_one, w_qkv, w_out, gain_two, w_in, w_back, head_gain
):
    tile_index = lax.axis_index("tile")
    tile_count = lax.axis_size("tile")
    own_rows = patches.shape[1]
    grid_rows = own_rows // WP
    classes = head_gain.shape[0]
    per_tile = -(-classes // tile_count)
    padded = per_tile * tile_count
    gathered = (
        lax.all_gather(w_qkv, "img", axis=0, tiled=True),
        lax.all_gather(w_out, "img", axis=0, tiled=True),
        lax.all_gather(w_in, "img", axis=0, tiled=True),
        lax.all_gather(w_back, "img", axis=0, tiled=True),
        lax.all_gather(gain_one, "img", axis=0, tiled=True),
        lax.all_gather(gain_two, "img", axis=0, tiled=True),
        lax.all_gather(cls_emb, "img", axis=1, tiled=True),
    )
    w_joint, w_project, w_expand, w_reduce, gain_first, gain_second, cls_full = gathered
    features = w_project.shape[1]
    head_size = features // HEADS
    gain_first = gain_first.astype(jnp.float32)
    gain_second = gain_second.astype(jnp.float32)
    weights = (w_joint, w_project, w_expand, w_reduce, gain_first, gain_second)
    cls_padded = jnp.pad(cls_full, ((0, padded - classes), (0, 0)))
    cls_rows = lax.dynamic_slice_in_dim(cls_padded, tile_index * per_tile, per_tile, 0)
    tokens = jnp.concatenate([patches[0], cls_rows], axis=0).astype(jnp.float32)
    row_count = own_rows + per_tile
    height = heights[0]
    key_index = jnp.arange(tile_count * row_count)
    key_owner = key_index // row_count
    key_place = key_index % row_count
    key_valid = jnp.where(
        key_place < own_rows,
        key_owner * grid_rows + key_place // WP < height,
        key_owner * per_tile + key_place - own_rows < classes,
    )
    final_rows, stored = forward_block(tokens, weights, key_valid)
    patch_final = final_rows[:own_rows]
    class_final = final_rows[own_rows:]
    patch_unit = unit_rows(patch_final).astype(jnp.bfloat16)
    class_unit = unit_rows(class_final).astype(jnp.bfloat16)
    class_all = lax.all_gather(class_unit, "tile", axis=0, tiled=True)[:classes]
    logits = times_transposed(patch_unit, class_all)
    gain_head = head_gain.astype(jnp.float32)
    normed = layer_norm(logits, gain_head).astype(jnp.bfloat16)
    grid = normed.reshape(grid_rows, WP, classes)
    rimmed = padded_2(grid, (("tile", 0),), 1)
    tile_pixels = grid_rows * UP
    pixel_limit = height * UP - tile_index * tile_pixels
    counted = jnp.arange(tile_pixels) < pixel_limit
    label_grid = jnp.where(counted[:, None], labels[0], -1)
    first = tile_index == 0
    last = tile_index == tile_count - 1
    rimmed = rimmed.at[0].set(jnp.where(first, rimmed[1], rimmed[0]))
    rimmed = rimmed.at[-1].set(jnp.where(last, rimmed[-2], rimmed[-1]))
    lanes = -(-classes // 16) * 16
    cells = jnp.pad(rimmed.reshape(-1, classes), ((0, 0), (0, lanes - classes)))
    mask_buffer, cell_sums = upsampled_loss(cells, label_grid, classes)
    rim_grad = cell_sums[:, :classes].reshape(grid_rows + 2, WP, classes)
    rim_pair = jnp.stack([rim_grad[0], rim_grad[-1]], axis=0)
    incoming = padded_2(rim_pair, (("tile", 0),), 1)
    grid_grad = rim_grad[1:-1]
    grid_grad = grid_grad.at[0].add(jnp.where(first, rim_grad[0], incoming[0]))
    grid_grad = grid_grad.at[-1].add(jnp.where(last, rim_grad[-1], incoming[-1]))
    normed_grad = lax.optimization_barrier(
        grid_grad.reshape(own_rows, classes).astype(jnp.bfloat16)
    ).astype(jnp.float32)
    unused, norm_head_back = jax.vjp(layer_norm, logits, gain_head)
    logit_grad, head_grad = norm_head_back(normed_grad)
    head_total = lax.psum(head_grad, ("img", "tile"))
    logit_low = logit_grad.astype(jnp.bfloat16)
    patch_unit_grad = product(logit_low, class_all)
    class_part = transposed_times(logit_low, patch_unit)
    class_part = jnp.pad(class_part, ((0, padded - classes), (0, 0)))
    class_unit_grad = lax.psum_scatter(class_part, "tile", scatter_dimension=0, tiled=True)
    unused, patch_norm_back = jax.vjp(unit_rows, patch_final)
    unused, class_norm_back = jax.vjp(unit_rows, class_final)
    final_grad = jnp.concatenate(
        [patch_norm_back(patch_unit_grad)[0], class_norm_back(class_unit_grad)[0]], axis=0
    )
    (
        h_one,
        queries,
        keys_all,
        values_all,
        probability,
        prob_low,
        mixed,
        after_attn,
        h_two,
        pre_act,
        activation,
    ) = stored
    branch_low = final_grad.astype(jnp.bfloat16)
    w_back_grad = transposed_times(activation, branch_low)
    act_grad = times_transposed(branch_low, w_reduce)
    unused, gelu_back = jax.vjp(jax.nn.gelu, pre_act)
    pre_low = gelu_back(act_grad)[0].astype(jnp.bfloat16)
    w_in_grad = transposed_times(h_two, pre_low)
    h_two_grad = times_transposed(pre_low, w_expand)
    unused, norm_two_back = jax.vjp(layer_norm, after_attn, gain_second)
    after_part, gain_two_grad = norm_two_back(h_two_grad)
    after_grad = final_grad + after_part
    attn_low = after_grad.astype(jnp.bfloat16)
    w_out_grad = transposed_times(mixed, attn_low)
    mixed_low = (
        times_transposed(attn_low, w_project)
        .astype(jnp.bfloat16)
        .reshape(row_count, HEADS, head_size)
    )
    prob_grad = jnp.einsum(
        "qhd,khd->hqk", mixed_low, values_all, preferred_element_type=jnp.float32
    )
    value_grad = jnp.einsum("hqk,qhd->khd", prob_low, mixed_low, preferred_element_type=jnp.float32)
    score_low = (
        probability * (prob_grad - jnp.sum(probability * prob_grad, axis=-1, keepdims=True))
    ).astype(jnp.bfloat16)
    score_scale = head_size ** (-0.5)
    query_grad = (
        jnp.einsum("hqk,khd->qhd", score_low, keys_all, preferred_element_type=jnp.float32)
        * score_scale
    )
    key_grad = (
        jnp.einsum("hqk,qhd->khd", score_low, queries, preferred_element_type=jnp.float32)
        * score_scale
    )
    pair_grad = jnp.concatenate(
        [key_grad.reshape(-1, features), value_grad.reshape(-1, features)], axis=1
    )
    own_pairs = lax.psum_scatter(
        pair_grad.astype(jnp.bfloat16), "tile", scatter_dimension=0, tiled=True
    ).astype(jnp.float32)
    joint_low = jnp.concatenate(
        [query_grad.reshape(row_count, features), own_pairs], axis=1
    ).astype(jnp.bfloat16)
    w_qkv_grad = transposed_times(h_one, joint_low)
    h_one_grad = times_transposed(joint_low, w_joint)
    unused, norm_one_back = jax.vjp(layer_norm, tokens, gain_first)
    token_part, gain_one_grad = norm_one_back(h_one_grad)
    token_grad = after_grad + token_part
    patch_grad = token_grad[:own_rows][None]
    class_rows_grad = lax.dynamic_update_slice_in_dim(
        jnp.zeros((padded, features), jnp.float32), token_grad[own_rows:], tile_index * per_tile, 0
    )[:classes]
    shares = (
        lax.psum_scatter(w_qkv_grad, "img", scatter_dimension=0, tiled=True),
        lax.psum_scatter(w_out_grad, "img", scatter_dimension=0, tiled=True),
        lax.psum_scatter(gain_one_grad, "img", scatter_dimension=0, tiled=True),
        lax.psum_scatter(class_rows_grad, "img", scatter_dimension=1, tiled=True),
        lax.psum_scatter(w_in_grad, "img", scatter_dimension=0, tiled=True),
        lax.psum_scatter(w_back_grad, "img", scatter_dimension=0, tiled=True),
        lax.psum_scatter(gain_two_grad, "img", scatter_dimension=0, tiled=True),
    )
    totals = (
        lax.psum(shares[0].astype(jnp.bfloat16), "tile").astype(jnp.float32),
        lax.psum(shares[1].astype(jnp.bfloat16), "tile").astype(jnp.float32),
        lax.psum(shares[2].astype(jnp.bfloat16), "tile").astype(jnp.float32),
        lax.psum(shares[3].astype(jnp.bfloat16), "tile").astype(jnp.float32),
        lax.psum(shares[4].astype(jnp.bfloat16), "tile").astype(jnp.float32),
        lax.psum(shares[5].astype(jnp.bfloat16), "tile").astype(jnp.float32),
        lax.psum(shares[6].astype(jnp.bfloat16), "tile").astype(jnp.float32),
    )
    return (
        mask_buffer[None],
        patch_grad,
        totals[3],
        totals[2],
        totals[0],
        totals[1],
        totals[6],
        totals[4],
        totals[5],
        head_total,
    )


def solution(mesh):
    in_specs = (
        P("img", "tile", None),
        P("img", "tile", None),
        P("img"),
        P(None, "img"),
        P("img"),
        P("img", None),
        P("img", None),
        P("img"),
        P("img", None),
        P("img", None),
        P(),
    )
    out_specs = (
        P("img", None, "tile", None),
        P("img", "tile", None),
        P(None, "img"),
        P("img"),
        P("img", None),
        P("img", None),
        P("img"),
        P("img", None),
        P("img", None),
        P(),
    )
    return jax.shard_map(shards, mesh=mesh, in_specs=in_specs, out_specs=out_specs, check_vma=False)
```

```python
import collections
import functools
import types

import jax
import jax.numpy as jnp
import numpy as np
from jax import lax
from jax.experimental import pallas as pl
from jax.experimental.pallas import tpu as pltpu
from jax.sharding import PartitionSpec as P

IMG = "img"
TILE = "tile"
HEADS = 12
WP = 16
UP = 16
BAND = 32
BAND_CELLS = 4
GROUP = 8
MESH = pl.DeviceIdType.MESH
F32 = jnp.float32
BF16 = jnp.bfloat16
PLANE = 2
BACK, INTO, JOINT = 0, 1, 2
VMEM_BYTES = 62 << 20


def product(left, right):
    return jnp.dot(left, right, preferred_element_type=F32)


def times_transposed(left, right):
    return lax.dot_general(left, right, (((1,), (1,)), ((), ())), preferred_element_type=F32)


def transposed_times(left, right):
    return lax.dot_general(left, right, (((0,), (0,)), ((), ())), preferred_element_type=F32)


def layer_norm_parts(value):
    centre = jnp.mean(value, axis=-1, keepdims=True)
    centred = value - centre
    spread = jnp.mean(centred * centred, axis=-1, keepdims=True)
    scale = lax.rsqrt(spread + 1e-05)
    return centred * scale, scale


def layer_norm_back(unit, scale, gain, upstream):
    weighted = upstream * gain
    mean = jnp.mean(weighted, axis=-1, keepdims=True)
    along = jnp.mean(weighted * unit, axis=-1, keepdims=True)
    gain_row = jnp.sum(upstream * unit, axis=0, keepdims=True)
    return scale * (weighted - mean - unit * along), gain_row


def gelu_pair(x):
    root = np.float32(np.sqrt(2.0 / np.pi))
    square = x * x
    turned = jnp.tanh(root * x * (1.0 + np.float32(0.044715) * square))
    half = 0.5 * (1.0 + turned)
    slope = half + 0.5 * x * (1.0 - turned * turned) * root * (
        1.0 + np.float32(3 * 0.044715) * square
    )
    return x * half, slope


def lane_iota(rows, lanes):
    return lax.broadcasted_iota(jnp.int32, (rows, lanes), 1)


def row_iota(rows, lanes):
    return lax.broadcasted_iota(jnp.int32, (rows, lanes), 0)


class Net:
    def __init__(self, k):
        self.k = k
        self.sent = []
        self.stage_sends = []

    def send(self, source, target, base, slot, device, when=None):
        k = self.k
        copy = pltpu.make_async_remote_copy(
            src_ref=source,
            dst_ref=target,
            send_sem=k.send_sem.at[len(self.sent)],
            recv_sem=k.recv_sem.at[base + slot],
            device_id=device,
            device_id_type=MESH,
        )
        self.sent.append((copy, when))
        if when is None:
            copy.start()
        else:
            pl.when(when)(copy.start)
        return len(self.sent) - 1

    def arrived(self, target, base, slot):
        k = self.k
        pltpu.make_async_remote_copy(
            src_ref=target,
            dst_ref=target,
            send_sem=k.send_sem.at[0],
            recv_sem=k.recv_sem.at[base + slot],
            device_id=k.sibling,
            device_id_type=MESH,
        ).wait_recv()

    def gone(self, number):
        if self.sent[number] is None:
            return
        copy, when = self.sent[number]
        self.sent[number] = None
        if when is None:
            copy.wait_send()
        else:
            pl.when(when)(copy.wait_send)

    def drain(self):
        for number in range(len(self.sent)):
            self.gone(number)


def place(k):
    k.i = lax.axis_index(IMG)
    k.t = lax.axis_index(TILE)
    k.y = k.i % PLANE
    k.z = k.i // PLANE
    k.planes = k.s.images // PLANE
    k.ts = k.t + 1 - 2 * (k.t % 2)
    k.tx = (k.t + 2) % 4
    k.td = (k.ts + 2) % 4
    k.sibling = (k.i, k.ts)
    k.across = (k.i, k.tx)
    k.diagonal = (k.i, k.td)
    k.mate = (k.i + 1 - 2 * k.y, k.t)


def line_peer(k, step):
    z = (k.z + step) % k.planes
    return z, (PLANE * z + k.y, k.t)


def enter(k):
    barrier = pltpu.get_barrier_semaphore()
    peers = [k.sibling, k.across, k.diagonal]
    if k.s.img_comm:
        peers += [k.mate] + [line_peer(k, step)[1] for step in range(1, k.planes)]
    for peer in peers:
        pl.semaphore_signal(barrier, inc=1, device_id=peer, device_id_type=MESH)
    pl.semaphore_wait(barrier, len(peers))


def spread_start(k, own, slots, name):
    for step in range(1, k.planes):
        k.net.send(own, slots.at[k.i], name, k.i, line_peer(k, step)[1])
    k.net.send(own, slots.at[k.i], name, k.i, k.mate)


def spread_pass(k, slots, name):
    for step in range(1, k.planes):
        z = (k.z + k.planes - step) % k.planes
        i = PLANE * z + k.y
        k.net.arrived(slots.at[i], name, i)
        k.net.send(slots.at[i], slots.at[i], name, i, k.mate)


def spread_end(k, slots, name):
    for z in range(k.planes):
        i = PLANE * z + 1 - k.y
        k.net.arrived(slots.at[i], name, i)


def slot_part(slots, slot, rows):
    return slots.at[slot] if rows is None else slots.at[slot, rows]


def share_start(k, slots, base, rows=None):
    own = slot_part(slots, k.t, rows)
    k.net.send(own, own, base, k.t, k.across)
    k.net.send(own, own, base, k.t, k.sibling)


def share_pass(k, slots, base, rows=None):
    part = slot_part(slots, k.tx, rows)
    k.net.arrived(part, base, k.tx)
    k.net.send(part, part, base, k.tx, k.sibling)


def reduce_over_tile(k, name, part, before):
    sends = k.net.stage_sends
    for number in sends:
        k.net.gone(number)
    sends.clear()
    k.own_part[...] = part(k.t)
    before(k.ts)
    k.stage[0] = part(k.ts).astype(BF16)
    sends.append(k.net.send(k.stage.at[0], k.from_sib.at[0], name, 0, k.sibling))
    before(k.tx)
    k.across_part[...] = part(k.tx)
    before(k.td)
    k.stage[1] = part(k.td).astype(BF16)
    sends.append(k.net.send(k.stage.at[1], k.from_sib.at[1], name, 1, k.sibling))
    k.net.arrived(k.from_sib.at[1], name, 1)
    k.stage[2] = (k.across_part[...] + k.from_sib[1].astype(F32)).astype(BF16)
    sends.append(k.net.send(k.stage.at[2], k.from_across, name, 2, k.across))


def reduced_over_tile(k, name):
    k.net.arrived(k.from_sib.at[0], name, 0)
    k.net.arrived(k.from_across, name, 2)
    return k.own_part[...] + k.from_sib[0].astype(F32) + k.from_across[...].astype(F32)


def key_bias(k, slot, height):
    s = k.s
    rows = row_iota(s.rows, s.head)
    cls = rows - s.own
    patch_ok = (rows < s.own) & (rows < (height - slot * s.grid) * WP)
    class_ok = (cls >= 0) & (cls < s.step) & (slot * s.step + cls < s.classes)
    off = jnp.where(patch_ok | class_ok, 0.0, -1e30)
    return jnp.where(lane_iota(s.rows, s.head) == 0, off, 0.0)


def class_rows(k, slot):
    s = k.s
    rows = k.cls_rows[pl.ds(pl.multiple_of(slot * s.step, 8), s.step), :]
    return jnp.concatenate([rows, jnp.zeros((s.slot - s.step, s.dim), F32)], axis=0)


def slot_rows(k, slot):
    return pl.ds(pl.multiple_of(slot * k.s.rows, 16), k.s.rows)


def block_scores(k, head, slot):
    return times_transposed(k.q[head, slot_rows(k, slot), :], k.keys[head])


def deal_start(k, own, slots, base):
    mine = k.z == k.t

    @pl.when(mine)
    def _():
        slots[k.t, k.y] = own[...]

    for step in range(1, k.planes):
        k.net.send(own, slots.at[k.t, k.y], base, 0, line_peer(k, step)[1], mine)


def deal_pass(k, slots, base):
    @pl.when(k.z != k.t)
    def _():
        k.net.arrived(slots.at[k.t, k.y], base, 0)

    k.net.send(slots.at[k.t, k.y], slots.at[k.t, k.y], base, 1, k.mate)


def deal_end(k, slots, base):
    k.net.arrived(slots.at[k.t, 1 - k.y], base, 1)


def pick_columns(k):
    s = k.s
    wide, part = s.here * s.head, s.hidden // s.images
    for n in range(4):

        @pl.when(k.t == n)
        def _(n=n):
            cut = [
                k.w_qkv[:, s.dim * m + wide * n + s.head * h :][:, : s.head]
                for h in range(s.here)
                for m in range(3)
            ]
            k.wq[...] = jnp.concatenate(cut, axis=1)
            cut = [k.w_in[:, part * (4 * i + n) :][:, :part] for i in range(s.images)]
            k.wi[...] = jnp.concatenate(cut, axis=1)


def forward_kernel(k):
    s = k.s
    place(k)
    net = k.net
    i, t = k.i, k.t
    head_gain = k.gain_row[...].astype(F32)
    head_gain = jnp.concatenate([head_gain, jnp.zeros((1, s.lanes - s.classes), F32)], axis=1)
    k.head_gain[...] = jnp.broadcast_to(head_gain, (8, s.lanes))
    if s.img_comm:
        shard = s.dim // s.images
        rows = [ref[...].astype(F32) for ref in (k.cls_emb, k.gain_one, k.gain_two)]
        rows += [jnp.zeros((s.lanes - s.classes - 2, shard), F32)]
        table = jnp.concatenate(rows, axis=0)
        table = jnp.concatenate([table, jnp.zeros((s.lanes, 128 - shard), F32)], axis=1)
        k.small[...] = table.astype(BF16)
        k.smalls[i] = table.astype(BF16)
        pick_columns(k)
    enter(k)
    if s.img_comm:
        spread_start(k, k.small, k.smalls, k.at.small)
    k.tokens[t] = k.patches[0]
    net.send(k.patches.at[0], k.tokens.at[t], k.at.tokens, t, k.across)
    net.send(k.patches.at[0], k.tokens.at[t], k.at.tokens, t, k.sibling)
    if s.img_comm:
        spread_start(k, k.wq, k.w_joint, k.at.w_joint)
        k.w_joint[i] = k.wq[...]
        k.w_expand[i] = k.wi[...]
        k.w_reduce[i] = k.wb[t]
        spread_pass(k, k.smalls, k.at.small)
        spread_end(k, k.smalls, k.at.small)
        pieces = [k.smalls[n].astype(F32)[:, :shard] for n in range(s.images)]
        full = jnp.concatenate(pieces, axis=1)
    else:
        full = k.small_full[...].astype(F32)
    k.gains[0:2] = full[s.classes : s.classes + 2]
    k.cls_rows[...] = jnp.where(row_iota(s.lanes, s.dim) < s.classes, full, 0.0)
    gain_one, gain_two = k.gains[0:1], k.gains[1:2]

    def normed_tokens(slot):
        value = jnp.concatenate([k.tokens[slot].astype(F32), class_rows(k, slot)], axis=0)
        k.h_one[slot] = (layer_norm_parts(value)[0] * gain_one).astype(BF16)

    k.token_rows[0 : s.own] = k.patches[0].astype(F32)
    k.token_rows[s.own : s.rows] = class_rows(k, t)
    normed_tokens(t)
    net.arrived(k.tokens.at[k.ts], k.at.tokens, k.ts)
    normed_tokens(k.ts)
    net.arrived(k.tokens.at[k.tx], k.at.tokens, k.tx)
    net.send(k.tokens.at[k.tx], k.tokens.at[k.tx], k.at.tokens, k.tx, k.sibling)
    normed_tokens(k.tx)
    if s.img_comm:
        spread_pass(k, k.w_joint, k.at.w_joint)
        deal_start(k, k.wo, k.w_project, k.at.w_project)
        spread_start(k, k.wi, k.w_expand, k.at.w_expand)
    net.arrived(k.tokens.at[k.td], k.at.tokens, k.td)
    normed_tokens(k.td)
    if s.img_comm:
        spread_end(k, k.w_joint, k.at.w_joint)

    lane = lane_iota(s.rows, s.head)
    one = jnp.where(lane == 0, 1.0, 0.0)
    ones = jnp.where(lane < 2, 1.0, 0.0)
    height = k.height[0]

    def joint(slot, carry):
        value = product(k.h_one[slot], k.w_joint[...].reshape(s.dim, s.here * 3 * s.head))
        bias = key_bias(k, slot, height)
        rows = slot_rows(k, slot)
        for h in range(s.here):
            cut = [
                value[:, (3 * h + n) * s.head : (3 * h + n + 1) * s.head] for n in range(3)
            ]
            for ref, part, extra in zip(
                (k.q, k.keys, k.values), (cut[0] * s.head**-0.5, cut[1], cut[2]), (one, bias, ones)
            ):
                ref[h, rows, :] = jnp.concatenate([part, extra], axis=1).astype(BF16)
        return carry

    lax.fori_loop(0, 4, joint, 0)

    def attend(slot):
        rows = slot_rows(k, slot)
        wide_lane = lane_iota(s.rows, 2 * s.head)
        parts = []
        for h in range(s.here):
            scores = block_scores(k, h, slot)
            largest = jnp.max(scores, axis=-1, keepdims=True)
            powers = jnp.exp(scores - largest).astype(BF16)
            out = product(powers, k.values[h])
            parts.append(out[:, : s.head] / out[:, s.head : s.head + 1])
            k.outs[h, rows, :] = jnp.where(wide_lane == s.head + 1, largest, out)
        k.mixed[slot] = jnp.concatenate(parts, axis=1).astype(BF16)

    for step in range(1, 5):
        slot = (t + step) % 4
        attend(slot)
        if step < 4:
            net.send(k.mixed.at[slot], k.mixed_all.at[t], k.at.mixed, t, (i, slot))
        if s.img_comm:
            if step == 2:
                deal_pass(k, k.w_project, k.at.w_project)
            if step == 3:
                spread_start(k, k.wb.at[t], k.w_reduce, k.at.w_reduce)
    k.mixed_all[t] = k.mixed[t]
    if s.img_comm:
        deal_end(k, k.w_project, k.at.w_project)
        share_start(k, k.w_project, k.at.w_shared)
        spread_pass(k, k.w_expand, k.at.w_expand)
        share_pass(k, k.w_project, k.at.w_shared)
        net.arrived(k.w_project.at[k.ts], k.at.w_shared, k.ts)
        net.arrived(k.w_project.at[k.td], k.at.w_shared, k.td)
    after = k.token_rows[...]
    w_project = k.w_project[...].reshape(s.dim, s.dim)
    for step in range(1, 4):
        slot = (t + step) % 4
        net.arrived(k.mixed_all.at[slot], k.at.mixed, slot)
    wide = s.here * s.head
    for n in range(4):
        after = after + product(k.mixed_all[n], w_project[wide * n : wide * (n + 1)])
    k.after[...] = after
    k.h_two[t] = (layer_norm_parts(after)[0] * gain_two).astype(BF16)
    share_start(k, k.h_two, k.at.h_two)
    if s.img_comm:
        spread_end(k, k.w_expand, k.at.w_expand)
        spread_pass(k, k.w_reduce, k.at.w_reduce)
        spread_end(k, k.w_reduce, k.at.w_reduce)

    def feed(slot):
        pre = product(k.h_two[slot], k.w_expand[...].reshape(s.dim, s.hidden))
        act, slope = gelu_pair(pre)
        act = act.astype(BF16)
        k.act[slot] = act
        k.slope[slot] = slope.astype(BF16)
        return product(act, k.w_reduce[...].reshape(s.hidden, s.dim))

    def ready(slot):
        if slot is k.tx:
            share_pass(k, k.h_two, k.at.h_two)
        else:
            net.arrived(k.h_two.at[slot], k.at.h_two, slot)

    reduce_over_tile(k, k.at.feed, feed, ready)
    final = k.after[...] + reduced_over_tile(k, k.at.feed)
    k.final[...] = final
    unit = (final * lax.rsqrt(jnp.sum(final * final, axis=-1, keepdims=True) + 1e-06)).astype(BF16)
    k.cls_units[t] = unit[s.own :]
    k.patch_unit[WP : WP + s.own] = unit[: s.own]
    top, bottom = pl.ds(0, WP), pl.ds(WP + s.own, WP)
    for slot in (k.tx, k.td, k.ts):
        net.send(k.cls_units.at[t], k.cls_units.at[t], k.at.units, t, (i, slot))
    net.send(k.patch_unit.at[pl.ds(WP, WP)], k.patch_unit.at[bottom], k.at.rim, 1, (i, (t + 3) % 4))
    net.send(k.patch_unit.at[pl.ds(s.own, WP)], k.patch_unit.at[top], k.at.rim, 0, (i, (t + 1) % 4))
    for slot in (k.ts, k.tx, k.td):
        net.arrived(k.cls_units.at[slot], k.at.units, slot)
    net.arrived(k.patch_unit.at[top], k.at.rim, 0)
    net.arrived(k.patch_unit.at[bottom], k.at.rim, 1)
    units = jnp.concatenate([k.cls_units[n].astype(F32)[: s.step] for n in range(4)], axis=0)
    units = jnp.where(row_iota(s.lanes, s.dim) < s.classes, units, 0.0).astype(BF16)
    k.class_unit[...] = units
    logits = times_transposed(k.patch_unit[...], units)
    unit_logits, scale = class_norm_parts(k, logits)
    k.logit_unit[...] = unit_logits[WP : WP + s.own]
    k.logit_scale[...] = jnp.broadcast_to(scale[WP : WP + s.own], (s.own, 128))
    normed = (unit_logits * k.head_gain[0:1]).astype(BF16)
    k.cells[WP : WP + s.own] = normed[WP : WP + s.own]
    k.cells[:WP] = jnp.where(t == 0, normed[WP : 2 * WP], normed[:WP])
    k.cells[WP + s.own :] = jnp.where(t == 3, normed[s.own : WP + s.own], normed[WP + s.own :])
    net.drain()


def class_norm_parts(k, value):
    s = k.s
    real = lane_iota(value.shape[0], s.lanes) < s.classes
    centre = jnp.sum(value, axis=-1, keepdims=True) / s.classes
    centred = jnp.where(real, value - centre, 0.0)
    spread = jnp.sum(centred * centred, axis=-1, keepdims=True) / s.classes
    scale = lax.rsqrt(spread + 1e-05)
    return centred * scale, scale


def sum_start(k, name):
    g = k.grads[name]
    k.net.send(g.blocks.at[1 - k.y], g.from_mate, g.at_mate, 0, k.mate)


def sum_pass(k, name):
    g = k.grads[name]
    k.net.arrived(g.from_mate, g.at_mate, 0)
    for step in range(k.planes):
        z = (k.z + step) % k.planes
        both = g.blocks[k.y, z].astype(F32) + g.from_mate[z].astype(F32)
        g.both[z] = both.astype(BF16)
        if step:
            k.net.send(g.both.at[z], g.from_line.at[k.z], g.at_line, k.z, line_peer(k, step)[1])


def sum_end(k, name):
    g = k.grads[name]
    total = g.both[k.z].astype(F32)
    for step in range(1, k.planes):
        z = (k.z + step) % k.planes
        k.net.arrived(g.from_line.at[z], g.at_line, z)
        total = total + g.from_line[z].astype(F32)
    g.out[k.t] = total.astype(BF16)
    share_start(k, g.out, g.at_out)


def sum_share(k, name):
    g = k.grads[name]
    share_pass(k, g.out, g.at_out)


def sum_close(k, name):
    g = k.grads[name]
    k.net.arrived(g.out.at[k.ts], g.at_out, k.ts)
    k.net.arrived(g.out.at[k.td], g.at_out, k.td)


def put_blocks(k, name, value):
    g = k.grads[name]
    if not k.s.img_comm:
        g.out[...] = value.astype(BF16)
        return
    rows = value.shape[0] // k.s.images
    for i in range(k.s.images):
        g.blocks[i % PLANE, i // PLANE] = value[rows * i : rows * (i + 1)].astype(BF16)


def backward_kernel(k):
    s = k.s
    place(k)
    enter(k)
    net = k.net
    i, t = k.i, k.t
    comm = s.img_comm
    patch_part, class_part = pl.ds(0, s.own), pl.ds(s.own, s.slot)

    net.send(k.cell_sums.at[0:WP], k.rim_in.at[1], k.at.rim, 1, (i, (t + 3) % 4))
    net.send(k.cell_sums.at[WP + s.own : 2 * WP + s.own], k.rim_in.at[0], k.at.rim, 0, (i, (t + 1) % 4))
    net.arrived(k.rim_in.at[0], k.at.rim, 0)
    net.arrived(k.rim_in.at[1], k.at.rim, 1)
    top = jnp.where(t == 0, k.cell_sums[:WP], k.rim_in[0])
    bottom = jnp.where(t == 3, k.cell_sums[WP + s.own :], k.rim_in[1])
    own = k.cell_sums[WP : WP + s.own]
    own = jnp.concatenate(
        [own[:WP] + top, own[WP : s.own - WP], own[s.own - WP :] + bottom], axis=0
    )
    upstream = own.astype(BF16).astype(F32)
    unit, scale = k.logit_unit[...], k.logit_scale[:, :1]
    weighted = upstream * k.head_gain[0:1]
    mean = jnp.sum(weighted, axis=-1, keepdims=True) / s.classes
    along = jnp.sum(weighted * unit, axis=-1, keepdims=True) / s.classes
    head_row = jnp.sum(upstream * unit, axis=0, keepdims=True)
    d_logits = scale * (weighted - mean - unit * along)
    d_logits = jnp.where(lane_iota(s.own, s.lanes) < s.classes, d_logits, 0.0).astype(BF16)
    d_class = transposed_times(d_logits, k.patch_unit[WP : WP + s.own])
    for n in range(4):
        k.class_out[n] = jnp.concatenate(
            [d_class[s.step * n : s.step * (n + 1)], jnp.zeros((s.slot - s.step, s.dim), F32)], axis=0
        ).astype(BF16)
    for slot in (k.ts, k.tx, k.td):
        net.send(k.class_out.at[slot], k.class_in.at[t], k.at.class_, t, (i, slot))
    final = k.final[...]
    c = lax.rsqrt(jnp.sum(final * final, axis=-1, keepdims=True) + 1e-06)
    u = final * c

    def unit_back(rows, du):
        return c[rows] * (du - u[rows] * jnp.sum(u[rows] * du, axis=-1, keepdims=True))

    d_patch = unit_back(slice(0, s.own), product(d_logits, k.class_unit[...]))
    k.d_rows[: s.own] = d_patch
    k.d_branch[t, : s.own] = d_patch.astype(BF16)
    share_start(k, k.d_branch, k.at.d_branch, patch_part)
    d_class_unit = k.class_out[t].astype(F32)
    for slot in (k.ts, k.tx, k.td):
        net.arrived(k.class_in.at[slot], k.at.class_, slot)
        d_class_unit = d_class_unit + k.class_in[slot].astype(F32)
    d_class = unit_back(slice(s.own, s.rows), d_class_unit)
    k.d_rows[s.own :] = d_class
    k.d_branch[t, s.own :] = d_class.astype(BF16)
    share_start(k, k.d_branch, k.at.d_class, class_part)

    def feed_back(slot):
        d_act = times_transposed(k.d_branch[slot], k.w_reduce[...].reshape(s.hidden, s.dim))
        d_pre = (d_act * k.slope[slot].astype(F32)).astype(BF16)
        k.d_pre[slot] = d_pre
        return times_transposed(d_pre, k.w_expand[...].reshape(s.dim, s.hidden))

    def ready(slot):
        if slot is k.tx:
            share_pass(k, k.d_branch, k.at.d_branch, patch_part)
            share_pass(k, k.d_branch, k.at.d_class, class_part)
        else:
            net.arrived(k.d_branch.at[slot, patch_part], k.at.d_branch, slot)
            net.arrived(k.d_branch.at[slot, class_part], k.at.d_class, slot)

    reduce_over_tile(k, k.at.feed, feed_back, ready)
    tall = 4 * s.rows
    put_blocks(
        k,
        BACK,
        transposed_times(k.act[...].reshape(tall, s.hidden), k.d_branch[...].reshape(tall, s.dim)),
    )
    if comm:
        sum_start(k, BACK)
    put_blocks(
        k,
        INTO,
        transposed_times(k.h_two[...].reshape(tall, s.dim), k.d_pre[...].reshape(tall, s.hidden)),
    )
    if comm:
        sum_start(k, INTO)

    unit, scale = layer_norm_parts(k.after[...])
    part, gain_two_row = layer_norm_back(unit, scale, k.gains[1:2], reduced_over_tile(k, k.at.feed))
    d_after = k.d_rows[...] + part
    k.d_rows[...] = d_after
    d_attn = d_after.astype(BF16)
    k.d_attn[t] = d_attn
    wide = s.here * s.head
    w_project = k.w_project[...].reshape(s.dim, s.dim)
    for n in range(4):
        k.d_mixed_out[n] = times_transposed(d_attn, w_project[wide * n : wide * (n + 1)]).astype(BF16)
    k.d_mixed[t] = k.d_mixed_out[t]
    for slot in (k.tx, k.td, k.ts):
        net.send(k.d_mixed_out.at[slot], k.d_mixed.at[t], k.at.d_mixed, t, (i, slot))
    share_start(k, k.d_attn, k.at.d_attn)
    if comm:
        sum_pass(k, BACK)

    for h in range(s.here):

        def block(slot):
            rows = slot_rows(k, slot)
            out = k.outs[h, rows, :]
            inverse = 1.0 / out[:, s.head : s.head + 1]
            largest = out[:, s.head + 1 : s.head + 2]
            powers = jnp.exp(block_scores(k, h, slot) - largest).astype(BF16)
            k.powers[rows, :] = powers
            d_mixed = k.d_mixed[slot][:, s.head * h : s.head * (h + 1)].astype(F32)
            scaled = (d_mixed * inverse).astype(BF16).astype(F32)
            along = jnp.sum(scaled * out[:, : s.head], axis=-1, keepdims=True) * inverse
            high = along.astype(BF16).astype(F32)
            lane = lane_iota(s.rows, s.head)
            tail = jnp.where(lane == 0, -high, jnp.where(lane == 1, high - along, 0.0))
            left = jnp.concatenate([scaled, tail], axis=1).astype(BF16)
            k.d_out[rows, :] = left
            d_scores = (powers.astype(F32) * times_transposed(left, k.values[h])).astype(BF16)
            k.d_scores[rows, :] = d_scores
            k.d_q[rows, :] = product(d_scores, k.keys[h])

        for slot in (t, k.ts, k.tx, k.td):
            if h == 0 and slot is not t:
                net.arrived(k.d_mixed.at[slot], k.at.d_mixed, slot)
            block(slot)
        d_k = transposed_times(k.q[h][:, : s.head], k.d_scores[...])
        d_v = transposed_times(k.d_out[:, : s.head], k.powers[...])
        k.d_joint[h] = jnp.concatenate(
            [k.d_q[:, : s.head] * s.head**-0.5, d_k.T, d_v.T], axis=1
        ).astype(BF16)
        put_blocks(
            k,
            JOINT + h,
            transposed_times(k.h_one[...].reshape(tall, s.dim), k.d_joint[h]),
        )
        if comm:
            sum_start(k, JOINT + h)
        if h == 0:
            share_pass(k, k.d_attn, k.at.d_attn)
            if comm:
                sum_pass(k, INTO)
        if h == 1:
            net.arrived(k.d_attn.at[k.ts], k.at.d_attn, k.ts)
            net.arrived(k.d_attn.at[k.td], k.at.d_attn, k.td)
            d_project = transposed_times(
                k.mixed[...].reshape(tall, wide), k.d_attn[...].reshape(tall, s.dim)
            )
            if comm:
                shard = s.dim // s.images
                for y in range(PLANE):
                    k.project_out[y] = d_project[shard * y : shard * (y + 1)].astype(BF16)
                net.send(k.project_out.at[1 - k.y], k.project_mate, k.at.project_mate, 0, k.mate)
                sum_pass(k, JOINT)
                sum_end(k, BACK)
            else:
                k.d_project[...] = d_project.astype(BF16)

    w_joint = k.w_joint[...].reshape(s.dim, 3 * wide)

    def joint_back(slot):
        rows = slot_rows(k, slot)
        left = jnp.concatenate([k.d_joint[h, rows, :] for h in range(s.here)], axis=1)
        return times_transposed(left, w_joint)

    reduce_over_tile(k, k.at.joint, joint_back, lambda slot: None)

    if comm:
        sum_pass(k, JOINT + 1)
        sum_end(k, INTO)
        sum_share(k, BACK)
        sum_pass_project(k)
        sum_pass(k, JOINT + 2)
        sum_end(k, JOINT)

    unit, scale = layer_norm_parts(k.token_rows[...])
    part, gain_one_row = layer_norm_back(unit, scale, k.gains[0:1], reduced_over_tile(k, k.at.joint))
    d_tokens = k.d_rows[...] + part
    k.patch_grad[0] = d_tokens[: s.own]

    rows = row_iota(s.slot, s.dim)
    table = jnp.where(rows < s.step, d_tokens[s.own :], 0.0)
    table = jnp.where(rows == s.step, gain_one_row, table)
    table = jnp.where(rows == s.step + 1, gain_two_row, table)
    rows = row_iota(s.slot, 128)
    head_rows = jnp.where(rows == s.step + 2, head_row[:, :128], 0.0)
    rest = jnp.concatenate(
        [head_row[:, 128:], jnp.zeros((1, 256 - s.lanes), F32)], axis=1
    )
    head_rows = jnp.where(rows == s.step + 3, rest, head_rows)
    if not comm:
        k.small_out[...] = table
        k.head_out[...] = head_rows
        net.drain()
        return
    pad = jnp.zeros((s.slot, 128 - shard), F32)
    for n in range(s.images):
        cut = table[:, shard * n : shard * (n + 1)]
        k.small_out[n] = jnp.concatenate([cut, pad], axis=1) + head_rows
    for step in range(1, s.images):
        n = (i + step) % s.images
        net.send(k.small_out.at[n], k.small_in.at[i], k.at.small, i, (n, t))
    sum_share(k, INTO)
    total = k.small_out[i]
    for step in range(1, s.images):
        n = (i + step) % s.images
        net.arrived(k.small_in.at[n], k.at.small, n)
        total = total + k.small_in[n]
    k.small_sum[t] = total
    for slot in (k.ts, k.tx, k.td):
        net.send(k.small_sum.at[t], k.small_sum.at[t], k.at.small_sum, t, (i, slot))
    sum_end(k, JOINT + 1)
    sum_end_project(k)
    sum_end(k, JOINT + 2)
    for h in range(s.here):
        sum_share(k, JOINT + h)
    write_gradients(k)
    net.drain()


def write_gradients(k):
    s = k.s
    shard = s.dim // s.images
    for name in range(len(k.grads)):
        sum_close(k, name)
    for n in range(4):
        k.d_w_back[shard * n : shard * (n + 1)] = k.grads[BACK].out[n].astype(F32)
    part = s.hidden // s.images
    cut = [k.grads[INTO].out[n].astype(F32) for n in range(4)]
    cut = [cut[n][:, part * i : part * (i + 1)] for i in range(s.images) for n in range(4)]
    k.d_w_in[...] = jnp.concatenate(cut, axis=1)
    for m in range(3):
        cut = [
            k.grads[JOINT + h].out[n].astype(F32)[:, s.head * m : s.head * (m + 1)]
            for n in range(4)
            for h in range(s.here)
        ]
        k.d_w_qkv[:, s.dim * m : s.dim * (m + 1)] = jnp.concatenate(cut, axis=1)
    k.d_w_out[...] = k.d_project[...].astype(F32)
    for slot in (k.ts, k.tx, k.td):
        k.net.arrived(k.small_sum.at[slot], k.at.small_sum, slot)
    rows = jnp.concatenate([k.small_sum[n][: s.step] for n in range(4)], axis=0)
    k.d_cls[...] = rows[: s.classes, :shard]
    rest = k.small_sum[0] + k.small_sum[1] + k.small_sum[2] + k.small_sum[3]
    k.d_gains[...] = rest[s.step : s.step + 8]


def sum_pass_project(k):
    net = k.net
    net.arrived(k.project_mate, k.at.project_mate, 0)
    both = k.project_out[k.y].astype(F32) + k.project_mate[...].astype(F32)
    k.project_both[...] = both.astype(BF16)
    net.send(
        k.project_both, k.project_line.at[k.z], k.at.project_line, k.z, (PLANE * k.t + k.y, k.t), k.z != k.t
    )


def sum_end_project(k):
    net = k.net
    mine = k.z == k.t

    @pl.when(mine)
    def _():
        total = k.project_both[...].astype(F32)
        for step in range(1, k.planes):
            z = (k.z + step) % k.planes
            net.arrived(k.project_line.at[z], k.at.project_line, z)
            total = total + k.project_line[z].astype(F32)
        k.d_project[...] = total.astype(BF16)

    for step in range(1, 4):
        slot = (k.t + step) % 4
        net.send(k.d_project, k.d_project, k.at.project, 0, (k.i, slot), mine)

    @pl.when(jnp.logical_not(mine))
    def _():
        net.arrived(k.d_project, k.at.project, 0)


def tent(pixels, cells, first):
    place = (np.arange(pixels) + 0.5) / UP - 0.5 - first
    return np.maximum(0.0, 1.0 - np.abs(place[:, None] - np.arange(cells)[None, :]))


def band_tables():
    across = (np.clip((np.arange(WP * UP) + 0.5) / UP - 0.5, 0, WP - 1))[None, :]
    across = np.maximum(0.0, 1.0 - np.abs(across - np.arange(WP)[:, None]))
    down = tent(BAND, BAND_CELLS, -1)
    up = np.zeros((GROUP, BAND, 2, BAND_CELLS, GROUP), np.float32)
    back = np.zeros((BAND_CELLS, GROUP, GROUP, BAND), np.float32)
    for c in range(GROUP):
        up[c, :, :, :, c] = down[:, None, :]
        back[:, c, c, :] = down.T
    up = up.reshape(GROUP * BAND, 2 * BAND_CELLS * GROUP)
    back = back.reshape(BAND_CELLS * GROUP, GROUP * BAND)
    return [jnp.asarray(t, BF16) for t in (across, up, back)]


def two_parts(value):
    high = value.astype(BF16)
    return high, (value - high.astype(F32)).astype(BF16)


def upsample_kernel(
    classes, bands, height_ref, cell_ref, label_ref, across_ref, up_ref, back_ref, mask_ref, sum_ref,
    wide, wide_grad, powers,
):
    band = pl.program_id(0)
    groups = -(-classes // GROUP)
    tail = classes - GROUP * (groups - 1)
    rows = cell_ref.shape[0] // WP
    pixels = label_ref.shape[2]

    @pl.when(band == 0)
    def _():
        for r in range(rows):
            wide[r] = lax.dot_general(
                cell_ref[WP * r : WP * (r + 1), :], across_ref[...], (((0,), (0,)), ((), ())),
                preferred_element_type=F32,
            )
        wide_grad[...] = jnp.zeros_like(wide_grad)

    step = BAND // UP

    def forward(g, total, count):
        part = wide[pl.ds(step * band, BAND_CELLS), pl.ds(GROUP * g, GROUP), :]
        both = jnp.concatenate(two_parts(part.reshape(BAND_CELLS * GROUP, pixels)), axis=0)
        upsampled = product(up_ref[: count * BAND, :], both).reshape(count, BAND, pixels)
        mask_ref[pl.ds(GROUP * g, count)] = upsampled.astype(BF16)
        power = jnp.exp(upsampled)
        powers[pl.ds(GROUP * g, count)] = power
        return total + jnp.sum(power, axis=0)

    total = jnp.zeros((BAND, pixels), F32)
    for g in range(groups):
        total = forward(g, total, GROUP if g < groups - 1 else tail)
    pixel_rows = lax.broadcasted_iota(jnp.int32, (BAND, pixels), 0) + BAND * band
    limit = (height_ref[0] - lax.axis_index(TILE) * (bands * BAND // UP)) * UP
    label = jnp.where(pixel_rows < limit, label_ref[0], -1)
    share = 1.0 / (UP * UP)
    inverse = jnp.where(label >= 0, share, 0.0) / total

    def backward(g, count):
        parts = []
        for c in range(count):
            target = jnp.where(label == GROUP * g + c, share, 0.0)
            parts.append((powers[GROUP * g + c] * inverse - target).astype(BF16))
        summed = product(back_ref[:, : count * BAND], jnp.concatenate(parts, axis=0))
        wide_grad[pl.ds(step * band, BAND_CELLS), pl.ds(GROUP * g, GROUP), :] += summed.reshape(
            BAND_CELLS, GROUP, pixels
        )

    for g in range(groups):
        backward(g, GROUP if g < groups - 1 else tail)

    @pl.when(band == bands - 1)
    def _():
        for r in range(rows):
            high, low = two_parts(wide_grad[r])
            sum_ref[WP * r : WP * (r + 1), :] = times_transposed(
                across_ref[...], high
            ) + times_transposed(across_ref[...], low)


def upsampled_loss(cells, labels, heights, classes):
    rows, lanes = cells.shape[0] // WP, cells.shape[1]
    tile_pixels, wide_pixels = labels.shape[1:]
    tables = band_tables()
    bands = tile_pixels // BAND

    def whole(shape):
        return pl.BlockSpec(shape, lambda i: (0,) * len(shape))

    return pl.pallas_call(
        functools.partial(upsample_kernel, classes, bands),
        grid=(bands,),
        out_shape=(
            jax.ShapeDtypeStruct((classes, tile_pixels, wide_pixels), BF16),
            jax.ShapeDtypeStruct(cells.shape, F32),
        ),
        in_specs=[
            pl.BlockSpec(memory_space=pltpu.SMEM),
            whole(cells.shape),
            pl.BlockSpec((1, BAND, wide_pixels), lambda i: (0, i, 0)),
        ]
        + [whole(t.shape) for t in tables],
        out_specs=(
            pl.BlockSpec((classes, BAND, wide_pixels), lambda i: (0, i, 0)),
            whole(cells.shape),
        ),
        scratch_shapes=[
            pltpu.VMEM((rows, lanes, wide_pixels), F32),
            pltpu.VMEM((rows, lanes, wide_pixels), F32),
            pltpu.VMEM((lanes, BAND, wide_pixels), F32),
        ],
        compiler_params=pltpu.CompilerParams(vmem_limit_bytes=56 << 20),
        name=upsample_kernel.__name__,
    )(heights, cells, labels, *tables)


CELLS = "cells"
GRAD_REFS = ("out", "blocks", "from_mate", "both", "from_line")
GRAD_PLACES = ("at_mate", "at_line", "at_out")
Grad = collections.namedtuple("Grad", GRAD_REFS + GRAD_PLACES)


def run_kernel(body, s, inputs, outputs, scratch, recv, sends, number):
    names_in, names_out, names_scratch = list(inputs), list(outputs), list(scratch)

    places = types.SimpleNamespace()
    arrivals = 0
    for name, count in recv.items():
        setattr(places, name, arrivals)
        arrivals += count

    def kernel(*refs):
        k = types.SimpleNamespace(s=s, at=places)
        for name, ref in zip(names_in + names_out + names_scratch, refs):
            setattr(k, name, ref)
        k.send_sem, k.recv_sem = refs[-2:]
        k.net = Net(k)
        k.grads = []
        for n in range(JOINT + s.here):
            of = [getattr(k, word + str(n), None) for word in GRAD_REFS]
            at = [getattr(places, word + str(n), None) for word in GRAD_PLACES]
            k.grads.append(Grad(*of, *at))
        body(k)

    def space(name):
        scalar = name in inputs and inputs[name].ndim == 1
        return pl.BlockSpec(memory_space=pltpu.SMEM if scalar else pltpu.VMEM)

    results = pl.pallas_call(
        kernel,
        out_shape=[jax.ShapeDtypeStruct(*outputs[n]) for n in names_out],
        in_specs=[space(n) for n in names_in],
        out_specs=[space(n) for n in names_out],
        scratch_shapes=[pltpu.VMEM(*scratch[n]) for n in names_scratch]
        + [pltpu.SemaphoreType.DMA((sends,)), pltpu.SemaphoreType.DMA((arrivals,))],
        compiler_params=pltpu.CompilerParams(
            collective_id=number, has_side_effects=True, vmem_limit_bytes=VMEM_BYTES
        ),
        name=body.__name__,
    )(*inputs.values())
    return dict(zip(names_out, results))


def reduce_scratch(s):
    return dict(
        stage=((3, s.rows, s.dim), BF16),
        from_sib=((2, s.rows, s.dim), BF16),
        from_across=((s.rows, s.dim), BF16),
        own_part=((s.rows, s.dim), F32),
        across_part=((s.rows, s.dim), F32),
    )


def forward_call(s, inputs):
    wide = s.here * s.head
    all_rows = 4 * s.rows
    outputs = dict(
        h_one=((4, s.rows, s.dim), BF16),
        q=((s.here, all_rows, 2 * s.head), BF16),
        keys=((s.here, all_rows, 2 * s.head), BF16),
        values=((s.here, all_rows, 2 * s.head), BF16),
        outs=((s.here, all_rows, 2 * s.head), F32),
        mixed=((4, s.rows, wide), BF16),
        token_rows=((s.rows, s.dim), F32),
        after=((s.rows, s.dim), F32),
        h_two=((4, s.rows, s.dim), BF16),
        act=((4, s.rows, s.hidden), BF16),
        slope=((4, s.rows, s.hidden), BF16),
        final=((s.rows, s.dim), F32),
        patch_unit=((s.own + 2 * WP, s.dim), BF16),
        head_gain=((8, s.lanes), F32),
        class_unit=((s.lanes, s.dim), BF16),
        logit_unit=((s.own, s.lanes), F32),
        logit_scale=((s.own, 128), F32),
        cells=((s.own + 2 * WP, s.lanes), BF16),
        gains=((8, s.dim), F32),
    )
    scratch = dict(
        tokens=((4, s.own, s.dim), BF16),
        cls_rows=((s.lanes, s.dim), F32),
        mixed_all=((4, s.rows, wide), BF16),
        cls_units=((4, s.slot, s.dim), BF16),
        **reduce_scratch(s),
    )
    recv = dict(tokens=4, mixed=4, h_two=4, feed=3, units=4, rim=2)
    sends = 3 + 3 + 3 + 3 + 3 + 2
    if s.img_comm:
        shard = s.dim // s.images
        outputs.update(w_joint=((s.images, shard, 3 * wide), BF16))
        outputs.update(w_project=((4, PLANE, shard, s.dim), BF16))
        scratch.update(small=((s.lanes, 128), BF16), wq=((shard, 3 * wide), BF16))
        scratch.update(wi=((shard, s.hidden), BF16))
        outputs.update(w_expand=((s.images, shard, s.hidden), BF16))
        outputs.update(w_reduce=((s.images, shard, s.dim), BF16))
        scratch.update(smalls=((s.images, s.lanes, 128), BF16))
        n = s.images
        recv.update(small=n, w_joint=n, w_project=2, w_shared=4, w_expand=n, w_reduce=n)
        sends += 4 * (2 * (n // PLANE) - 1) + n // PLANE + 3
    return run_kernel(forward_kernel, s, inputs, outputs, scratch, recv, sends, 1)


def backward_call(s, inputs):
    wide = s.here * s.head
    all_rows = 4 * s.rows
    outputs = dict(patch_grad=((1, s.own, s.dim), F32))
    scratch = dict(
        rim_in=((2, WP, s.lanes), F32),
        class_out=((4, s.slot, s.dim), BF16),
        class_in=((4, s.slot, s.dim), BF16),
        d_rows=((s.rows, s.dim), F32),
        d_branch=((4, s.rows, s.dim), BF16),
        d_pre=((4, s.rows, s.hidden), BF16),
        d_attn=((4, s.rows, s.dim), BF16),
        d_mixed_out=((4, s.rows, wide), BF16),
        d_mixed=((4, s.rows, wide), BF16),
        powers=((all_rows, all_rows), BF16),
        d_scores=((all_rows, all_rows), BF16),
        d_out=((all_rows, 2 * s.head), BF16),
        d_q=((all_rows, 2 * s.head), F32),
        d_joint=((s.here, all_rows, 3 * s.head), BF16),
        **reduce_scratch(s),
    )
    recv = dict(rim=2, class_=4, d_branch=4, d_class=4, feed=3, d_mixed=4, d_attn=4, joint=3)
    sends = 2 + 3 + 3 + 3 + 3 + 3 + 3 + 3
    columns = [s.dim, s.hidden] + [3 * s.head] * s.here
    planes, shard = s.images // PLANE, s.dim // s.images
    for n, cols in enumerate(columns):
        out, blocks, from_mate, both, from_line = [word + str(n) for word in GRAD_REFS]
        at_mate, at_line, at_out = [word + str(n) for word in GRAD_PLACES]
        if not s.img_comm:
            outputs[out] = ((s.dim, cols), BF16)
            continue
        scratch[out] = ((4, shard, cols), BF16)
        scratch[blocks] = ((PLANE, planes, shard, cols), BF16)
        for what in (from_mate, both, from_line):
            scratch[what] = ((planes, shard, cols), BF16)
        recv[at_mate] = 1
        recv[at_line] = planes
        recv[at_out] = 4
        sends += 1 + planes - 1 + 3
    if s.img_comm:
        outputs.update(d_w_back=((4 * shard, s.dim), F32))
        outputs.update(d_w_in=((shard, 4 * s.hidden), F32))
        outputs.update(d_w_qkv=((shard, 12 * wide), F32))
        outputs.update(d_w_out=((shard, s.dim), F32))
        outputs.update(d_cls=((s.classes, shard), F32))
        outputs.update(d_gains=((8, 128), F32))
        scratch.update(d_project=((shard, s.dim), BF16))
        scratch.update(small_sum=((4, s.slot, 128), F32))
        scratch.update(project_out=((PLANE, shard, s.dim), BF16))
        scratch.update(project_mate=((shard, s.dim), BF16))
        scratch.update(project_both=((shard, s.dim), BF16))
        scratch.update(project_line=((planes, shard, s.dim), BF16))
        scratch.update(small_out=((s.images, s.slot, 128), F32))
        scratch.update(small_in=((s.images, s.slot, 128), F32))
        recv.update(project_mate=1, project_line=planes, project=1, small=s.images, small_sum=4)
        sends += 1 + 1 + 3 + s.images - 1 + 3
    else:
        outputs.update(d_project=((wide, s.dim), BF16))
        outputs.update(small_out=((s.slot, s.dim), F32))
        outputs.update(head_out=((s.slot, 128), F32))
    return run_kernel(backward_kernel, s, inputs, outputs, scratch, recv, sends, 2)


def sizes(patches, cls_emb, w_joint, w_back, head_gain):
    images, tiles = lax.axis_size(IMG), lax.axis_size(TILE)
    s = types.SimpleNamespace(images=images, tiles=tiles)
    s.dim = patches.shape[2]
    s.own = patches.shape[1]
    s.grid = s.own // WP
    s.classes = head_gain.shape[0]
    s.step = -(-s.classes // (8 * tiles)) * 8
    s.slot = -(-s.step // 16) * 16
    s.lanes = s.step * tiles
    s.rows = s.own + s.slot
    s.head = s.dim // HEADS
    s.here = HEADS // tiles
    s.hidden = w_back.shape[0] * images // tiles
    shard = w_joint.shape[0]
    s.img_comm = images == PLANE * tiles and shard % 16 == 0 and shard <= 128
    return s


def shards(
    patches, labels, heights, cls_emb, gain_one, w_qkv, w_out, gain_two, w_in, w_back, head_gain
):
    s = sizes(patches, cls_emb, w_qkv, w_back, head_gain)
    t = lax.axis_index(TILE)
    shard = w_qkv.shape[0]
    wide = s.here * s.head

    part = w_back.shape[0] // s.tiles
    w_back = w_back.reshape(s.tiles, part, s.dim)
    cls_emb, gain_one, gain_two = cls_emb, gain_one[None], gain_two[None]
    inputs = dict(patches=patches, height=heights, gain_row=head_gain[None])
    common = {}
    if s.img_comm:
        inputs.update(cls_emb=cls_emb, gain_one=gain_one, gain_two=gain_two)
        inputs.update(w_qkv=w_qkv, wo=w_out, w_in=w_in, wb=w_back)
    else:

        def gather(value, axis=0):
            return lax.all_gather(value, IMG, axis=axis, tiled=True)

        def pick(value, axis):
            return lax.dynamic_index_in_dim(value, t, axis, keepdims=False)

        joint = pick(w_qkv.reshape(shard, 3, s.tiles, s.here, s.head), 2)
        joint = joint.transpose(0, 2, 1, 3).reshape(shard, 3 * wide)
        expand = pick(w_in.reshape(shard, s.images, s.tiles, part), 2).reshape(shard, s.hidden)
        reduce = pick(w_back, 0)
        small = jnp.concatenate([cls_emb, gain_one, gain_two], axis=0)
        small = jnp.pad(small, ((0, s.lanes - small.shape[0]), (0, 0)))
        common.update(
            w_joint=gather(joint)[None],
            w_project=gather(w_out)[None],
            w_expand=gather(expand)[None],
            w_reduce=gather(reduce)[None],
        )
        inputs.update(small_full=gather(small, 1), **common)
    kept = forward_call(s, inputs)
    cells = kept.pop(CELLS)
    masks, cell_sums = upsampled_loss(cells, labels, heights, s.classes)
    grads = backward_call(s, dict(**kept, **common, cell_sums=cell_sums))
    grads = types.SimpleNamespace(**grads)
    if s.img_comm:
        head_grad = grads.d_gains[2:4].reshape(-1)[: s.classes]
        return (
            masks[None],
            grads.patch_grad,
            grads.d_cls,
            grads.d_gains[0, :shard],
            grads.d_w_qkv,
            grads.d_w_out,
            grads.d_gains[1, :shard],
            grads.d_w_in,
            grads.d_w_back,
            head_grad,
        )

    def across(value):
        return lax.all_gather(value, TILE, axis=0, tiled=False)

    def total(value, axis=0):
        return lax.psum_scatter(value, IMG, scatter_dimension=axis, tiled=True)

    pieces = [getattr(grads, GRAD_REFS[0] + str(n)) for n in range(JOINT + s.here)]
    pieces = [across(total(v)) for v in pieces]
    project = total(lax.all_gather(grads.d_project, TILE, axis=0, tiled=True))
    small = across(total(grads.small_out, 1))
    head_rows = across(lax.psum(grads.head_out, IMG))
    joint = jnp.stack(pieces[JOINT:], axis=0)
    joint = joint.reshape(s.here, s.tiles, shard, 3, s.head).transpose(2, 3, 1, 0, 4)
    expand = pieces[INTO].reshape(s.tiles, shard, s.images, part).transpose(1, 2, 0, 3)
    cls_grad = small[:, : s.step, :shard].reshape(s.lanes, shard)[: s.classes]
    gain_grads = jnp.sum(small[:, s.step : s.step + 2, :shard], axis=0)
    head_grad = jnp.sum(head_rows[:, s.step + 2 : s.step + 4, :128], axis=0).reshape(-1)[: s.classes]
    return (
        masks[None],
        grads.patch_grad,
        cls_grad,
        gain_grads[0],
        joint.reshape(shard, -1).astype(F32),
        project.astype(F32),
        gain_grads[1],
        expand.reshape(shard, -1).astype(F32),
        pieces[BACK].reshape(-1, s.dim).astype(F32),
        head_grad,
    )


def solution(mesh):
    in_specs = (
        P(IMG, TILE, None),
        P(IMG, TILE, None),
        P(IMG),
        P(None, IMG),
        P(IMG),
        P(IMG, None),
        P(IMG, None),
        P(IMG),
        P(IMG, None),
        P(IMG, None),
        P(),
    )
    out_specs = (
        P(IMG, None, TILE, None),
        P(IMG, TILE, None),
        P(None, IMG),
        P(IMG),
        P(IMG, None),
        P(IMG, None),
        P(IMG),
        P(IMG, None),
        P(IMG, None),
        P(),
    )
    return jax.shard_map(shards, mesh=mesh, in_specs=in_specs, out_specs=out_specs, check_vma=False)
```

```python
import collections
import functools
import types

import jax
import jax.numpy as jnp
import numpy as np
from jax import lax
from jax.experimental import pallas as pl
from jax.experimental.pallas import tpu as pltpu
from jax.sharding import PartitionSpec as P

IMG = "img"
TILE = "tile"
HEADS = 12
WP = 16
UP = 16
BAND = 32
BAND_CELLS = 4
GROUP = 8
EDGE = UP // 2
MESH = pl.DeviceIdType.MESH
LOGIT_UNIT = "logit_unit"
LOGIT_SCALE = "logit_scale"
HEAD_GAIN = "head_gain"
PATCH_UNIT = "patch_unit"
CLASS_UNIT = "class_unit"
FINAL = "final"
W_REDUCE = "w_reduce"
SLOPE = "slope"
W_EXPAND = "w_expand"
ACT = "act"
H_TWO = "h_two"
AFTER = "after"
GAINS = "gains"
W_PROJECT = "w_project"
Q = "q"
KEYS = "keys"
OUTS = "outs"
VALUES = "values"
MIXED = "mixed"
H_ONE = "h_one"
W_JOINT = "w_joint"
TOKEN_ROWS = "token_rows"
F32 = jnp.float32
BF16 = jnp.bfloat16
PLANE = 2
BACK, INTO, JOINT, LAST, PROJECT = 0, 2, 4, 5, 6
VMEM_BYTES = 62 << 20


def product(left, right):
    return jnp.dot(left, right, preferred_element_type=F32)


def times_transposed(left, right):
    return lax.dot_general(left, right, (((1,), (1,)), ((), ())), preferred_element_type=F32)


def transposed_times(left, right):
    return lax.dot_general(left, right, (((0,), (0,)), ((), ())), preferred_element_type=F32)


def layer_norm_parts(value):
    centre = jnp.mean(value, axis=-1, keepdims=True)
    centred = value - centre
    spread = jnp.mean(centred * centred, axis=-1, keepdims=True)
    scale = lax.rsqrt(spread + 1e-05)
    return centred * scale, scale


def layer_norm_back(unit, scale, gain, upstream):
    weighted = upstream * gain
    mean = jnp.mean(weighted, axis=-1, keepdims=True)
    along = jnp.mean(weighted * unit, axis=-1, keepdims=True)
    return scale * (weighted - mean - unit * along)


def gelu_pair(x):
    root = np.float32(np.sqrt(2.0 / np.pi))
    square = x * x
    turned = jnp.tanh(root * x * (1.0 + np.float32(0.044715) * square))
    half = 0.5 * (1.0 + turned)
    slope = half + 0.5 * x * (1.0 - turned * turned) * root * (
        1.0 + np.float32(3 * 0.044715) * square
    )
    return x * half, slope


def lane_iota(rows, lanes):
    return lax.broadcasted_iota(jnp.int32, (rows, lanes), 1)


def row_iota(rows, lanes):
    return lax.broadcasted_iota(jnp.int32, (rows, lanes), 0)


def carry_copy(k, name, back=False):
    near, far = getattr(k, name), k.far[name]
    n = list(k.far).index(name)
    ends = (far, near) if back else (near, far)
    return pltpu.make_async_copy(*ends, k.carry_sem.at[n])


def keep(k, name):
    if name in k.far:
        carry_copy(k, name).start()


def kept(k):
    for name in k.far:
        carry_copy(k, name).wait()


def fetch_all(k):
    for name in k.far:
        carry_copy(k, name, True).start()


def have(k, *names):
    for name in names:
        if name in k.far:
            carry_copy(k, name, True).wait()


class Net:
    def __init__(self, k):
        self.k = k
        self.sent = []
        self.stage_sends = []

    def send(self, source, target, base, slot, device, when=None):
        k = self.k
        copy = pltpu.make_async_remote_copy(
            src_ref=source,
            dst_ref=target,
            send_sem=k.send_sem.at[len(self.sent)],
            recv_sem=k.recv_sem.at[base + slot],
            device_id=device,
            device_id_type=MESH,
        )
        self.sent.append((copy, when))
        if when is None:
            copy.start()
        else:
            pl.when(when)(copy.start)
        return len(self.sent) - 1

    def arrived(self, target, base, slot):
        k = self.k
        pltpu.make_async_remote_copy(
            src_ref=target,
            dst_ref=target,
            send_sem=k.send_sem.at[0],
            recv_sem=k.recv_sem.at[base + slot],
            device_id=k.sibling,
            device_id_type=MESH,
        ).wait_recv()

    def gone(self, number):
        if self.sent[number] is None:
            return
        copy, when = self.sent[number]
        self.sent[number] = None
        if when is None:
            copy.wait_send()
        else:
            pl.when(when)(copy.wait_send)

    def drain(self):
        for number in range(len(self.sent)):
            self.gone(number)


def place(k):
    k.i = lax.axis_index(IMG)
    k.t = lax.axis_index(TILE)
    k.y = k.i % PLANE
    k.z = k.i // PLANE
    k.planes = k.s.images // PLANE
    k.ts = k.t + 1 - 2 * (k.t % 2)
    k.tx = (k.t + 2) % 4
    k.td = (k.ts + 2) % 4
    k.sibling = (k.i, k.ts)
    k.across = (k.i, k.tx)
    k.diagonal = (k.i, k.td)
    k.mate = (k.i + 1 - 2 * k.y, k.t)


def line_peer(k, step):
    z = (k.z + step) % k.planes
    return z, (PLANE * z + k.y, k.t)


def enter(k, beside=None):
    barrier = pltpu.get_barrier_semaphore()
    peers = [k.sibling, k.across, k.diagonal]
    if k.s.img_comm:
        peers += [k.mate] + [line_peer(k, step)[1] for step in range(1, k.planes)]
    for peer in peers:
        pl.semaphore_signal(barrier, inc=1, device_id=peer, device_id_type=MESH)
    if beside:
        beside()
    pl.semaphore_wait(barrier, len(peers))


def spread_start(k, own, slots, name):
    for step in range(1, k.planes):
        k.net.send(own, slots.at[k.i], name, k.i, line_peer(k, step)[1])
    k.net.send(own, slots.at[k.i], name, k.i, k.mate)


def spread_pass(k, slots, name):
    for step in range(1, k.planes):
        z = (k.z + k.planes - step) % k.planes
        i = PLANE * z + k.y
        k.net.arrived(slots.at[i], name, i)
        k.net.send(slots.at[i], slots.at[i], name, i, k.mate)


def spread_end(k, slots, name):
    for z in range(k.planes):
        i = PLANE * z + 1 - k.y
        k.net.arrived(slots.at[i], name, i)


def line_start(k, own, slots, base, cut):
    send = k.net.send
    own, there = own.at[cut], slots.at[(k.i, *cut)]
    send(own, there, base, k.i, line_peer(k, 1)[1], k.z < k.planes - 1)
    send(own, there, base, k.i, line_peer(k, k.planes - 1)[1], k.z > 0)
    send(own, there, base, k.i, k.mate)


def line_end(k, slots, base, cut):
    for z in range(k.planes):
        i = PLANE * z + 1 - k.y
        k.net.arrived(slots.at[(i, *cut)], base, i)


def line_hop(k, slots, base, far, cut):
    send = k.net.send
    for sign in (-1, 1):
        here = k.z >= far if sign < 0 else k.z < k.planes - far
        more = k.z < k.planes - 1 if sign < 0 else k.z > 0
        i = PLANE * ((k.z + sign * far + k.planes) % k.planes) + k.y
        there = slots.at[(i, *cut)]

        @pl.when(here)
        def _(i=i, there=there):
            k.net.arrived(there, base, i)

        if far < k.planes - 1:
            peer = line_peer(k, 1 if sign < 0 else k.planes - 1)[1]
            send(there, there, base, i, peer, here & more)
        send(there, there, base, i, k.mate, here)


def project_cut(k, tile):
    rows, columns = k.s.dim // k.s.images // 2, k.s.dim // 2
    return (
        pl.ds(pl.multiple_of(rows * (tile // 2), 16), rows),
        pl.ds(pl.multiple_of(columns * (tile % 2), 128), columns),
    )


def project_part(k, tile):
    rows, columns = project_cut(k, tile)
    return k.w_project.at[:, rows, columns]


def slot_part(slots, slot, rows):
    return slots.at[slot] if rows is None else slots.at[slot, rows]


def share_start(k, slots, base, rows=None):
    own = slot_part(slots, k.t, rows)
    k.net.send(own, own, base, k.t, k.across)
    k.net.send(own, own, base, k.t, k.sibling)


def share_pass(k, slots, base, rows=None):
    part = slot_part(slots, k.tx, rows)
    k.net.arrived(part, base, k.tx)
    k.net.send(part, part, base, k.tx, k.sibling)


def halves(s):
    return [pl.ds(n * s.dim // 2, s.dim // 2) for n in range(2)]


def column_cuts(s):
    return [(pl.ds(0, s.rows), columns) for columns in halves(s)]


def row_cuts(s):
    return [(pl.ds(s.own, s.slot), pl.ds(0, s.dim)), (pl.ds(0, s.own), pl.ds(0, s.dim))]


def reduce_over_tile(k, base, part, cuts, before=None, ready=None):
    sends = k.net.stage_sends
    for number in sends:
        k.net.gone(number)
    sends.clear()

    def to_sibling(n, kind, slot):
        at = (kind, *cuts[n])
        k.stage[at] = part(slot, *cuts[n]).astype(BF16)
        sends.append(k.net.send(k.stage.at[at], k.from_sib.at[at], base, 3 * n + kind, k.sibling))

    def near(n):
        k.own_part[cuts[n]] = part(k.t, *cuts[n])
        if before and n == 0:
            before(k.ts)
        to_sibling(n, 0, k.ts)

    if before:
        near(0)
        near(1)
        before(k.tx)
        before(k.td)
    for n in range(2):
        if ready:
            ready(n)
        to_sibling(n, 1, k.td)
        total = part(k.tx, *cuts[n])
        k.across_part[cuts[n]] = total
        k.net.arrived(k.from_sib.at[(1, *cuts[n])], base, 3 * n + 1)
        total = k.across_part[cuts[n]] + k.from_sib[(1, *cuts[n])].astype(F32)
        k.stage[(2, *cuts[n])] = total.astype(BF16)
        ends = k.stage.at[(2, *cuts[n])], k.from_across.at[cuts[n]]
        sends.append(k.net.send(*ends, base, 3 * n + 2, k.across))
        if not before:
            near(n)


def reduced_over_tile(k, base, cuts, which=(0, 1)):
    for n in which:
        k.net.arrived(k.from_sib.at[(0, *cuts[n])], base, 3 * n)
        k.net.arrived(k.from_across.at[cuts[n]], base, 3 * n + 2)
    if len(which) == 1:
        at = cuts[which[0]]
        return k.own_part[at] + k.from_sib[(0, *at)].astype(F32) + k.from_across[at].astype(F32)
    return k.own_part[...] + k.from_sib[0].astype(F32) + k.from_across[...].astype(F32)


def key_bias(k, slot, height):
    s = k.s
    rows = row_iota(s.rows, s.head)
    cls = rows - s.own
    patch_ok = (rows < s.own) & (rows < (height - slot * s.grid) * WP)
    class_ok = (cls >= 0) & (cls < s.step) & (slot * s.step + cls < s.classes)
    off = jnp.where(patch_ok | class_ok, 0.0, -1e30)
    lane = lane_iota(s.rows, s.head)
    return jnp.where(lane == 0, off, jnp.where(lane < 4, 1.0, 0.0))


def class_rows(k, slot):
    s = k.s
    rows = k.cls_rows[pl.ds(pl.multiple_of(slot * s.step, 8), s.step), :]
    return jnp.concatenate([rows, jnp.zeros((s.slot - s.step, s.dim), F32)], axis=0)


def slot_rows(k, slot):
    return pl.ds(pl.multiple_of(slot * k.s.rows, 16), k.s.rows)


def block_scores(k, head, slot):
    return times_transposed(k.q[head, slot_rows(k, slot), :], k.keys[head])


def local_copy(k, source, target, number):
    return pltpu.make_async_copy(source, target, k.local_sem.at[number])


def pick_columns(k):
    s = k.s
    wide = s.here * s.head
    for n in range(4):

        @pl.when(k.t == n)
        def _(n=n):
            cut = [
                k.w_qkv[:, s.dim * m + wide * n + s.head * h :][:, : s.head]
                for h in range(s.here)
                for m in range(3)
            ]
            k.wq[...] = jnp.concatenate(cut, axis=1)


def pick_hidden(k):
    part = k.s.hidden // k.s.images
    for n in range(4):

        @pl.when(k.t == n)
        def _(n=n):
            cut = [k.w_in_near[:, part * (4 * i + n) :][:, :part] for i in range(k.s.images)]
            k.wi[...] = jnp.concatenate(cut, axis=1)


def forward_kernel(k):
    s = k.s
    place(k)
    net = k.net
    i, t = k.i, k.t
    shard = s.dim // s.images

    def prepare():
        head_gain = k.gain_row[...].astype(F32)
        head_gain = jnp.concatenate([head_gain, jnp.zeros((1, s.lanes - s.classes), F32)], axis=1)
        k.head_gain[...] = jnp.broadcast_to(head_gain, (8, s.lanes))
        if s.img_comm:
            rows = [ref[...].astype(F32) for ref in (k.cls_emb, k.gain_one, k.gain_two)]
            rows += [jnp.zeros((s.lanes - s.classes - 2, shard), F32)]
            table = jnp.concatenate(rows, axis=0)
            table = jnp.concatenate([table, jnp.zeros((s.lanes, 128 - shard), F32)], axis=1)
            k.small[...] = table.astype(BF16)
            pick_columns(k)

    patches, labels = k.patches.at[0], k.labels.at[0]
    tokens_in = local_copy(k, patches, k.tokens.at[t], 1)
    tokens_in.start()
    if s.img_comm:
        w_in_copy = local_copy(k, k.w_in, k.w_in_near, 2)
        w_in_copy.start()
        w_back_copy = local_copy(k, k.wb.at[t], k.w_reduce.at[i], 3)
        w_back_copy.start()
    enter(k, prepare)
    keep(k, HEAD_GAIN)
    comm = s.img_comm
    wide = s.here * s.head
    first, second = halves(s)
    early = pl.ds(0, 3 * s.head * (s.here - 1))
    late = pl.ds(3 * s.head * (s.here - 1), 3 * s.head)
    joint = expand = reduce = (None, None)
    project = None
    if comm:
        at = k.at
        every = pl.ds(0, shard)
        joint = ((k.wq, k.w_joint, at.joint0, early), (k.wq, k.w_joint, at.joint1, late))
        expand = ((k.wi, k.w_expand, at.expand0, first), (k.wi, k.w_expand, at.expand1, second))
        back = k.wb.at[t]
        reduce = ((back, k.w_reduce, at.reduce0, first), (back, k.w_reduce, at.reduce1, second))
        joint, expand, reduce = [
            [(*item[:3], (every, item[3])) for item in pair] for pair in (joint, expand, reduce)
        ]
        project = (k.wo, k.w_project, at.w_project, project_cut(k, t))
        wo_copy = local_copy(k, k.wo.at[project[3]], k.w_project.at[(i, *project[3])], 0)
        wo_copy.start()

    def start(item):
        if comm:
            line_start(k, *item)

    def hop(item, far):
        if comm:
            line_hop(k, *item[1:3], far, item[3])

    def end(item):
        if comm:
            line_end(k, *item[1:])

    if comm:
        spread_start(k, k.small, k.smalls, k.at.small)
        k.smalls[i] = k.small[...]
        start(joint[0])
        start(joint[1])
        start(project)
    net.send(patches, k.tokens.at[t], k.at.tokens, t, k.across)
    net.send(patches, k.tokens.at[t], k.at.tokens, t, k.sibling)
    top, bottom, last = pl.ds(0, EDGE), pl.ds(EDGE, EDGE), pl.ds(s.grid * UP - EDGE, EDGE)
    net.send(labels.at[top], k.halo.at[bottom], k.at.halo, 1, (i, (t + 3) % 4))
    net.send(labels.at[last], k.halo.at[top], k.at.halo, 0, (i, (t + 1) % 4))
    if comm:
        k.w_joint[i] = k.wq[...]
        spread_pass(k, k.smalls, k.at.small)
        hop(joint[0], 1)
        hop(joint[1], 1)
        hop(project, 1)
        w_in_copy.wait()
        pick_hidden(k)
        k.w_expand[i] = k.wi[...]
        start(expand[0])
        hop(joint[0], 2)
        hop(joint[1], 2)
        hop(project, 2)
        spread_end(k, k.smalls, k.at.small)
        pieces = [k.smalls[n].astype(F32)[:, :shard] for n in range(s.images)]
        full = jnp.concatenate(pieces, axis=1)
    else:
        full = k.small_full[...].astype(F32)
    k.gains[0:2] = full[s.classes : s.classes + 2]
    k.cls_rows[...] = jnp.where(row_iota(s.lanes, s.dim) < s.classes, full, 0.0)
    gain_one, gain_two = k.gains[0:1], k.gains[1:2]
    keep(k, GAINS)

    def normed_tokens(slot):
        value = jnp.concatenate([k.tokens[slot].astype(F32), class_rows(k, slot)], axis=0)
        k.h_one[slot] = (layer_norm_parts(value)[0] * gain_one).astype(BF16)

    tokens_in.wait()
    k.token_rows[0 : s.own] = k.tokens[t].astype(F32)
    k.token_rows[s.own : s.rows] = class_rows(k, t)
    keep(k, TOKEN_ROWS)
    normed_tokens(t)
    if comm:
        hop(joint[0], 3)
        hop(joint[1], 3)
        hop(project, 3)
        start(expand[1])
    net.arrived(k.tokens.at[k.ts], k.at.tokens, k.ts)
    normed_tokens(k.ts)
    net.arrived(k.tokens.at[k.tx], k.at.tokens, k.tx)
    net.send(k.tokens.at[k.tx], k.tokens.at[k.tx], k.at.tokens, k.tx, k.sibling)
    normed_tokens(k.tx)
    hop(expand[0], 1)
    net.arrived(k.tokens.at[k.td], k.at.tokens, k.td)
    normed_tokens(k.td)
    keep(k, H_ONE)
    if comm:
        end(joint[0])
        end(joint[1])
        keep(k, W_JOINT)
        end(project)
        wo_copy.wait()
        part = project_part(k, t)
        net.send(part, part, at.w_shared, t, k.across)
        net.send(part, part, at.w_shared, t, k.sibling)

    lane = lane_iota(s.rows, s.head)
    one = jnp.where(lane == 0, 1.0, 0.0)
    ones = jnp.where(lane < 2, 1.0, 0.0)
    height = k.height[0]

    def joint_rows(slot):
        value = product(k.h_one[slot], k.w_joint[...].reshape(s.dim, s.here * 3 * s.head))
        bias = key_bias(k, slot, height)
        rows = slot_rows(k, slot)
        for h in range(s.here):
            cut = [
                value[:, (3 * h + n) * s.head : (3 * h + n + 1) * s.head] for n in range(3)
            ]
            for ref, part, extra in zip(
                (k.q, k.keys, k.values), (cut[0] * s.head**-0.5, cut[1], cut[2]), (one, bias, ones)
            ):
                ref[h, rows, :] = jnp.concatenate([part, extra], axis=1).astype(BF16)

    joint_rows(0)
    hop(expand[0], 2)
    joint_rows(1)
    start(reduce[0])
    joint_rows(2)
    hop(expand[0], 3)
    joint_rows(3)
    keep(k, Q)
    keep(k, KEYS)
    keep(k, VALUES)
    hop(expand[1], 1)

    def attend(slot):
        rows = slot_rows(k, slot)
        wide_lane = lane_iota(s.rows, 2 * s.head)
        parts = []
        for h in range(s.here):
            scores = block_scores(k, h, slot)
            largest = jnp.max(scores, axis=-1, keepdims=True)
            powers = jnp.exp(scores - largest).astype(BF16)
            out = product(powers, k.values[h])
            parts.append(out[:, : s.head] / out[:, s.head : s.head + 1])
            k.outs[h, rows, :] = jnp.where(wide_lane == s.head + 1, largest, out)
        k.mixed[slot] = jnp.concatenate(parts, axis=1).astype(BF16)

    for step, slot in enumerate((k.tx, k.td, k.ts, t), 1):
        attend(slot)
        if step < 4:
            net.send(k.mixed.at[slot], k.mixed_all.at[t], k.at.mixed, t, (i, slot))
        if step == 1:
            hop(expand[1], 2)
            start(reduce[1])
        if step == 2:
            hop(expand[1], 3)
            if comm:
                part = project_part(k, k.tx)
                net.arrived(part, at.w_shared, k.tx)
                net.send(part, part, at.w_shared, k.tx, k.sibling)
        if step == 3:
            hop(reduce[0], 1)
    keep(k, OUTS)
    keep(k, MIXED)
    k.mixed_all[t] = k.mixed[t]
    hop(reduce[0], 2)
    hop(reduce[0], 3)
    if comm:
        for slot in (k.ts, k.td):
            net.arrived(project_part(k, slot), at.w_shared, slot)
        keep(k, W_PROJECT)
    after = k.token_rows[...]
    w_project = k.w_project[...].reshape(s.dim, s.dim)
    for step in range(1, 4):
        slot = (t + step) % 4
        net.arrived(k.mixed_all.at[slot], k.at.mixed, slot)
    for n in range(4):
        after = after + product(k.mixed_all[n], w_project[wide * n : wide * (n + 1)])
    k.after[...] = after
    keep(k, AFTER)
    k.h_two[t] = (layer_norm_parts(after)[0] * gain_two).astype(BF16)
    share_start(k, k.h_two, k.at.h_two)
    hop(reduce[1], 1)
    if comm:
        end(expand[0])
        end(expand[1])
        keep(k, W_EXPAND)

    def hidden(slot):
        pre = product(k.h_two[slot], k.w_expand[...].reshape(s.dim, s.hidden))
        act, slope = gelu_pair(pre)
        k.act[slot] = act.astype(BF16)
        k.slope[slot] = slope.astype(BF16)

    hidden(t)
    hop(reduce[1], 2)
    net.arrived(k.h_two.at[k.ts], k.at.h_two, k.ts)
    hidden(k.ts)
    hop(reduce[1], 3)
    share_pass(k, k.h_two, k.at.h_two)
    hidden(k.tx)
    net.arrived(k.h_two.at[k.td], k.at.h_two, k.td)
    hidden(k.td)
    keep(k, H_TWO)
    keep(k, ACT)
    keep(k, SLOPE)

    def contract(slot, rows, columns):
        return product(k.act[slot], k.w_reduce[:, :, columns].reshape(s.hidden, s.dim // 2))

    if comm:
        w_back_copy.wait()
    cuts = column_cuts(s)
    reduce_over_tile(
        k, k.at.feed, contract, cuts, ready=(lambda n: end(reduce[n])) if comm else None
    )
    if comm:
        keep(k, W_REDUCE)
    final = k.after[...] + reduced_over_tile(k, k.at.feed, cuts)
    k.final[...] = final
    keep(k, FINAL)
    unit = (final * lax.rsqrt(jnp.sum(final * final, axis=-1, keepdims=True) + 1e-06)).astype(BF16)
    k.cls_units[t] = unit[s.own :]
    k.patch_unit[WP : WP + s.own] = unit[: s.own]
    above, below = pl.ds(0, WP), pl.ds(WP + s.own, WP)
    for slot in (k.tx, k.td, k.ts):
        net.send(k.cls_units.at[t], k.cls_units.at[t], k.at.units, t, (i, slot))
    net.send(k.patch_unit.at[pl.ds(WP, WP)], k.patch_unit.at[below], k.at.rim, 1, (i, (t + 3) % 4))
    net.send(k.patch_unit.at[pl.ds(s.own, WP)], k.patch_unit.at[above], k.at.rim, 0, (i, (t + 1) % 4))
    for slot in (k.ts, k.tx, k.td):
        net.arrived(k.cls_units.at[slot], k.at.units, slot)
    net.arrived(k.patch_unit.at[above], k.at.rim, 0)
    net.arrived(k.patch_unit.at[below], k.at.rim, 1)
    units = jnp.concatenate([k.cls_units[n].astype(F32)[: s.step] for n in range(4)], axis=0)
    units = jnp.where(row_iota(s.lanes, s.dim) < s.classes, units, 0.0).astype(BF16)
    k.class_unit[...] = units
    keep(k, CLASS_UNIT)
    keep(k, PATCH_UNIT)
    logits = times_transposed(k.patch_unit[...], units)
    unit_logits, scale = class_norm_parts(k, logits)
    k.logit_unit[...] = unit_logits[WP : WP + s.own]
    k.logit_scale[...] = jnp.broadcast_to(scale[WP : WP + s.own], (s.own, 128))
    keep(k, LOGIT_UNIT)
    keep(k, LOGIT_SCALE)
    normed = (unit_logits * k.head_gain[0:1]).astype(BF16)
    k.cells[WP : WP + s.own] = normed[WP : WP + s.own]
    k.cells[:WP] = jnp.where(t == 0, normed[WP : 2 * WP], normed[:WP])
    k.cells[WP + s.own :] = jnp.where(t == 3, normed[s.own : WP + s.own], normed[WP + s.own :])
    net.arrived(k.halo.at[pl.ds(0, EDGE)], k.at.halo, 0)
    net.arrived(k.halo.at[pl.ds(EDGE, EDGE)], k.at.halo, 1)
    kept(k)
    net.drain()


def class_norm_parts(k, value):
    s = k.s
    real = lane_iota(value.shape[0], s.lanes) < s.classes
    centre = jnp.sum(value, axis=-1, keepdims=True) / s.classes
    centred = jnp.where(real, value - centre, 0.0)
    spread = jnp.sum(centred * centred, axis=-1, keepdims=True) / s.classes
    scale = lax.rsqrt(spread + 1e-05)
    return centred * scale, scale


def sum_start(k, name):
    g = k.grads[name]
    k.net.send(g.blocks.at[1 - k.y], g.from_mate, g.at_mate, 0, k.mate)


def sum_pass(k, name):
    g = k.grads[name]
    k.net.arrived(g.from_mate, g.at_mate, 0)
    for step in range(k.planes):
        z = (k.z + step) % k.planes
        both = g.blocks[k.y, z].astype(F32) + g.from_mate[z].astype(F32)
        g.blocks[k.y, z] = both.astype(BF16)
        if step:
            k.net.send(g.blocks.at[k.y, z], g.from_line.at[k.z], g.at_line, k.z, line_peer(k, step)[1])


def sum_end(k, name):
    g = k.grads[name]
    total = g.blocks[k.y, k.z].astype(F32)
    for step in range(1, k.planes):
        z = (k.z + step) % k.planes
        k.net.arrived(g.from_line.at[z], g.at_line, z)
        total = total + g.from_line[z].astype(F32)
    g.out[k.t] = total.astype(BF16)
    share_start(k, g.out, g.at_out)


def sum_share(k, name):
    g = k.grads[name]
    share_pass(k, g.out, g.at_out)


def sum_close(k, name):
    g = k.grads[name]
    k.net.arrived(g.out.at[k.ts], g.at_out, k.ts)
    k.net.arrived(g.out.at[k.td], g.at_out, k.td)


def put_blocks(k, name, value):
    g = k.grads[name]
    if not k.s.img_comm:
        g.out[...] = value.astype(BF16)
        return
    rows = value.shape[0] // k.s.images
    for i in range(k.s.images):
        g.blocks[i % PLANE, i // PLANE] = value[rows * i : rows * (i + 1)].astype(BF16)


def head_powers(k, h):
    s = k.s
    out = k.outs[h]
    total = out[:, s.head + 1 : s.head + 2] + jnp.log(out[:, s.head : s.head + 1])
    first = total.astype(BF16).astype(F32)
    second = (total - first).astype(BF16).astype(F32)
    lane = lane_iota(4 * s.rows, 2 * s.head) - s.head
    value = jnp.where(lane == 1, -first, k.q[h].astype(F32))
    value = jnp.where(lane == 2, -second, value)
    k.q_back[...] = jnp.where(lane == 3, first + second - total, value).astype(BF16)

    def block(slot, carry):
        rows = slot_rows(k, slot)
        scores = times_transposed(k.keys[h, rows, :], k.q_back[...])
        k.powers[rows, :] = jnp.exp(scores).astype(BF16)
        return carry

    lax.fori_loop(0, 4, block, 0, unroll=True)


def row_half(value, columns):
    return value[columns.start : columns.start + columns.size]


def expand_rows(k, columns):
    s = k.s
    return row_half(k.w_expand[...].reshape(s.dim, s.hidden), columns)


def pick_rows(value, slot, size):
    parts = [value[size * n : size * (n + 1)] for n in range(4)]
    for n in range(1, 4):
        parts[0] = jnp.where(slot == n, parts[n], parts[0])
    return parts[0]


def backward_kernel(k):
    s = k.s
    place(k)
    fetch_all(k)
    enter(k)
    net = k.net
    i, t = k.i, k.t
    comm = s.img_comm
    patch_part, class_part = pl.ds(0, s.own), pl.ds(s.own, s.slot)

    top = jnp.where(t == 0, k.cell_sums[:WP], 0.0)
    bottom = jnp.where(t == 3, k.cell_sums[WP + s.own :], 0.0)
    own = k.cell_sums[WP : WP + s.own]
    own = jnp.concatenate(
        [own[:WP] + top, own[WP : s.own - WP], own[s.own - WP :] + bottom], axis=0
    )
    upstream = own.astype(BF16).astype(F32)
    have(k, LOGIT_UNIT, LOGIT_SCALE, HEAD_GAIN, PATCH_UNIT, CLASS_UNIT, FINAL)
    unit, scale = k.logit_unit[...], k.logit_scale[:, :1]
    weighted = upstream * k.head_gain[0:1]
    mean = jnp.sum(weighted, axis=-1, keepdims=True) / s.classes
    along = jnp.sum(weighted * unit, axis=-1, keepdims=True) / s.classes
    head_row = jnp.sum(upstream * unit, axis=0, keepdims=True)
    d_logits = scale * (weighted - mean - unit * along)
    d_logits = jnp.where(lane_iota(s.own, s.lanes) < s.classes, d_logits, 0.0).astype(BF16)
    d_class = transposed_times(d_logits, k.patch_unit[WP : WP + s.own])
    for n in range(4):
        k.class_out[n] = jnp.concatenate(
            [d_class[s.step * n : s.step * (n + 1)], jnp.zeros((s.slot - s.step, s.dim), F32)], axis=0
        ).astype(BF16)
    for slot in (k.ts, k.tx, k.td):
        net.send(k.class_out.at[slot], k.class_in.at[t], k.at.class_, t, (i, slot))
    final = k.final[...]
    c = lax.rsqrt(jnp.sum(final * final, axis=-1, keepdims=True) + 1e-06)
    u = final * c

    def unit_back(rows, du):
        return c[rows] * (du - u[rows] * jnp.sum(u[rows] * du, axis=-1, keepdims=True))

    d_patch = unit_back(slice(0, s.own), product(d_logits, k.class_unit[...]))
    k.d_rows[: s.own] = d_patch
    k.d_branch[t, : s.own] = d_patch.astype(BF16)
    share_start(k, k.d_branch, k.at.d_branch, patch_part)
    d_class_unit = k.class_out[t].astype(F32)
    for slot in (k.ts, k.tx, k.td):
        net.arrived(k.class_in.at[slot], k.at.class_, slot)
        d_class_unit = d_class_unit + k.class_in[slot].astype(F32)
    d_class = unit_back(slice(s.own, s.rows), d_class_unit)
    k.d_rows[s.own :] = d_class
    k.d_branch[t, s.own :] = d_class.astype(BF16)
    share_start(k, k.d_branch, k.at.d_class, class_part)

    have(k, W_REDUCE, SLOPE, W_EXPAND)

    def contract_back(slot):
        d_act = times_transposed(k.d_branch[slot], k.w_reduce[...].reshape(s.hidden, s.dim))
        k.d_pre[slot] = (d_act * k.slope[slot].astype(F32)).astype(BF16)

    def expand_back(slot, rows, columns):
        return times_transposed(k.d_pre[slot], expand_rows(k, columns))

    def before(slot):
        if slot is k.tx:
            have(k, Q, KEYS, OUTS)
            head_powers(k, 0)
            share_pass(k, k.d_branch, k.at.d_branch, patch_part)
            share_pass(k, k.d_branch, k.at.d_class, class_part)
        else:
            net.arrived(k.d_branch.at[slot, patch_part], k.at.d_branch, slot)
            net.arrived(k.d_branch.at[slot, class_part], k.at.d_class, slot)
        contract_back(slot)

    contract_back(t)
    cuts = column_cuts(s)
    reduce_over_tile(k, k.at.feed, expand_back, cuts, before)
    tall = 4 * s.rows
    have(k, ACT, H_TWO)
    for n, columns in enumerate(halves(s)):
        right = k.d_branch[:, :, columns].reshape(tall, s.dim // 2)
        put_blocks(k, BACK + n, transposed_times(k.act[...].reshape(tall, s.hidden), right))
        if comm:
            sum_start(k, BACK + n)
    for n, columns in enumerate(halves(s)):
        right = k.d_pre[:, :, columns].reshape(tall, s.hidden // 2)
        put_blocks(k, INTO + n, transposed_times(k.h_two[...].reshape(tall, s.dim), right))
        if comm:
            sum_start(k, INTO + n)

    have(k, AFTER, GAINS, W_PROJECT, VALUES, MIXED, H_ONE, W_JOINT, TOKEN_ROWS)
    unit, scale = layer_norm_parts(k.after[...])
    part = layer_norm_back(unit, scale, k.gains[1:2], reduced_over_tile(k, k.at.feed, cuts))
    d_after = k.d_rows[...] + part
    k.d_rows[...] = d_after
    d_attn = d_after.astype(BF16)
    k.d_attn[t] = d_attn
    wide = s.here * s.head
    w_project = k.w_project[...].reshape(s.dim, s.dim)
    for slot in (k.tx, k.td, k.ts, t):
        rows = k.w_project[pl.ds(PLANE * slot, PLANE)].reshape(wide, s.dim) if comm else pick_rows(w_project, slot, wide)
        k.d_mixed_out[slot] = times_transposed(d_attn, rows).astype(BF16)
        if slot is not t:
            net.send(k.d_mixed_out.at[slot], k.d_mixed.at[t], k.at.d_mixed, t, (i, slot))
    k.d_mixed[t] = k.d_mixed_out[t]
    share_start(k, k.d_attn, k.at.d_attn)
    if comm:
        sum_pass(k, BACK)
        sum_pass(k, BACK + 1)

    for slot in (k.ts, k.tx, k.td):
        net.arrived(k.d_mixed.at[slot], k.at.d_mixed, slot)

    for h in range(s.here):
        if h:
            head_powers(k, h)
        if comm and h == 1:
            sum_pass(k, INTO + 1)
            sum_end(k, BACK + 1)
        if comm and h == 2:
            sum_end(k, INTO)
            sum_share(k, BACK + 1)
        out = k.outs[h]
        d_mixed = k.d_mixed[...].reshape(tall, wide)[:, s.head * h : s.head * (h + 1)].astype(F32)
        along = jnp.sum(d_mixed * out[:, : s.head], axis=-1, keepdims=True)
        along = along / out[:, s.head : s.head + 1]
        high = along.astype(BF16).astype(F32)
        lane = lane_iota(tall, s.head)
        tail = jnp.where(lane == 0, -high, jnp.where(lane == 1, high - along, 0.0))
        k.d_out[...] = jnp.concatenate([d_mixed, tail], axis=1).astype(BF16)

        def block(slot, carry, h=h):
            rows = slot_rows(k, slot)
            powers = k.powers[rows, :]
            slopes = times_transposed(k.values[h, rows, :], k.d_out[...])
            d_scores = (powers.astype(F32) * slopes).astype(BF16)
            k.d_scores[rows, :] = d_scores
            d_k = product(d_scores, k.q_back[...])
            d_v = product(powers, k.d_out[...])
            both = jnp.concatenate([d_k[:, : s.head], d_v[:, : s.head]], axis=1)
            k.d_pair[rows, :] = both
            return carry

        lax.fori_loop(0, 4, block, 0)
        if comm and h == 0:
            sum_pass(k, INTO)
        if comm and h == 1:
            sum_share(k, BACK)
        if comm and h == 2:
            project_end(k)
            sum_end(k, INTO + 1)
        d_q = transposed_times(k.keys[h][:, : s.head], k.d_scores[...]).T * s.head**-0.5
        k.d_joint[h] = jnp.concatenate([d_q, k.d_pair[...]], axis=1).astype(BF16)
        if h == s.here - 2:
            pair = jnp.concatenate([k.d_joint[n] for n in range(h + 1)], axis=1)
            put_blocks(k, JOINT, transposed_times(k.h_one[...].reshape(tall, s.dim), pair))
        if h == s.here - 1:
            put_blocks(k, LAST, transposed_times(k.h_one[...].reshape(tall, s.dim), k.d_joint[h]))
        if comm and h >= s.here - 2:
            sum_start(k, JOINT if h == s.here - 2 else LAST)
        if h == 0:
            share_pass(k, k.d_attn, k.at.d_attn)
            if comm:
                sum_end(k, BACK)
        if h == 1:
            net.arrived(k.d_attn.at[k.ts], k.at.d_attn, k.ts)
            net.arrived(k.d_attn.at[k.td], k.at.d_attn, k.td)
            d_project = transposed_times(
                k.mixed[...].reshape(tall, wide), k.d_attn[...].reshape(tall, s.dim)
            )
            if comm:
                project_start(k, d_project.astype(BF16))
            else:
                k.d_project[...] = d_project.astype(BF16)

    w_joint = k.w_joint[...].reshape(s.dim, 3 * wide)

    def joint_back(slot, rows, columns):
        rows = pl.ds(pl.multiple_of(slot * s.rows + rows.start, 16), rows.size)
        left = jnp.concatenate([k.d_joint[h, rows, :] for h in range(s.here)], axis=1)
        return times_transposed(left, w_joint)

    cuts = row_cuts(s)
    reduce_over_tile(k, k.at.joint, joint_back, cuts)
    unit, scale = layer_norm_parts(k.token_rows[...])
    if comm:
        sum_share(k, INTO)
        sum_pass(k, JOINT)
        sum_pass(k, PROJECT)

    def norm_back(rows, upstream):
        return k.d_rows[rows] + layer_norm_back(unit[rows], scale[rows], k.gains[0:1], upstream)

    own_rows, cls_rows = slice(0, s.own), slice(s.own, s.rows)
    table = norm_back(cls_rows, reduced_over_tile(k, k.at.joint, cuts, (0,)))
    table = jnp.where(row_iota(s.slot, s.dim) < s.step, table, 0.0)
    rows = row_iota(s.slot, 128)
    head_rows = jnp.where(rows == s.step, head_row[:, :128], 0.0)
    rest = jnp.concatenate([head_row[:, 128:], jnp.zeros((1, 256 - s.lanes), F32)], axis=1)
    head_rows = jnp.where(rows == s.step + 1, rest, head_rows)
    if comm:
        small_start(k, table, head_rows)
        sum_pass(k, LAST)
        sum_share(k, INTO + 1)
        sum_end(k, JOINT)
        small_end(k)
    k.patch_grad[0] = norm_back(own_rows, reduced_over_tile(k, k.at.joint, cuts, (1,)))
    if not comm:
        k.small_out[...] = table
        k.head_out[...] = head_rows
        net.drain()
        return
    sum_end(k, PROJECT)
    sum_end(k, LAST)
    sum_share(k, JOINT)
    sum_share(k, PROJECT)
    sum_share(k, LAST)
    for name in range(len(k.grads)):
        sum_close(k, name)
    for slot in (k.ts, k.tx, k.td):
        net.arrived(k.small_sum.at[slot], k.at.small_sum, slot)
    net.drain()


def project_start(k, value):
    s = k.s
    blocks = k.grads[PROJECT].blocks
    shard = s.dim // s.images
    rows, columns = shard // 2, s.dim // 2
    for n in range(4):
        for y in range(PLANE):
            first = shard * y + rows * (n // 2)
            k.project_out[n, y] = value[first : first + rows, columns * (n % 2) :][:, :columns]
    blocks[:, k.t] = k.project_out[k.t]
    for slot in (k.tx, k.td, k.ts):
        k.net.send(k.project_out.at[slot], blocks.at[:, k.t], k.at.project, k.t, (k.i, slot))


def project_end(k):
    blocks = k.grads[PROJECT].blocks
    for slot in (k.ts, k.tx, k.td):
        k.net.arrived(blocks.at[:, slot], k.at.project, slot)
    sum_start(k, PROJECT)


def small_start(k, table, head_rows):
    s = k.s
    shard = s.dim // s.images
    pad = jnp.zeros((s.slot, 128 - shard), F32)
    for n in range(s.images):
        cut = jnp.concatenate([table[:, shard * n : shard * (n + 1)], pad], axis=1)
        k.small_out[n] = (cut + head_rows).astype(BF16)
    for step in range(1, s.images):
        n = (k.i + step) % s.images
        k.net.send(k.small_out.at[n], k.small_in.at[k.i], k.at.small, k.i, (n, k.t))


def small_end(k):
    s = k.s
    total = k.small_out[k.i].astype(F32)
    for step in range(1, s.images):
        n = (k.i + step) % s.images
        k.net.arrived(k.small_in.at[n], k.at.small, n)
        total = total + k.small_in[n].astype(F32)
    k.small_sum[k.t] = total
    for slot in (k.ts, k.tx, k.td):
        k.net.send(k.small_sum.at[k.t], k.small_sum.at[k.t], k.at.small_sum, k.t, (k.i, slot))


def gain_sums(weight, grad):
    return jnp.sum(weight.astype(F32) * grad, axis=1, keepdims=True)


def write_kernel(k):
    s = k.s
    shard = s.dim // s.images
    k.patch_grad[...] = k.patch_rows[...]
    half = s.dim // 2
    for n in range(2):
        k.d_w_back[:, half * n : half * (n + 1)] = k.back[n][...].astype(F32).reshape(4 * shard, half)
    part = s.hidden // s.images
    cut = [jnp.concatenate([ref[n].astype(F32) for ref in k.into], axis=1) for n in range(4)]
    cut = [cut[n][:, part * i : part * (i + 1)] for i in range(s.images) for n in range(4)]
    k.d_w_in[...] = jnp.concatenate(cut, axis=1)
    both = [[k.pair[n].astype(F32), k.last[n].astype(F32)] for n in range(4)]
    split = s.here - 1
    for m in range(3):
        cut = [
            both[n][h // split][:, s.head * (3 * (h % split) + m) :][:, : s.head]
            for n in range(4)
            for h in range(s.here)
        ]
        k.d_w_qkv[:, s.dim * m : s.dim * (m + 1)] = jnp.concatenate(cut, axis=1)
    for n in range(4):
        rows, columns = shard // 2 * (n // 2), half * (n % 2)
        k.d_w_out[rows : rows + shard // 2, columns : columns + half] = k.project[n].astype(F32)
    rows = jnp.concatenate([k.small_sum[n][: s.step] for n in range(4)], axis=0)
    k.d_cls[...] = rows[: s.classes, :shard]
    rest = k.small_sum[0] + k.small_sum[1] + k.small_sum[2] + k.small_sum[3]
    one = gain_sums(k.w_qkv[...], k.d_w_qkv[...])
    two = gain_sums(k.w_in[...], k.d_w_in[...])
    both = jnp.concatenate([one, two, jnp.zeros((shard, 126), F32)], axis=1).T
    k.d_gain_one[...] = both[0:1] / k.gain_one[...].astype(F32)
    k.d_gain_two[...] = both[1:2] / k.gain_two[...].astype(F32)
    head = jnp.concatenate([rest[s.step : s.step + 1], rest[s.step + 1 : s.step + 2]], axis=1)
    k.d_head[...] = head[:, : s.classes]


def tent(pixels, cells, first):
    place = (np.arange(pixels) + 0.5) / UP - 0.5 - first
    return np.maximum(0.0, 1.0 - np.abs(place[:, None] - np.arange(cells)[None, :]))


def band_tables():
    edge = tent(2 * UP, 2, 0)[EDGE : 3 * EDGE]
    edge = np.concatenate([edge[:EDGE], np.zeros((EDGE, 2)), np.zeros((EDGE, 2)), edge[EDGE:]], axis=0)
    edge = edge.reshape(2, 2 * EDGE, 2).transpose(1, 0, 2).reshape(2 * EDGE, BAND_CELLS)
    across = (np.clip((np.arange(WP * UP) + 0.5) / UP - 0.5, 0, WP - 1))[None, :]
    across = np.maximum(0.0, 1.0 - np.abs(across - np.arange(WP)[:, None]))
    down = tent(BAND, BAND_CELLS, -1)
    tables = [across]
    for table in (down, edge):
        rows = table.shape[0]
        up = np.zeros((GROUP, rows, 2, BAND_CELLS, GROUP), np.float32)
        back = np.zeros((BAND_CELLS, GROUP, GROUP, rows), np.float32)
        for c in range(GROUP):
            up[c, :, :, :, c] = table[:, None, :]
            back[:, c, c, :] = table.T
        tables.append(up.reshape(GROUP * rows, 2 * BAND_CELLS * GROUP))
        tables.append(back.reshape(BAND_CELLS * GROUP, GROUP * rows))
    return [jnp.asarray(t, BF16) for t in tables]


def two_parts(value):
    high = value.astype(BF16)
    return high, (value - high.astype(F32)).astype(BF16)


def upsample_kernel(
    classes, bands, height_ref, cell_ref, label_ref, halo_ref, across_ref, up_ref, back_ref,
    edge_up_ref, edge_back_ref, mask_ref, sum_ref, wide, wide_grad, powers,
):
    band = pl.program_id(0)
    groups = -(-classes // GROUP)
    tail = classes - GROUP * (groups - 1)
    cell_rows = cell_ref.shape[0] // WP
    pixels = label_ref.shape[2]
    tile = lax.axis_index(TILE)
    limit = (height_ref[0] - tile * (bands * BAND // UP)) * UP
    share = 1.0 / (UP * UP)
    counts = [GROUP] * (groups - 1) + [tail]

    @pl.when(band == 0)
    def _():
        for r in range(cell_rows):
            wide[r] = lax.dot_general(
                cell_ref[WP * r : WP * (r + 1), :], across_ref[...], (((0,), (0,)), ((), ())),
                preferred_element_type=F32,
            )
        wide_grad[...] = jnp.zeros_like(wide_grad)

    def pixel_rows(rows, label, first, second, up, back, masked):
        def forward(g, total, count):
            at = pl.ds(GROUP * g, GROUP)
            part = jnp.concatenate([wide[pl.ds(r, 2), at, :] for r in (first, second)], axis=0)
            both = jnp.concatenate(two_parts(part.reshape(BAND_CELLS * GROUP, pixels)), axis=0)
            upsampled = product(up[: count * rows, :], both).reshape(count, rows, pixels)
            if masked:
                mask_ref[pl.ds(GROUP * g, count)] = upsampled.astype(BF16)
            power = jnp.exp(upsampled)
            powers[pl.ds(GROUP * g, count), :rows] = power
            return total + jnp.sum(power, axis=0)

        total = jnp.zeros((rows, pixels), F32)
        for g, count in enumerate(counts):
            total = forward(g, total, count)
        inverse = jnp.where(label >= 0, share, 0.0) / total
        for g, count in enumerate(counts):
            parts = []
            for c in range(count):
                target = jnp.where(label == GROUP * g + c, share, 0.0)
                parts.append((powers[GROUP * g + c, :rows] * inverse - target).astype(BF16))
            summed = product(back[:, : count * rows], jnp.concatenate(parts, axis=0))
            summed = summed.reshape(BAND_CELLS, GROUP, pixels)
            at = pl.ds(GROUP * g, GROUP)
            wide_grad[pl.ds(first, 2), at, :] += summed[:2]
            wide_grad[pl.ds(second, 2), at, :] += summed[2:]

    @pl.when(band < bands)
    def _():
        rows = lax.broadcasted_iota(jnp.int32, (BAND, pixels), 0) + BAND * band
        label = jnp.where(rows < limit, label_ref[0], -1)
        first = BAND // UP * band
        pixel_rows(BAND, label, first, first + 2, up_ref, back_ref, True)

    @pl.when(band == bands)
    def _():
        rows = lax.broadcasted_iota(jnp.int32, (2 * EDGE, pixels), 0)
        below = rows >= EDGE
        rows = rows - EDGE + jnp.where(below, bands * BAND, 0)
        label = jnp.where((rows < limit) & (below | (tile > 0)), halo_ref[...], -1)
        pixel_rows(2 * EDGE, label, 0, cell_rows - 2, edge_up_ref, edge_back_ref, False)
        for r in range(cell_rows):
            high, low = two_parts(wide_grad[r])
            sum_ref[WP * r : WP * (r + 1), :] = times_transposed(
                across_ref[...], high
            ) + times_transposed(across_ref[...], low)


def upsampled_loss(cells, labels, halo, heights, classes):
    rows, lanes = cells.shape[0] // WP, cells.shape[1]
    tile_pixels, wide_pixels = labels.shape[1:]
    tables = band_tables()
    bands = tile_pixels // BAND

    def whole(shape):
        return pl.BlockSpec(shape, lambda i: (0,) * len(shape))

    return pl.pallas_call(
        functools.partial(upsample_kernel, classes, bands),
        grid=(bands + 1,),
        out_shape=(
            jax.ShapeDtypeStruct((classes, tile_pixels, wide_pixels), BF16),
            jax.ShapeDtypeStruct(cells.shape, F32),
        ),
        in_specs=[
            pl.BlockSpec(memory_space=pltpu.SMEM),
            whole(cells.shape),
            pl.BlockSpec((1, BAND, wide_pixels), lambda i: (0, jnp.minimum(i, bands - 1), 0)),
            whole(halo.shape),
        ]
        + [whole(t.shape) for t in tables],
        out_specs=(
            pl.BlockSpec((classes, BAND, wide_pixels), lambda i: (0, jnp.minimum(i, bands - 1), 0)),
            whole(cells.shape),
        ),
        scratch_shapes=[
            pltpu.VMEM((rows, lanes, wide_pixels), F32),
            pltpu.VMEM((rows, lanes, wide_pixels), F32),
            pltpu.VMEM((lanes, BAND, wide_pixels), F32),
        ],
        compiler_params=pltpu.CompilerParams(vmem_limit_bytes=56 << 20),
        name=upsample_kernel.__name__,
    )(heights, cells, labels, halo, *tables)


CELLS = "cells"
HALO = "halo"
FAR_INPUTS = ("patches", "labels", "wo", "w_in", "wb")
CARRIED = (
    LOGIT_UNIT,
    LOGIT_SCALE,
    HEAD_GAIN,
    PATCH_UNIT,
    CLASS_UNIT,
    FINAL,
    W_REDUCE,
    SLOPE,
    W_EXPAND,
    ACT,
    H_TWO,
    AFTER,
    GAINS,
    W_PROJECT,
    Q,
    KEYS,
    OUTS,
    VALUES,
    MIXED,
    H_ONE,
    W_JOINT,
    TOKEN_ROWS,
)
GRAD_REFS = ("out", "blocks", "from_mate", "from_line")
GRAD_PLACES = ("at_mate", "at_line", "at_out")
Grad = collections.namedtuple("Grad", GRAD_REFS + GRAD_PLACES)


def run_kernel(body, s, inputs, outputs, scratch, recv, sends, number, carried, back=False):
    if back:
        inputs.update({n: inputs.pop(n) for n in carried})
        near = {n: (inputs[n].shape, inputs[n].dtype) for n in carried}
    else:
        near = {n: outputs.pop(n) for n in carried}
        outputs = {**near, **outputs}
    scratch = {**near, **scratch}
    names_in, names_out, names_scratch = list(inputs), list(outputs), list(scratch)

    places = types.SimpleNamespace()
    arrivals = 0
    for name, count in recv.items():
        setattr(places, name, arrivals)
        arrivals += count

    def kernel(*refs):
        k = types.SimpleNamespace(s=s, at=places)
        for name, ref in zip(names_in + names_out + names_scratch, refs):
            setattr(k, name, ref)
        k.far = {}
        for name, ref in zip(carried, refs[len(names_in) - len(carried) :] if back else refs[len(names_in) :]):
            k.far[name] = ref
        for name, ref in zip(carried, refs[len(names_in) + len(names_out) :]):
            setattr(k, name, ref)
        k.send_sem, k.recv_sem, k.carry_sem, k.local_sem = refs[-4:]
        k.net = Net(k)
        k.grads = []
        for n in range(PROJECT + 1):
            of = [getattr(k, word + str(n), None) for word in GRAD_REFS]
            at = [getattr(places, word + str(n), None) for word in GRAD_PLACES]
            k.grads.append(Grad(*of, *at))
        body(k)

    def space(name):
        if name in carried or name in FAR_INPUTS:
            return pl.BlockSpec(memory_space=pl.ANY)
        scalar = name in inputs and inputs[name].ndim == 1
        return pl.BlockSpec(memory_space=pltpu.SMEM if scalar else pltpu.VMEM)

    results = pl.pallas_call(
        kernel,
        out_shape=[jax.ShapeDtypeStruct(*outputs[n]) for n in names_out],
        in_specs=[space(n) for n in names_in],
        out_specs=[space(n) for n in names_out],
        scratch_shapes=[pltpu.VMEM(*scratch[n]) for n in names_scratch]
        + [pltpu.SemaphoreType.DMA((sends,)), pltpu.SemaphoreType.DMA((arrivals,)), pltpu.SemaphoreType.DMA((len(carried),)), pltpu.SemaphoreType.DMA((4,))],
        compiler_params=pltpu.CompilerParams(
            collective_id=number, has_side_effects=True, vmem_limit_bytes=VMEM_BYTES
        ),
        name=body.__name__,
    )(*inputs.values())
    return dict(zip(names_out, results))


def reduce_scratch(s):
    return dict(
        stage=((3, s.rows, s.dim), BF16),
        from_sib=((2, s.rows, s.dim), BF16),
        from_across=((s.rows, s.dim), BF16),
        own_part=((s.rows, s.dim), F32),
        across_part=((s.rows, s.dim), F32),
    )


def forward_call(s, inputs):
    wide = s.here * s.head
    all_rows = 4 * s.rows
    outputs = dict(
        h_one=((4, s.rows, s.dim), BF16),
        q=((s.here, all_rows, 2 * s.head), BF16),
        keys=((s.here, all_rows, 2 * s.head), BF16),
        values=((s.here, all_rows, 2 * s.head), BF16),
        outs=((s.here, all_rows, 2 * s.head), F32),
        mixed=((4, s.rows, wide), BF16),
        token_rows=((s.rows, s.dim), F32),
        after=((s.rows, s.dim), F32),
        h_two=((4, s.rows, s.dim), BF16),
        act=((4, s.rows, s.hidden), BF16),
        slope=((4, s.rows, s.hidden), BF16),
        final=((s.rows, s.dim), F32),
        patch_unit=((s.own + 2 * WP, s.dim), BF16),
        head_gain=((8, s.lanes), F32),
        class_unit=((s.lanes, s.dim), BF16),
        logit_unit=((s.own, s.lanes), F32),
        logit_scale=((s.own, 128), F32),
        cells=((s.own + 2 * WP, s.lanes), BF16),
        halo=((2 * EDGE, s.wide_pixels), jnp.int32),
        gains=((8, s.dim), F32),
    )
    scratch = dict(
        tokens=((4, s.own, s.dim), BF16),
        cls_rows=((s.lanes, s.dim), F32),
        mixed_all=((4, s.rows, wide), BF16),
        cls_units=((4, s.slot, s.dim), BF16),
        **reduce_scratch(s),
    )
    recv = dict(tokens=4, mixed=4, h_two=4, feed=6, units=4, rim=2, halo=2)
    sends = 3 + 3 + 3 + 6 + 3 + 2 + 2
    if s.img_comm:
        shard = s.dim // s.images
        outputs.update(w_joint=((s.images, shard, 3 * wide), BF16))
        outputs.update(w_project=((s.images, shard, s.dim), BF16))
        scratch.update(small=((s.lanes, 128), BF16), wq=((shard, 3 * wide), BF16))
        scratch.update(wi=((shard, s.hidden), BF16), w_in_near=((shard, 4 * s.hidden), BF16))
        outputs.update(w_expand=((s.images, shard, s.hidden), BF16))
        outputs.update(w_reduce=((s.images, shard, s.dim), BF16))
        scratch.update(smalls=((s.images, s.lanes, 128), BF16))
        n = s.images
        recv.update(small=n, joint0=n, joint1=n, w_project=n, w_shared=4)
        recv.update(expand0=n, expand1=n, reduce0=n, reduce1=n)
        sends += 2 * (n // PLANE) - 1 + 7 * (4 * (n // PLANE) - 3) + 3
    carried = [n for n in CARRIED if n in outputs]
    return run_kernel(forward_kernel, s, inputs, outputs, scratch, recv, sends, 1, carried)


def backward_call(s, inputs, carried):
    wide = s.here * s.head
    all_rows = 4 * s.rows
    outputs = dict(patch_grad=((1, s.own, s.dim), F32))
    scratch = dict(
        class_out=((4, s.slot, s.dim), BF16),
        class_in=((4, s.slot, s.dim), BF16),
        d_rows=((s.rows, s.dim), F32),
        d_branch=((4, s.rows, s.dim), BF16),
        d_pre=((4, s.rows, s.hidden), BF16),
        d_attn=((4, s.rows, s.dim), BF16),
        d_mixed_out=((4, s.rows, wide), BF16),
        d_mixed=((4, s.rows, wide), BF16),
        powers=((all_rows, all_rows), BF16),
        d_scores=((all_rows, all_rows), BF16),
        d_out=((all_rows, 2 * s.head), BF16),
        q_back=((all_rows, 2 * s.head), BF16),
        d_pair=((all_rows, 2 * s.head), F32),
        d_joint=((s.here, all_rows, 3 * s.head), BF16),
        **reduce_scratch(s),
    )
    recv = dict(class_=4, d_branch=4, d_class=4, feed=6, d_mixed=4, d_attn=4, joint=6)
    sends = 3 + 3 + 3 + 6 + 3 + 3 + 6
    columns = [s.dim // 2] * 2 + [s.hidden // 2] * 2 + [3 * s.head * (s.here - 1), 3 * s.head]
    columns += [s.dim // 2] * s.img_comm
    planes, shard = s.images // PLANE, s.dim // s.images
    for n, cols in enumerate(columns):
        out, blocks, from_mate, from_line = [word + str(n) for word in GRAD_REFS]
        at_mate, at_line, at_out = [word + str(n) for word in GRAD_PLACES]
        if not s.img_comm:
            outputs[out] = ((s.dim, cols), BF16)
            continue
        rows = shard // 2 if n == PROJECT else shard
        outputs[out] = ((4, rows, cols), BF16)
        scratch[blocks] = ((PLANE, planes, rows, cols), BF16)
        for what in (from_mate, from_line):
            scratch[what] = ((planes, rows, cols), BF16)
        recv[at_mate] = 1
        recv[at_line] = planes
        recv[at_out] = 4
        sends += 1 + planes - 1 + 3
    if s.img_comm:
        outputs.update(small_sum=((4, s.slot, 128), F32))
        scratch.update(project_out=((4, PLANE, shard // 2, s.dim // 2), BF16))
        scratch.update(small_out=((s.images, s.slot, 128), BF16))
        scratch.update(small_in=((s.images, s.slot, 128), BF16))
        recv.update(project=4, small=s.images, small_sum=4)
        sends += 3 + s.images - 1 + 3
    else:
        outputs.update(d_project=((wide, s.dim), BF16))
        outputs.update(small_out=((s.slot, s.dim), F32))
        outputs.update(head_out=((s.slot, 128), F32))
    return run_kernel(backward_kernel, s, inputs, outputs, scratch, recv, sends, 2, carried, True)


def write_call(s, grads, pieces, raw):
    shard = s.dim // s.images
    outputs = dict(
        patch_grad=((1, s.own, s.dim), F32),
        d_w_back=((4 * shard, s.dim), F32),
        d_w_in=((shard, 4 * s.hidden), F32),
        d_w_qkv=((shard, 3 * s.dim), F32),
        d_w_out=((shard, s.dim), F32),
        d_cls=((s.classes, shard), F32),
        d_gain_one=((1, shard), F32),
        d_gain_two=((1, shard), F32),
        d_head=((1, s.classes), F32),
    )
    inputs = dict(patch_rows=grads.patch_grad, project=pieces[PROJECT], small_sum=grads.small_sum)
    inputs.update(back0=pieces[0], back1=pieces[1], into0=pieces[2], into1=pieces[3])
    inputs.update(pair=pieces[JOINT], last=pieces[LAST], **raw)

    def kernel(*refs):
        k = types.SimpleNamespace(s=s, **dict(zip(list(inputs) + list(outputs), refs)))
        k.back, k.into = (k.back0, k.back1), (k.into0, k.into1)
        write_kernel(k)

    whole = pl.BlockSpec(memory_space=pltpu.VMEM)
    results = pl.pallas_call(
        kernel,
        out_shape=[jax.ShapeDtypeStruct(*v) for v in outputs.values()],
        in_specs=[whole] * len(inputs),
        out_specs=[whole] * len(outputs),
        compiler_params=pltpu.CompilerParams(vmem_limit_bytes=VMEM_BYTES),
        name=write_kernel.__name__,
    )(*inputs.values())
    return types.SimpleNamespace(**dict(zip(outputs, results)))


def sizes(patches, cls_emb, w_joint, w_back, head_gain):
    images, tiles = lax.axis_size(IMG), lax.axis_size(TILE)
    s = types.SimpleNamespace(images=images, tiles=tiles)
    s.dim = patches.shape[2]
    s.own = patches.shape[1]
    s.grid = s.own // WP
    s.wide_pixels = WP * UP
    s.classes = head_gain.shape[0]
    s.step = -(-s.classes // (8 * tiles)) * 8
    s.slot = -(-s.step // 16) * 16
    s.lanes = s.step * tiles
    s.rows = s.own + s.slot
    s.head = s.dim // HEADS
    s.here = HEADS // tiles
    s.hidden = w_back.shape[0] * images // tiles
    shard = w_joint.shape[0]
    s.img_comm = images == PLANE * tiles and shard % 16 == 0 and shard <= 128
    return s


def shards(
    patches, labels, heights, cls_emb, gain_one, w_qkv, w_out, gain_two, w_in, w_back, head_gain
):
    s = sizes(patches, cls_emb, w_qkv, w_back, head_gain)
    t = lax.axis_index(TILE)
    shard = w_qkv.shape[0]
    wide = s.here * s.head

    part = w_back.shape[0] // s.tiles
    w_back = w_back.reshape(s.tiles, part, s.dim)
    cls_emb, gain_one, gain_two = cls_emb, gain_one[None], gain_two[None]
    inputs = dict(patches=patches, labels=labels, height=heights, gain_row=head_gain[None])
    common = {}
    if s.img_comm:
        inputs.update(cls_emb=cls_emb, gain_one=gain_one, gain_two=gain_two)
        inputs.update(w_qkv=w_qkv, wo=w_out, w_in=w_in, wb=w_back)
    else:

        def gather(value, axis=0):
            return lax.all_gather(value, IMG, axis=axis, tiled=True)

        def pick(value, axis):
            return lax.dynamic_index_in_dim(value, t, axis, keepdims=False)

        joint = pick(w_qkv.reshape(shard, 3, s.tiles, s.here, s.head), 2)
        joint = joint.transpose(0, 2, 1, 3).reshape(shard, 3 * wide)
        expand = pick(w_in.reshape(shard, s.images, s.tiles, part), 2).reshape(shard, s.hidden)
        reduce = pick(w_back, 0)
        small = jnp.concatenate([cls_emb, gain_one, gain_two], axis=0)
        small = jnp.pad(small, ((0, s.lanes - small.shape[0]), (0, 0)))
        common.update(
            w_joint=gather(joint)[None],
            w_project=gather(w_out)[None],
            w_expand=gather(expand)[None],
            w_reduce=gather(reduce)[None],
        )
        inputs.update(small_full=gather(small, 1), **common)
    arrays = forward_call(s, inputs)
    cells, halo = arrays.pop(CELLS), arrays.pop(HALO)
    masks, cell_sums = upsampled_loss(cells, labels, halo, heights, s.classes)
    carried = [n for n in CARRIED if n in arrays]
    grads = backward_call(s, dict(**arrays, **common, cell_sums=cell_sums), carried)
    grads = types.SimpleNamespace(**grads)
    count = PROJECT + 1 if s.img_comm else PROJECT
    pieces = [getattr(grads, GRAD_REFS[0] + str(n)) for n in range(count)]
    if s.img_comm:
        raw = dict(w_qkv=w_qkv, w_in=w_in, gain_one=gain_one, gain_two=gain_two)
        written = write_call(s, grads, pieces, raw)
        return (
            masks[None],
            written.patch_grad,
            written.d_cls,
            written.d_gain_one[0],
            written.d_w_qkv,
            written.d_w_out,
            written.d_gain_two[0],
            written.d_w_in,
            written.d_w_back,
            written.d_head[0],
        )

    def across(value):
        return lax.all_gather(value, TILE, axis=0, tiled=False)

    def total(value, axis=0):
        return lax.psum_scatter(value, IMG, scatter_dimension=axis, tiled=True)

    pieces = [across(total(v)) for v in pieces]
    back, into = [jnp.concatenate(pieces[n : n + 2], axis=2) for n in (BACK, INTO)]
    project = total(lax.all_gather(grads.d_project, TILE, axis=0, tiled=True))
    small = across(total(grads.small_out, 1))
    head_rows = across(lax.psum(grads.head_out, IMG))
    joint = jnp.concatenate(pieces[JOINT:], axis=2)
    joint = joint.reshape(s.tiles, shard, s.here, 3, s.head).transpose(1, 3, 0, 2, 4)
    joint = joint.reshape(shard, -1).astype(F32)
    expand = into.reshape(s.tiles, shard, s.images, part).transpose(1, 2, 0, 3)
    expand = expand.reshape(shard, -1).astype(F32)
    cls_grad = small[:, : s.step, :shard].reshape(s.lanes, shard)[: s.classes]
    head_grad = jnp.sum(head_rows[:, s.step : s.step + 2, :128], axis=0).reshape(-1)[: s.classes]
    return (
        masks[None],
        grads.patch_grad,
        cls_grad,
        gain_sums(w_qkv, joint)[:, 0] / gain_one[0].astype(F32),
        joint,
        project.astype(F32),
        gain_sums(w_in, expand)[:, 0] / gain_two[0].astype(F32),
        expand,
        back.reshape(-1, s.dim).astype(F32),
        head_grad,
    )


def solution(mesh):
    in_specs = (
        P(IMG, TILE, None),
        P(IMG, TILE, None),
        P(IMG),
        P(None, IMG),
        P(IMG),
        P(IMG, None),
        P(IMG, None),
        P(IMG),
        P(IMG, None),
        P(IMG, None),
        P(),
    )
    out_specs = (
        P(IMG, None, TILE, None),
        P(IMG, TILE, None),
        P(None, IMG),
        P(IMG),
        P(IMG, None),
        P(IMG, None),
        P(IMG),
        P(IMG, None),
        P(IMG, None),
        P(),
    )
    return jax.shard_map(shards, mesh=mesh, in_specs=in_specs, out_specs=out_specs, check_vma=False)
```

```python
import collections
import functools
import types

import jax
import jax.numpy as jnp
import numpy as np
from jax import lax
from jax.experimental import pallas as pl
from jax.experimental.pallas import tpu as pltpu
from jax.sharding import PartitionSpec as P

IMG = "img"
TILE = "tile"
HEADS = 12
WP = 16
UP = 16
BAND = 32
BAND_CELLS = 4
GROUP = 8
EDGE = UP // 2
MESH = pl.DeviceIdType.MESH
LOGIT_UNIT = "logit_unit"
LOGIT_SCALE = "logit_scale"
HEAD_GAIN = "head_gain"
PATCH_UNIT = "patch_unit"
CLASS_UNIT = "class_unit"
FINAL = "final"
W_REDUCE = "w_reduce"
SLOPE = "slope"
W_EXPAND = "w_expand"
ACT = "act"
H_TWO = "h_two"
AFTER = "after"
GAINS = "gains"
W_PROJECT = "w_project"
Q = "q"
KEYS = "keys"
OUTS = "outs"
VALUES = "values"
MIXED_MAIN = "mixed_main"
MIXED_THIRD = "mixed_third"
H_ONE = "h_one"
W_JOINT = "w_joint"
TOKEN_ROWS = "token_rows"
F32 = jnp.float32
BF16 = jnp.bfloat16
PLANE = 2
BACK, INTO, JOINT, LAST, PROJECT = 0, 2, 4, 5, 6
VMEM_BYTES = 62 << 20


def product(left, right):
    return jnp.dot(left, right, preferred_element_type=F32)


def times_transposed(left, right):
    return lax.dot_general(left, right, (((1,), (1,)), ((), ())), preferred_element_type=F32)


def transposed_times(left, right):
    return lax.dot_general(left, right, (((0,), (0,)), ((), ())), preferred_element_type=F32)


def layer_norm_parts(value):
    centre = jnp.mean(value, axis=-1, keepdims=True)
    centred = value - centre
    spread = jnp.mean(centred * centred, axis=-1, keepdims=True)
    scale = lax.rsqrt(spread + 1e-05)
    return centred * scale, scale


def layer_norm_back(unit, scale, gain, upstream):
    weighted = upstream * gain
    mean = jnp.mean(weighted, axis=-1, keepdims=True)
    along = jnp.mean(weighted * unit, axis=-1, keepdims=True)
    return scale * (weighted - mean - unit * along)


def gelu_pair(x):
    root = np.float32(np.sqrt(2.0 / np.pi))
    square = x * x
    turned = jnp.tanh(root * x * (1.0 + np.float32(0.044715) * square))
    half = 0.5 * (1.0 + turned)
    slope = half + 0.5 * x * (1.0 - turned * turned) * root * (
        1.0 + np.float32(3 * 0.044715) * square
    )
    return x * half, slope


def lane_iota(rows, lanes):
    return lax.broadcasted_iota(jnp.int32, (rows, lanes), 1)


def row_iota(rows, lanes):
    return lax.broadcasted_iota(jnp.int32, (rows, lanes), 0)


def carry_copy(k, name, back=False):
    near, far = getattr(k, name), k.far[name]
    n = list(k.far).index(name)
    ends = (far, near) if back else (near, far)
    return pltpu.make_async_copy(*ends, k.carry_sem.at[n])


def keep(k, name):
    if name in k.far:
        carry_copy(k, name).start()


def kept(k):
    for name in k.far:
        carry_copy(k, name).wait()


def fetch_all(k):
    for name in k.far:
        carry_copy(k, name, True).start()


def have(k, *names):
    for name in names:
        if name in k.far:
            carry_copy(k, name, True).wait()


class Net:
    def __init__(self, k):
        self.k = k
        self.sent = []
        self.stage_sends = []

    def send(self, source, target, base, slot, device, when=None):
        k = self.k
        copy = pltpu.make_async_remote_copy(
            src_ref=source,
            dst_ref=target,
            send_sem=k.send_sem.at[len(self.sent)],
            recv_sem=k.recv_sem.at[base + slot],
            device_id=device,
            device_id_type=MESH,
        )
        self.sent.append((copy, when))
        if when is None:
            copy.start()
        else:
            pl.when(when)(copy.start)
        return len(self.sent) - 1

    def arrived(self, target, base, slot):
        k = self.k
        pltpu.make_async_remote_copy(
            src_ref=target,
            dst_ref=target,
            send_sem=k.send_sem.at[0],
            recv_sem=k.recv_sem.at[base + slot],
            device_id=k.sibling,
            device_id_type=MESH,
        ).wait_recv()

    def gone(self, number):
        if self.sent[number] is None:
            return
        copy, when = self.sent[number]
        self.sent[number] = None
        if when is None:
            copy.wait_send()
        else:
            pl.when(when)(copy.wait_send)

    def drain(self):
        for number in range(len(self.sent)):
            self.gone(number)


def place(k):
    k.i = lax.axis_index(IMG)
    k.t = lax.axis_index(TILE)
    k.y = k.i % PLANE
    k.z = k.i // PLANE
    k.planes = k.s.images // PLANE
    k.ts = k.t + 1 - 2 * (k.t % 2)
    k.tx = (k.t + 2) % 4
    k.td = (k.ts + 2) % 4
    k.sibling = (k.i, k.ts)
    k.across = (k.i, k.tx)
    k.diagonal = (k.i, k.td)
    k.mate = (k.i + 1 - 2 * k.y, k.t)


def line_peer(k, step):
    z = (k.z + step) % k.planes
    return z, (PLANE * z + k.y, k.t)


def enter(k, beside=None):
    barrier = pltpu.get_barrier_semaphore()
    peers = [k.sibling, k.across, k.diagonal]
    if k.s.img_comm:
        peers += [k.mate] + [line_peer(k, step)[1] for step in range(1, k.planes)]
    for peer in peers:
        pl.semaphore_signal(barrier, inc=1, device_id=peer, device_id_type=MESH)
    if beside:
        beside()
    pl.semaphore_wait(barrier, len(peers))


def spread_start(k, own, slots, name):
    for step in range(1, k.planes):
        k.net.send(own, slots.at[k.i], name, k.i, line_peer(k, step)[1])
    k.net.send(own, slots.at[k.i], name, k.i, k.mate)


def spread_pass(k, slots, name):
    for step in range(1, k.planes):
        z = (k.z + k.planes - step) % k.planes
        i = PLANE * z + k.y
        k.net.arrived(slots.at[i], name, i)
        k.net.send(slots.at[i], slots.at[i], name, i, k.mate)


def spread_end(k, slots, name):
    for z in range(k.planes):
        i = PLANE * z + 1 - k.y
        k.net.arrived(slots.at[i], name, i)


def line_start(k, own, slots, base, cut):
    send = k.net.send
    own, there = own.at[cut], slots.at[(k.i, *cut)]
    send(own, there, base, k.i, line_peer(k, 1)[1], k.z < k.planes - 1)
    send(own, there, base, k.i, line_peer(k, k.planes - 1)[1], k.z > 0)
    send(own, there, base, k.i, k.mate)


def line_end(k, slots, base, cut):
    for z in range(k.planes):
        i = PLANE * z + 1 - k.y
        k.net.arrived(slots.at[(i, *cut)], base, i)


def line_hop(k, slots, base, far, cut):
    send = k.net.send
    for sign in (-1, 1):
        here = k.z >= far if sign < 0 else k.z < k.planes - far
        more = k.z < k.planes - 1 if sign < 0 else k.z > 0
        i = PLANE * ((k.z + sign * far + k.planes) % k.planes) + k.y
        there = slots.at[(i, *cut)]

        @pl.when(here)
        def _(i=i, there=there):
            k.net.arrived(there, base, i)

        if far < k.planes - 1:
            peer = line_peer(k, 1 if sign < 0 else k.planes - 1)[1]
            send(there, there, base, i, peer, here & more)
        send(there, there, base, i, k.mate, here)


def project_cut(k, tile):
    rows, columns = k.s.dim // k.s.images // 2, k.s.dim // 2
    return (
        pl.ds(pl.multiple_of(rows * (tile // 2), 16), rows),
        pl.ds(pl.multiple_of(columns * (tile % 2), 128), columns),
    )


def project_part(k, tile):
    rows, columns = project_cut(k, tile)
    return k.w_project.at[:, rows, columns]


def slot_part(slots, slot, rows):
    return slots.at[slot] if rows is None else slots.at[slot, rows]


def share_start(k, slots, base, rows=None):
    own = slot_part(slots, k.t, rows)
    k.net.send(own, own, base, k.t, k.across)
    k.net.send(own, own, base, k.t, k.sibling)


def share_pass(k, slots, base, rows=None):
    part = slot_part(slots, k.tx, rows)
    k.net.arrived(part, base, k.tx)
    k.net.send(part, part, base, k.tx, k.sibling)


def halves(s):
    return [pl.ds(n * s.dim // 2, s.dim // 2) for n in range(2)]


def column_cuts(s):
    return [(pl.ds(0, s.rows), columns) for columns in halves(s)]


def row_cuts(s):
    return [(pl.ds(s.own, s.slot), pl.ds(0, s.dim)), (pl.ds(0, s.own), pl.ds(0, s.dim))]


def reduce_over_tile(k, base, part, cuts, before=None, ready=None):
    sends = k.net.stage_sends
    for number in sends:
        k.net.gone(number)
    sends.clear()

    def to_sibling(n, kind, slot):
        at = (kind, *cuts[n])
        k.stage[at] = part(slot, *cuts[n]).astype(BF16)
        sends.append(k.net.send(k.stage.at[at], k.from_sib.at[at], base, 3 * n + kind, k.sibling))

    def near(n):
        if before:
            before(k.t, n)
        k.own_part[cuts[n]] = part(k.t, *cuts[n])
        if before:
            before(k.ts, n)
        to_sibling(n, 0, k.ts)

    if before:
        near(0)
        near(1)
    for n in range(2):
        if ready:
            ready(n)
        if before:
            before(k.tx, n)
            before(k.td, n)
        to_sibling(n, 1, k.td)
        total = part(k.tx, *cuts[n])
        k.across_part[cuts[n]] = total
        k.net.arrived(k.from_sib.at[(1, *cuts[n])], base, 3 * n + 1)
        total = k.across_part[cuts[n]] + k.from_sib[(1, *cuts[n])].astype(F32)
        k.stage[(2, *cuts[n])] = total.astype(BF16)
        ends = k.stage.at[(2, *cuts[n])], k.from_across.at[cuts[n]]
        sends.append(k.net.send(*ends, base, 3 * n + 2, k.across))
        if not before:
            near(n)


def reduced_over_tile(k, base, cuts, which=(0, 1)):
    for n in which:
        k.net.arrived(k.from_sib.at[(0, *cuts[n])], base, 3 * n)
        k.net.arrived(k.from_across.at[cuts[n]], base, 3 * n + 2)
    if len(which) == 1:
        at = cuts[which[0]]
        return k.own_part[at] + k.from_sib[(0, *at)].astype(F32) + k.from_across[at].astype(F32)
    return k.own_part[...] + k.from_sib[0].astype(F32) + k.from_across[...].astype(F32)


def pack_third(s, value):
    return jnp.concatenate([value[: s.pack], value[s.rows - s.pack :]], axis=1)


def third_rows(s, packed):
    rest = 2 * s.pack - s.rows
    return jnp.concatenate([packed[:, : s.head], packed[rest:, s.head :]], axis=0)


def key_bias(k, slot, height):
    s = k.s
    rows = row_iota(s.rows, s.head)
    cls = rows - s.own
    patch_ok = (rows < s.own) & (rows < (height - slot * s.grid) * WP)
    class_ok = (cls >= 0) & (cls < s.step) & (slot * s.step + cls < s.classes)
    off = jnp.where(patch_ok | class_ok, 0.0, -1e30)
    lane = lane_iota(s.rows, s.head)
    return jnp.where(lane == 0, off, jnp.where(lane < 4, 1.0, 0.0))


def class_rows(k, slot):
    s = k.s
    rows = k.cls_rows[pl.ds(pl.multiple_of(slot * s.step, 8), s.step), :]
    return jnp.concatenate([rows, jnp.zeros((s.slot - s.step, s.dim), F32)], axis=0)


def slot_rows(k, slot):
    return pl.ds(pl.multiple_of(slot * k.s.rows, 16), k.s.rows)


def block_scores(k, head, slot):
    return times_transposed(k.q[head, slot_rows(k, slot), :], k.keys[head])


def local_copy(k, source, target, number):
    return pltpu.make_async_copy(source, target, k.local_sem.at[number])


def pick_columns(k):
    s = k.s
    wide = s.here * s.head
    for n in range(4):

        @pl.when(k.t == n)
        def _(n=n):
            cut = [
                k.w_qkv[:, s.dim * m + wide * n + s.head * h :][:, : s.head]
                for h in range(s.here)
                for m in range(3)
            ]
            k.wq[...] = jnp.concatenate(cut, axis=1)


def pick_hidden(k):
    part = k.s.hidden // k.s.images
    for n in range(4):

        @pl.when(k.t == n)
        def _(n=n):
            cut = [k.w_in_near[:, part * (4 * i + n) :][:, :part] for i in range(k.s.images)]
            k.wi[...] = jnp.concatenate(cut, axis=1)


def forward_kernel(k):
    s = k.s
    place(k)
    net = k.net
    i, t = k.i, k.t
    shard = s.dim // s.images

    def prepare():
        head_gain = k.gain_row[...].astype(F32)
        head_gain = jnp.concatenate([head_gain, jnp.zeros((1, s.lanes - s.classes), F32)], axis=1)
        k.head_gain[...] = jnp.broadcast_to(head_gain, (8, s.lanes))
        if s.img_comm:
            rows = [ref[...].astype(F32) for ref in (k.cls_emb, k.gain_one, k.gain_two)]
            rows += [jnp.zeros((s.lanes - s.classes - 2, shard), F32)]
            table = jnp.concatenate(rows, axis=0)
            table = jnp.concatenate([table, jnp.zeros((s.lanes, 128 - shard), F32)], axis=1)
            k.small[...] = table.astype(BF16)
            pick_columns(k)

    patches, labels = k.patches.at[0], k.labels.at[0]
    tokens_in = local_copy(k, patches, k.tokens.at[t], 1)
    tokens_in.start()
    if s.img_comm:
        w_in_copy = local_copy(k, k.w_in, k.w_in_near, 2)
        w_in_copy.start()
        w_back_copy = local_copy(k, k.wb.at[t], k.w_reduce.at[i], 3)
        w_back_copy.start()
    enter(k, prepare)
    keep(k, HEAD_GAIN)
    comm = s.img_comm
    wide = s.here * s.head
    first, second = halves(s)
    early = pl.ds(0, 3 * s.head * (s.here - 1))
    late = pl.ds(3 * s.head * (s.here - 1), 3 * s.head)
    joint = expand = reduce = (None, None)
    project = None
    if comm:
        at = k.at
        every = pl.ds(0, shard)
        joint = ((k.wq, k.w_joint, at.joint0, early), (k.wq, k.w_joint, at.joint1, late))
        expand = ((k.wi, k.w_expand, at.expand0, first), (k.wi, k.w_expand, at.expand1, second))
        back = k.wb.at[t]
        reduce = ((back, k.w_reduce, at.reduce0, first), (back, k.w_reduce, at.reduce1, second))
        joint, expand, reduce = [
            [(*item[:3], (every, item[3])) for item in pair] for pair in (joint, expand, reduce)
        ]
        project = (k.wo, k.w_project, at.w_project, project_cut(k, t))
        wo_copy = local_copy(k, k.wo.at[project[3]], k.w_project.at[(i, *project[3])], 0)
        wo_copy.start()

    def start(item):
        if comm:
            line_start(k, *item)

    def hop(item, far):
        if comm:
            line_hop(k, *item[1:3], far, item[3])

    def end(item):
        if comm:
            line_end(k, *item[1:])

    if comm:
        spread_start(k, k.small, k.smalls, k.at.small)
        k.smalls[i] = k.small[...]
        start(joint[0])
        start(joint[1])
        start(project)
    net.send(patches, k.tokens.at[t], k.at.tokens, t, k.across)
    net.send(patches, k.tokens.at[t], k.at.tokens, t, k.sibling)
    top, bottom, last = pl.ds(0, EDGE), pl.ds(EDGE, EDGE), pl.ds(s.grid * UP - EDGE, EDGE)
    net.send(labels.at[top], k.halo.at[bottom], k.at.halo, 1, (i, (t + 3) % 4))
    net.send(labels.at[last], k.halo.at[top], k.at.halo, 0, (i, (t + 1) % 4))
    if comm:
        k.w_joint[i] = k.wq[...]
        spread_pass(k, k.smalls, k.at.small)
        hop(joint[0], 1)
        hop(joint[1], 1)
        hop(project, 1)
        w_in_copy.wait()
        pick_hidden(k)
        k.w_expand[i] = k.wi[...]
        start(expand[0])
        hop(joint[0], 2)
        hop(joint[1], 2)
        hop(project, 2)
        spread_end(k, k.smalls, k.at.small)
        pieces = [k.smalls[n].astype(F32)[:, :shard] for n in range(s.images)]
        full = jnp.concatenate(pieces, axis=1)
    else:
        full = k.small_full[...].astype(F32)
    k.gains[0:2] = full[s.classes : s.classes + 2]
    k.cls_rows[...] = jnp.where(row_iota(s.lanes, s.dim) < s.classes, full, 0.0)
    gain_one, gain_two = k.gains[0:1], k.gains[1:2]
    keep(k, GAINS)

    def normed_tokens(slot):
        value = jnp.concatenate([k.tokens[slot].astype(F32), class_rows(k, slot)], axis=0)
        k.h_one[slot] = (layer_norm_parts(value)[0] * gain_one).astype(BF16)

    tokens_in.wait()
    k.token_rows[0 : s.own] = k.tokens[t].astype(F32)
    k.token_rows[s.own : s.rows] = class_rows(k, t)
    keep(k, TOKEN_ROWS)
    normed_tokens(t)
    if comm:
        hop(joint[0], 3)
        hop(joint[1], 3)
        hop(project, 3)
        start(expand[1])
    net.arrived(k.tokens.at[k.ts], k.at.tokens, k.ts)
    normed_tokens(k.ts)
    net.arrived(k.tokens.at[k.tx], k.at.tokens, k.tx)
    net.send(k.tokens.at[k.tx], k.tokens.at[k.tx], k.at.tokens, k.tx, k.sibling)
    normed_tokens(k.tx)
    hop(expand[0], 1)
    net.arrived(k.tokens.at[k.td], k.at.tokens, k.td)
    normed_tokens(k.td)
    keep(k, H_ONE)
    if comm:
        end(joint[0])
        end(joint[1])
        keep(k, W_JOINT)
        end(project)
        wo_copy.wait()
        part = project_part(k, t)
        net.send(part, part, at.w_shared, t, k.across)
        net.send(part, part, at.w_shared, t, k.sibling)

    lane = lane_iota(s.rows, s.head)
    one = jnp.where(lane == 0, 1.0, 0.0)
    ones = jnp.where(lane < 2, 1.0, 0.0)
    height = k.height[0]

    def joint_rows(slot):
        value = product(k.h_one[slot], k.w_joint[...].reshape(s.dim, s.here * 3 * s.head))
        bias = key_bias(k, slot, height)
        rows = slot_rows(k, slot)
        for h in range(s.here):
            cut = [
                value[:, (3 * h + n) * s.head : (3 * h + n + 1) * s.head] for n in range(3)
            ]
            for ref, part, extra in zip(
                (k.q, k.keys, k.values), (cut[0] * s.head**-0.5, cut[1], cut[2]), (one, bias, ones)
            ):
                ref[h, rows, :] = jnp.concatenate([part, extra], axis=1).astype(BF16)

    joint_rows(0)
    hop(expand[0], 2)
    joint_rows(1)
    start(reduce[0])
    joint_rows(2)
    hop(expand[0], 3)
    joint_rows(3)
    keep(k, Q)
    keep(k, KEYS)
    keep(k, VALUES)
    hop(expand[1], 1)

    def attend(slot):
        rows = slot_rows(k, slot)
        wide_lane = lane_iota(s.rows, 2 * s.head)
        parts = []
        for h in range(s.here):
            scores = block_scores(k, h, slot)
            largest = jnp.max(scores, axis=-1, keepdims=True)
            powers = jnp.exp(scores - largest).astype(BF16)
            out = product(powers, k.values[h])
            parts.append(out[:, : s.head] / out[:, s.head : s.head + 1])
            k.outs[h, rows, :] = jnp.where(wide_lane == s.head + 1, largest, out)
        k.mixed[slot] = jnp.concatenate(parts, axis=1).astype(BF16)
        k.third_out[slot] = pack_third(s, parts[2]).astype(BF16)

    for step, slot in enumerate((k.tx, k.td, k.ts, t), 1):
        attend(slot)
        if step < 4:
            main = k.mixed.at[slot, :, pl.ds(0, 2 * s.head)]
            net.send(main, k.mixed_main.at[t], k.at.mixed, t, (i, slot))
            net.send(k.third_out.at[slot], k.mixed_third.at[t], k.at.third, t, (i, slot))
        if step == 1:
            hop(expand[1], 2)
            start(reduce[1])
        if step == 2:
            hop(expand[1], 3)
            if comm:
                part = project_part(k, k.tx)
                net.arrived(part, at.w_shared, k.tx)
                net.send(part, part, at.w_shared, k.tx, k.sibling)
        if step == 3:
            hop(reduce[0], 1)
    keep(k, OUTS)
    k.mixed_main[t] = k.mixed[t, :, pl.ds(0, 2 * s.head)]
    k.mixed_third[t] = k.third_out[t]
    hop(reduce[0], 2)
    hop(reduce[0], 3)
    if comm:
        for slot in (k.ts, k.td):
            net.arrived(project_part(k, slot), at.w_shared, slot)
        keep(k, W_PROJECT)
    after = k.token_rows[...]
    w_project = k.w_project[...].reshape(s.dim, s.dim)
    for step in range(1, 4):
        slot = (t + step) % 4
        net.arrived(k.mixed_main.at[slot], k.at.mixed, slot)
        net.arrived(k.mixed_third.at[slot], k.at.third, slot)
    for n in range(4):
        rows = third_rows(s, k.mixed_third[n].astype(F32)).astype(BF16)
        mixed = jnp.concatenate([k.mixed_main[n], rows], axis=1)
        after = after + product(mixed, w_project[wide * n : wide * (n + 1)])
    keep(k, MIXED_MAIN)
    keep(k, MIXED_THIRD)
    k.after[...] = after
    keep(k, AFTER)
    k.h_two[t] = (layer_norm_parts(after)[0] * gain_two).astype(BF16)
    share_start(k, k.h_two, k.at.h_two)
    hop(reduce[1], 1)
    if comm:
        end(expand[0])
        end(expand[1])
        keep(k, W_EXPAND)

    def hidden(slot):
        pre = product(k.h_two[slot], k.w_expand[...].reshape(s.dim, s.hidden))
        act, slope = gelu_pair(pre)
        k.act[slot] = act.astype(BF16)
        k.slope[slot] = slope.astype(BF16)

    hidden(t)
    hop(reduce[1], 2)
    net.arrived(k.h_two.at[k.ts], k.at.h_two, k.ts)
    hidden(k.ts)
    hop(reduce[1], 3)
    share_pass(k, k.h_two, k.at.h_two)
    hidden(k.tx)
    net.arrived(k.h_two.at[k.td], k.at.h_two, k.td)
    hidden(k.td)
    keep(k, H_TWO)
    keep(k, ACT)
    keep(k, SLOPE)

    def contract(slot, rows, columns):
        return product(k.act[slot], k.w_reduce[:, :, columns].reshape(s.hidden, s.dim // 2))

    if comm:
        w_back_copy.wait()
    cuts = column_cuts(s)
    reduce_over_tile(
        k, k.at.feed, contract, cuts, ready=(lambda n: end(reduce[n])) if comm else None
    )
    if comm:
        keep(k, W_REDUCE)
    final = k.after[...] + reduced_over_tile(k, k.at.feed, cuts)
    k.final[...] = final
    keep(k, FINAL)
    unit = (final * lax.rsqrt(jnp.sum(final * final, axis=-1, keepdims=True) + 1e-06)).astype(BF16)
    k.cls_units[t] = unit[s.own :]
    k.patch_unit[WP : WP + s.own] = unit[: s.own]
    above, below = pl.ds(0, WP), pl.ds(WP + s.own, WP)
    for slot in (k.tx, k.td, k.ts):
        net.send(k.cls_units.at[t], k.cls_units.at[t], k.at.units, t, (i, slot))
    net.send(k.patch_unit.at[pl.ds(WP, WP)], k.patch_unit.at[below], k.at.rim, 1, (i, (t + 3) % 4))
    net.send(k.patch_unit.at[pl.ds(s.own, WP)], k.patch_unit.at[above], k.at.rim, 0, (i, (t + 1) % 4))
    for slot in (k.ts, k.tx, k.td):
        net.arrived(k.cls_units.at[slot], k.at.units, slot)
    net.arrived(k.patch_unit.at[above], k.at.rim, 0)
    net.arrived(k.patch_unit.at[below], k.at.rim, 1)
    units = jnp.concatenate([k.cls_units[n].astype(F32)[: s.step] for n in range(4)], axis=0)
    units = jnp.where(row_iota(s.lanes, s.dim) < s.classes, units, 0.0).astype(BF16)
    k.class_unit[...] = units
    keep(k, CLASS_UNIT)
    keep(k, PATCH_UNIT)
    logits = times_transposed(k.patch_unit[...], units)
    unit_logits, scale = class_norm_parts(k, logits)
    k.logit_unit[...] = unit_logits[WP : WP + s.own]
    k.logit_scale[...] = jnp.broadcast_to(scale[WP : WP + s.own], (s.own, 128))
    keep(k, LOGIT_UNIT)
    keep(k, LOGIT_SCALE)
    normed = (unit_logits * k.head_gain[0:1]).astype(BF16)
    k.cells[WP : WP + s.own] = normed[WP : WP + s.own]
    k.cells[:WP] = jnp.where(t == 0, normed[WP : 2 * WP], normed[:WP])
    k.cells[WP + s.own :] = jnp.where(t == 3, normed[s.own : WP + s.own], normed[WP + s.own :])
    net.arrived(k.halo.at[pl.ds(0, EDGE)], k.at.halo, 0)
    net.arrived(k.halo.at[pl.ds(EDGE, EDGE)], k.at.halo, 1)
    kept(k)
    net.drain()


def class_norm_parts(k, value):
    s = k.s
    real = lane_iota(value.shape[0], s.lanes) < s.classes
    centre = jnp.sum(value, axis=-1, keepdims=True) / s.classes
    centred = jnp.where(real, value - centre, 0.0)
    spread = jnp.sum(centred * centred, axis=-1, keepdims=True) / s.classes
    scale = lax.rsqrt(spread + 1e-05)
    return centred * scale, scale


def sum_start(k, name):
    g = k.grads[name]
    k.net.send(g.blocks.at[1 - k.y], g.from_mate, g.at_mate, 0, k.mate)


def sum_pass(k, name):
    g = k.grads[name]
    k.net.arrived(g.from_mate, g.at_mate, 0)
    for step in range(k.planes):
        z = (k.z + step) % k.planes
        both = g.blocks[k.y, z].astype(F32) + g.from_mate[z].astype(F32)
        g.blocks[k.y, z] = both.astype(BF16)
        if step:
            k.net.send(g.blocks.at[k.y, z], g.from_line.at[k.z], g.at_line, k.z, line_peer(k, step)[1])


def sum_end(k, name):
    g = k.grads[name]
    total = g.blocks[k.y, k.z].astype(F32)
    for step in range(1, k.planes):
        z = (k.z + step) % k.planes
        k.net.arrived(g.from_line.at[z], g.at_line, z)
        total = total + g.from_line[z].astype(F32)
    g.out[k.t] = total.astype(BF16)
    if name != LAST:
        share_start(k, g.out, g.at_out)
        return
    for slot in (k.tx, k.td, k.ts):
        k.net.send(g.out.at[k.t], g.out.at[k.t], g.at_out, k.t, (k.i, slot))


def sum_share(k, name):
    g = k.grads[name]
    share_pass(k, g.out, g.at_out)


def sum_close(k, name):
    g = k.grads[name]
    if name == LAST:
        k.net.arrived(g.out.at[k.tx], g.at_out, k.tx)
    k.net.arrived(g.out.at[k.ts], g.at_out, k.ts)
    k.net.arrived(g.out.at[k.td], g.at_out, k.td)


def put_blocks(k, name, value):
    g = k.grads[name]
    if not k.s.img_comm:
        g.out[...] = value.astype(BF16)
        return
    rows = value.shape[0] // k.s.images
    for i in range(k.s.images):
        g.blocks[i % PLANE, i // PLANE] = value[rows * i : rows * (i + 1)].astype(BF16)


def head_powers(k, h):
    s = k.s
    out = k.outs[h]
    total = out[:, s.head + 1 : s.head + 2] + jnp.log(out[:, s.head : s.head + 1])
    first = total.astype(BF16).astype(F32)
    second = (total - first).astype(BF16).astype(F32)
    lane = lane_iota(4 * s.rows, 2 * s.head) - s.head
    value = jnp.where(lane == 1, -first, k.q[h].astype(F32))
    value = jnp.where(lane == 2, -second, value)
    k.q_back[h] = jnp.where(lane == 3, first + second - total, value).astype(BF16)

    def block(slot, carry):
        rows = slot_rows(k, slot)
        scores = times_transposed(k.keys[h, rows, :], k.q_back[h])
        k.powers[h, rows, :] = jnp.exp(scores).astype(BF16)
        return carry

    lax.fori_loop(0, 4, block, 0, unroll=True)


def backward_kernel(k):
    s = k.s
    place(k)
    fetch_all(k)
    enter(k)
    net = k.net
    i, t = k.i, k.t
    comm = s.img_comm
    split = s.own // 2
    first_part, patch_part = pl.ds(0, split), pl.ds(split, s.own - split)
    class_part = pl.ds(s.own, s.slot)

    top = jnp.where(t == 0, k.cell_sums[:WP], 0.0)
    bottom = jnp.where(t == 3, k.cell_sums[WP + s.own :], 0.0)
    own = k.cell_sums[WP : WP + s.own]
    own = jnp.concatenate(
        [own[:WP] + top, own[WP : s.own - WP], own[s.own - WP :] + bottom], axis=0
    )
    upstream = own.astype(BF16).astype(F32)
    have(k, LOGIT_UNIT, LOGIT_SCALE, HEAD_GAIN, PATCH_UNIT, CLASS_UNIT, FINAL)
    unit, scale = k.logit_unit[...], k.logit_scale[:, :1]
    weighted = upstream * k.head_gain[0:1]
    mean = jnp.sum(weighted, axis=-1, keepdims=True) / s.classes
    along = jnp.sum(weighted * unit, axis=-1, keepdims=True) / s.classes
    head_row = jnp.sum(upstream * unit, axis=0, keepdims=True)
    d_logits = scale * (weighted - mean - unit * along)
    d_logits = jnp.where(lane_iota(s.own, s.lanes) < s.classes, d_logits, 0.0).astype(BF16)
    d_class = transposed_times(d_logits, k.patch_unit[WP : WP + s.own])
    for n in range(4):
        k.class_out[n] = jnp.concatenate(
            [d_class[s.step * n : s.step * (n + 1)], jnp.zeros((s.slot - s.step, s.dim), F32)], axis=0
        ).astype(BF16)
    for slot in (k.ts, k.tx, k.td):
        net.send(k.class_out.at[slot], k.class_in.at[t], k.at.class_, t, (i, slot))
    final = k.final[...]
    c = lax.rsqrt(jnp.sum(final * final, axis=-1, keepdims=True) + 1e-06)
    u = final * c

    def unit_back(rows, du):
        return c[rows] * (du - u[rows] * jnp.sum(u[rows] * du, axis=-1, keepdims=True))

    d_patch = unit_back(slice(0, s.own), product(d_logits, k.class_unit[...]))
    k.d_rows[: s.own] = d_patch
    k.d_branch[t, : s.own] = d_patch.astype(BF16)
    share_start(k, k.d_branch, k.at.d_first, first_part)
    share_start(k, k.d_branch, k.at.d_branch, patch_part)
    d_class_unit = k.class_out[t].astype(F32)
    for slot in (k.ts, k.tx, k.td):
        net.arrived(k.class_in.at[slot], k.at.class_, slot)
        d_class_unit = d_class_unit + k.class_in[slot].astype(F32)
    d_class = unit_back(slice(s.own, s.rows), d_class_unit)
    k.d_rows[s.own :] = d_class
    k.d_branch[t, s.own :] = d_class.astype(BF16)
    share_start(k, k.d_branch, k.at.d_class, class_part)

    have(k, W_REDUCE, SLOPE, W_EXPAND)

    every = pl.ds(0, s.dim)
    cuts = [(first_part, every), (pl.ds(split, s.rows - split), every)]

    def contract_back(slot, n):
        rows = cuts[n][0]
        d_act = times_transposed(k.d_branch[slot, rows], k.w_reduce[...].reshape(s.hidden, s.dim))
        k.d_pre[slot, rows] = (d_act * k.slope[slot, rows].astype(F32)).astype(BF16)

    def expand_back(slot, rows, columns):
        return times_transposed(k.d_pre[slot, rows], k.w_expand[...].reshape(s.dim, s.hidden))

    def before(slot, n):
        parts = ((first_part, k.at.d_first),)
        if n:
            parts = ((patch_part, k.at.d_branch), (class_part, k.at.d_class))
        if slot is k.tx and n == 0:
            have(k, Q, KEYS, OUTS)
            head_powers(k, 0)
        if slot is k.tx and n == 1:
            head_powers(k, 1)
        for rows, base in parts:
            if slot is k.tx:
                share_pass(k, k.d_branch, base, rows)
            elif slot is not t:
                net.arrived(k.d_branch.at[slot, rows], base, slot)
        contract_back(slot, n)

    reduce_over_tile(k, k.at.feed, expand_back, cuts, before)
    tall = 4 * s.rows
    have(k, ACT, H_TWO)
    for n, columns in enumerate(halves(s)):
        right = k.d_branch[:, :, columns].reshape(tall, s.dim // 2)
        put_blocks(k, BACK + n, transposed_times(k.act[...].reshape(tall, s.hidden), right))
        if comm:
            sum_start(k, BACK + n)
    for n, columns in enumerate(halves(s)):
        right = k.d_pre[:, :, columns].reshape(tall, s.hidden // 2)
        put_blocks(k, INTO + n, transposed_times(k.h_two[...].reshape(tall, s.dim), right))
        if comm:
            sum_start(k, INTO + n)
    head_powers(k, 2)

    have(k, AFTER, GAINS, W_PROJECT, VALUES, MIXED_MAIN, MIXED_THIRD, H_ONE, W_JOINT, TOKEN_ROWS)
    unit, scale = layer_norm_parts(k.after[...])
    part = layer_norm_back(unit, scale, k.gains[1:2], reduced_over_tile(k, k.at.feed, cuts))
    d_after = k.d_rows[...] + part
    k.d_rows[...] = d_after
    d_attn = d_after.astype(BF16)
    wide = s.here * s.head
    for slot in (k.tx, k.td, k.ts, t):
        if comm:
            rows = k.w_project[pl.ds(PLANE * slot, PLANE)].reshape(wide, s.dim)
        else:
            rows = k.w_project[0, pl.ds(pl.multiple_of(slot * wide, 16), wide), :]
        value = times_transposed(d_attn, rows)
        k.main_out[slot] = value[:, : 2 * s.head].astype(BF16)
        k.third_out[slot] = pack_third(s, value[:, 2 * s.head :]).astype(BF16)
        if slot is not t:
            net.send(k.main_out.at[slot], k.main_in.at[t], k.at.d_mixed, t, (i, slot))
    for slot in (k.tx, k.td, k.ts):
        net.send(k.third_out.at[slot], k.third_in.at[t], k.at.third, t, (i, slot))
    k.main_in[t] = k.main_out[t]
    k.third_in[t] = k.third_out[t]
    project_start(k, d_attn)
    if comm:
        sum_pass(k, BACK)
        project_across(k)
        sum_pass(k, BACK + 1)

    for slot in (k.ts, k.tx, k.td):
        net.arrived(k.main_in.at[slot], k.at.d_mixed, slot)

    for h in range(s.here):
        if comm and h == 2:
            sum_pass(k, INTO + 1)
        out = k.outs[h]
        if h < 2:
            d_mixed = k.main_in[...].reshape(tall, 2 * s.head)[:, s.head * h :][:, : s.head].astype(F32)
        else:
            for slot in (k.ts, k.tx, k.td):
                net.arrived(k.third_in.at[slot], k.at.third, slot)
            thirds = [third_rows(s, k.third_in[n].astype(F32)) for n in range(4)]
            d_mixed = jnp.concatenate(thirds, axis=0)
        along = jnp.sum(d_mixed * out[:, : s.head], axis=-1, keepdims=True)
        along = along / out[:, s.head : s.head + 1]
        high = along.astype(BF16).astype(F32)
        lane = lane_iota(tall, s.head)
        tail = jnp.where(lane == 0, -high, jnp.where(lane == 1, high - along, 0.0))
        k.d_out[...] = jnp.concatenate([d_mixed, tail], axis=1).astype(BF16)

        def block(slot, carry, h=h):
            rows = slot_rows(k, slot)
            powers = k.powers[h, rows, :]
            slopes = times_transposed(k.values[h, rows, :], k.d_out[...])
            d_scores = (powers.astype(F32) * slopes).astype(BF16)
            k.d_scores[rows, :] = d_scores
            d_k = product(d_scores, k.q_back[h])
            d_v = product(powers, k.d_out[...])
            both = jnp.concatenate([d_k[:, : s.head], d_v[:, : s.head]], axis=1)
            k.d_pair[rows, :] = both
            return carry

        lax.fori_loop(0, 4, block, 0)
        if comm and h == 0:
            project_end(k)
            sum_pass(k, INTO)
        if comm and h == 1:
            sum_end(k, BACK)
        if comm and h == 2:
            sum_share(k, BACK)
            sum_share(k, BACK + 1)
            sum_end(k, INTO)
            sum_pass(k, PROJECT)
        d_q = transposed_times(k.keys[h][:, : s.head], k.d_scores[...]).T * s.head**-0.5
        k.d_joint[h] = jnp.concatenate([d_q, k.d_pair[...]], axis=1).astype(BF16)
        if h == s.here - 2:
            pair = jnp.concatenate([k.d_joint[n] for n in range(h + 1)], axis=1)
            put_blocks(k, JOINT, transposed_times(k.h_one[...].reshape(tall, s.dim), pair))
        if h == s.here - 1:
            put_blocks(k, LAST, transposed_times(k.h_one[...].reshape(tall, s.dim), k.d_joint[h]))
        if comm and h >= s.here - 2:
            sum_start(k, JOINT if h == s.here - 2 else LAST)
        if comm and h == 1:
            sum_end(k, BACK + 1)

    w_joint = k.w_joint[...].reshape(s.dim, 3 * wide)

    def joint_back(slot, rows, columns):
        rows = pl.ds(pl.multiple_of(slot * s.rows + rows.start, 16), rows.size)
        left = jnp.concatenate([k.d_joint[h, rows, :] for h in range(s.here)], axis=1)
        return times_transposed(left, w_joint)

    cuts = row_cuts(s)
    reduce_over_tile(k, k.at.joint, joint_back, cuts)
    unit, scale = layer_norm_parts(k.token_rows[...])
    if comm:
        sum_pass(k, JOINT)
        sum_share(k, INTO)
        sum_end(k, INTO + 1)

    def norm_back(rows, upstream):
        return k.d_rows[rows] + layer_norm_back(unit[rows], scale[rows], k.gains[0:1], upstream)

    own_rows, cls_rows = slice(0, s.own), slice(s.own, s.rows)
    table = norm_back(cls_rows, reduced_over_tile(k, k.at.joint, cuts, (0,)))
    table = jnp.where(row_iota(s.slot, s.dim) < s.step, table, 0.0)
    rows = row_iota(s.slot, 128)
    head_rows = jnp.where(rows == s.step, head_row[:, :128], 0.0)
    rest = jnp.concatenate([head_row[:, 128:], jnp.zeros((1, 256 - s.lanes), F32)], axis=1)
    head_rows = jnp.where(rows == s.step + 1, rest, head_rows)
    if comm:
        small_start(k, table, head_rows)
        sum_pass(k, LAST)
        sum_end(k, PROJECT)
        small_end(k)
        sum_share(k, INTO + 1)
        sum_end(k, JOINT)
        sum_share(k, PROJECT)
    k.patch_grad[0] = norm_back(own_rows, reduced_over_tile(k, k.at.joint, cuts, (1,)))
    if not comm:
        k.small_out[...] = table
        k.head_out[...] = head_rows
        net.drain()
        return
    sum_end(k, LAST)
    sum_share(k, JOINT)
    for name in range(len(k.grads)):
        sum_close(k, name)
    for slot in (k.ts, k.tx, k.td):
        net.arrived(k.small_sum.at[slot], k.at.small_sum, slot)
    net.drain()


def project_start(k, d_attn):
    s = k.s
    shard = s.dim // s.images
    rows, columns = shard // 2, s.dim // 2
    for m in range(4):
        third = third_rows(s, k.mixed_third[m].astype(F32)).astype(BF16)
        mixed = jnp.concatenate([k.mixed_main[m], third], axis=1)
        value = transposed_times(mixed, d_attn).astype(BF16)
        if not s.img_comm:
            wide = s.here * s.head
            k.d_project[wide * m : wide * (m + 1)] = value
            continue
        for n in range(4):
            for y in range(PLANE):
                first = shard * y + rows * (n // 2)
                cut = value[first : first + rows, columns * (n % 2) :][:, :columns]
                k.p_out[n, PLANE * m + y] = cut
    if s.img_comm:
        k.net.send(k.p_out.at[k.td], k.p_sib.at[1], k.at.project, 1, k.sibling)
        k.net.send(k.p_out.at[k.ts], k.p_sib.at[0], k.at.project, 0, k.sibling)


def project_across(k):
    k.net.arrived(k.p_sib.at[1], k.at.project, 1)
    k.p_stage[...] = (k.p_out[k.tx].astype(F32) + k.p_sib[1].astype(F32)).astype(BF16)
    k.net.send(k.p_stage, k.p_across, k.at.project, 2, k.across)


def project_end(k):
    blocks = k.grads[PROJECT].blocks
    k.net.arrived(k.p_sib.at[0], k.at.project, 0)
    k.net.arrived(k.p_across, k.at.project, 2)
    total = k.p_out[k.t].astype(F32) + k.p_sib[0].astype(F32) + k.p_across[...].astype(F32)
    for i in range(k.s.images):
        blocks[i % PLANE, i // PLANE] = total[i].astype(BF16)
    sum_start(k, PROJECT)


def small_start(k, table, head_rows):
    s = k.s
    shard = s.dim // s.images
    pad = jnp.zeros((s.slot, 128 - shard), F32)
    for n in range(s.images):
        cut = jnp.concatenate([table[:, shard * n : shard * (n + 1)], pad], axis=1)
        k.small_out[n] = (cut + head_rows).astype(BF16)
    for step in range(1, s.images):
        n = (k.i + step) % s.images
        k.net.send(k.small_out.at[n], k.small_in.at[k.i], k.at.small, k.i, (n, k.t))


def small_end(k):
    s = k.s
    total = k.small_out[k.i].astype(F32)
    for step in range(1, s.images):
        n = (k.i + step) % s.images
        k.net.arrived(k.small_in.at[n], k.at.small, n)
        total = total + k.small_in[n].astype(F32)
    k.small_sum[k.t] = total
    for slot in (k.ts, k.tx, k.td):
        k.net.send(k.small_sum.at[k.t], k.small_sum.at[k.t], k.at.small_sum, k.t, (k.i, slot))


def gain_sums(weight, grad):
    return jnp.sum(weight.astype(F32) * grad, axis=1, keepdims=True)


def write_kernel(k):
    s = k.s
    shard = s.dim // s.images
    k.patch_grad[...] = k.patch_rows[...]
    half = s.dim // 2
    for n in range(2):
        k.d_w_back[:, half * n : half * (n + 1)] = k.back[n][...].astype(F32).reshape(4 * shard, half)
    part = s.hidden // s.images
    cut = [jnp.concatenate([ref[n].astype(F32) for ref in k.into], axis=1) for n in range(4)]
    cut = [cut[n][:, part * i : part * (i + 1)] for i in range(s.images) for n in range(4)]
    k.d_w_in[...] = jnp.concatenate(cut, axis=1)
    both = [[k.pair[n].astype(F32), k.last[n].astype(F32)] for n in range(4)]
    split = s.here - 1
    for m in range(3):
        cut = [
            both[n][h // split][:, s.head * (3 * (h % split) + m) :][:, : s.head]
            for n in range(4)
            for h in range(s.here)
        ]
        k.d_w_qkv[:, s.dim * m : s.dim * (m + 1)] = jnp.concatenate(cut, axis=1)
    for n in range(4):
        rows, columns = shard // 2 * (n // 2), half * (n % 2)
        k.d_w_out[rows : rows + shard // 2, columns : columns + half] = k.project[n].astype(F32)
    rows = jnp.concatenate([k.small_sum[n][: s.step] for n in range(4)], axis=0)
    k.d_cls[...] = rows[: s.classes, :shard]
    rest = k.small_sum[0] + k.small_sum[1] + k.small_sum[2] + k.small_sum[3]
    one = gain_sums(k.w_qkv[...], k.d_w_qkv[...])
    two = gain_sums(k.w_in[...], k.d_w_in[...])
    both = jnp.concatenate([one, two, jnp.zeros((shard, 126), F32)], axis=1).T
    k.d_gain_one[...] = both[0:1] / k.gain_one[...].astype(F32)
    k.d_gain_two[...] = both[1:2] / k.gain_two[...].astype(F32)
    head = jnp.concatenate([rest[s.step : s.step + 1], rest[s.step + 1 : s.step + 2]], axis=1)
    k.d_head[...] = head[:, : s.classes]


def tent(pixels, cells, first):
    place = (np.arange(pixels) + 0.5) / UP - 0.5 - first
    return np.maximum(0.0, 1.0 - np.abs(place[:, None] - np.arange(cells)[None, :]))


def band_tables():
    edge = tent(2 * UP, 2, 0)[EDGE : 3 * EDGE]
    edge = np.concatenate([edge[:EDGE], np.zeros((EDGE, 2)), np.zeros((EDGE, 2)), edge[EDGE:]], axis=0)
    edge = edge.reshape(2, 2 * EDGE, 2).transpose(1, 0, 2).reshape(2 * EDGE, BAND_CELLS)
    across = (np.clip((np.arange(WP * UP) + 0.5) / UP - 0.5, 0, WP - 1))[None, :]
    across = np.maximum(0.0, 1.0 - np.abs(across - np.arange(WP)[:, None]))
    down = tent(BAND, BAND_CELLS, -1)
    tables = [across]
    for table in (down, edge):
        rows = table.shape[0]
        up = np.zeros((GROUP, rows, 2, BAND_CELLS, GROUP), np.float32)
        back = np.zeros((BAND_CELLS, GROUP, GROUP, rows), np.float32)
        for c in range(GROUP):
            up[c, :, :, :, c] = table[:, None, :]
            back[:, c, c, :] = table.T
        tables.append(up.reshape(GROUP * rows, 2 * BAND_CELLS * GROUP))
        tables.append(back.reshape(BAND_CELLS * GROUP, GROUP * rows))
    return [jnp.asarray(t, BF16) for t in tables]


def two_parts(value):
    high = value.astype(BF16)
    return high, (value - high.astype(F32)).astype(BF16)


def upsample_kernel(
    classes, bands, height_ref, cell_ref, label_ref, halo_ref, across_ref, up_ref, back_ref,
    edge_up_ref, edge_back_ref, mask_ref, sum_ref, wide, wide_grad, powers,
):
    band = pl.program_id(0)
    groups = -(-classes // GROUP)
    tail = classes - GROUP * (groups - 1)
    cell_rows = cell_ref.shape[0] // WP
    pixels = label_ref.shape[2]
    tile = lax.axis_index(TILE)
    limit = (height_ref[0] - tile * (bands * BAND // UP)) * UP
    share = 1.0 / (UP * UP)
    counts = [GROUP] * (groups - 1) + [tail]

    @pl.when(band == 0)
    def _():
        for r in range(cell_rows):
            wide[r] = lax.dot_general(
                cell_ref[WP * r : WP * (r + 1), :], across_ref[...], (((0,), (0,)), ((), ())),
                preferred_element_type=F32,
            )
        wide_grad[...] = jnp.zeros_like(wide_grad)

    def pixel_rows(rows, label, first, second, up, back, masked):
        def forward(g, total, count):
            at = pl.ds(GROUP * g, GROUP)
            part = jnp.concatenate([wide[pl.ds(r, 2), at, :] for r in (first, second)], axis=0)
            both = jnp.concatenate(two_parts(part.reshape(BAND_CELLS * GROUP, pixels)), axis=0)
            upsampled = product(up[: count * rows, :], both).reshape(count, rows, pixels)
            if masked:
                mask_ref[pl.ds(GROUP * g, count)] = upsampled.astype(BF16)
            power = jnp.exp(upsampled)
            powers[pl.ds(GROUP * g, count), :rows] = power
            return total + jnp.sum(power, axis=0)

        total = jnp.zeros((rows, pixels), F32)
        for g, count in enumerate(counts):
            total = forward(g, total, count)
        inverse = jnp.where(label >= 0, share, 0.0) / total
        for g, count in enumerate(counts):
            parts = []
            for c in range(count):
                target = jnp.where(label == GROUP * g + c, share, 0.0)
                parts.append((powers[GROUP * g + c, :rows] * inverse - target).astype(BF16))
            summed = product(back[:, : count * rows], jnp.concatenate(parts, axis=0))
            summed = summed.reshape(BAND_CELLS, GROUP, pixels)
            at = pl.ds(GROUP * g, GROUP)
            wide_grad[pl.ds(first, 2), at, :] += summed[:2]
            wide_grad[pl.ds(second, 2), at, :] += summed[2:]

    @pl.when(band < bands)
    def _():
        rows = lax.broadcasted_iota(jnp.int32, (BAND, pixels), 0) + BAND * band
        label = jnp.where(rows < limit, label_ref[0], -1)
        first = BAND // UP * band
        pixel_rows(BAND, label, first, first + 2, up_ref, back_ref, True)

    @pl.when(band == bands)
    def _():
        rows = lax.broadcasted_iota(jnp.int32, (2 * EDGE, pixels), 0)
        below = rows >= EDGE
        rows = rows - EDGE + jnp.where(below, bands * BAND, 0)
        label = jnp.where((rows < limit) & (below | (tile > 0)), halo_ref[...], -1)
        pixel_rows(2 * EDGE, label, 0, cell_rows - 2, edge_up_ref, edge_back_ref, False)
        for r in range(cell_rows):
            high, low = two_parts(wide_grad[r])
            sum_ref[WP * r : WP * (r + 1), :] = times_transposed(
                across_ref[...], high
            ) + times_transposed(across_ref[...], low)


def upsampled_loss(cells, labels, halo, heights, classes):
    rows, lanes = cells.shape[0] // WP, cells.shape[1]
    tile_pixels, wide_pixels = labels.shape[1:]
    tables = band_tables()
    bands = tile_pixels // BAND

    def whole(shape):
        return pl.BlockSpec(shape, lambda i: (0,) * len(shape))

    return pl.pallas_call(
        functools.partial(upsample_kernel, classes, bands),
        grid=(bands + 1,),
        out_shape=(
            jax.ShapeDtypeStruct((classes, tile_pixels, wide_pixels), BF16),
            jax.ShapeDtypeStruct(cells.shape, F32),
        ),
        in_specs=[
            pl.BlockSpec(memory_space=pltpu.SMEM),
            whole(cells.shape),
            pl.BlockSpec((1, BAND, wide_pixels), lambda i: (0, jnp.minimum(i, bands - 1), 0)),
            whole(halo.shape),
        ]
        + [whole(t.shape) for t in tables],
        out_specs=(
            pl.BlockSpec((classes, BAND, wide_pixels), lambda i: (0, jnp.minimum(i, bands - 1), 0)),
            whole(cells.shape),
        ),
        scratch_shapes=[
            pltpu.VMEM((rows, lanes, wide_pixels), F32),
            pltpu.VMEM((rows, lanes, wide_pixels), F32),
            pltpu.VMEM((lanes, BAND, wide_pixels), F32),
        ],
        compiler_params=pltpu.CompilerParams(vmem_limit_bytes=56 << 20),
        name=upsample_kernel.__name__,
    )(heights, cells, labels, halo, *tables)


CELLS = "cells"
HALO = "halo"
FAR_INPUTS = ("patches", "labels", "wo", "w_in", "wb")
CARRIED = (
    LOGIT_UNIT,
    LOGIT_SCALE,
    HEAD_GAIN,
    PATCH_UNIT,
    CLASS_UNIT,
    FINAL,
    W_REDUCE,
    SLOPE,
    W_EXPAND,
    ACT,
    H_TWO,
    AFTER,
    GAINS,
    W_PROJECT,
    Q,
    KEYS,
    OUTS,
    VALUES,
    MIXED_MAIN,
    MIXED_THIRD,
    H_ONE,
    W_JOINT,
    TOKEN_ROWS,
)
GRAD_REFS = ("out", "blocks", "from_mate", "from_line")
GRAD_PLACES = ("at_mate", "at_line", "at_out")
Grad = collections.namedtuple("Grad", GRAD_REFS + GRAD_PLACES)


def run_kernel(body, s, inputs, outputs, scratch, recv, sends, number, carried, back=False):
    if back:
        inputs.update({n: inputs.pop(n) for n in carried})
        near = {n: (inputs[n].shape, inputs[n].dtype) for n in carried}
    else:
        near = {n: outputs.pop(n) for n in carried}
        outputs = {**near, **outputs}
    scratch = {**near, **scratch}
    names_in, names_out, names_scratch = list(inputs), list(outputs), list(scratch)

    places = types.SimpleNamespace()
    arrivals = 0
    for name, count in recv.items():
        setattr(places, name, arrivals)
        arrivals += count

    def kernel(*refs):
        k = types.SimpleNamespace(s=s, at=places)
        for name, ref in zip(names_in + names_out + names_scratch, refs):
            setattr(k, name, ref)
        k.far = {}
        for name, ref in zip(carried, refs[len(names_in) - len(carried) :] if back else refs[len(names_in) :]):
            k.far[name] = ref
        for name, ref in zip(carried, refs[len(names_in) + len(names_out) :]):
            setattr(k, name, ref)
        k.send_sem, k.recv_sem, k.carry_sem, k.local_sem = refs[-4:]
        k.net = Net(k)
        k.grads = []
        for n in range(PROJECT + 1):
            of = [getattr(k, word + str(n), None) for word in GRAD_REFS]
            at = [getattr(places, word + str(n), None) for word in GRAD_PLACES]
            k.grads.append(Grad(*of, *at))
        body(k)

    def space(name):
        if name in carried or name in FAR_INPUTS:
            return pl.BlockSpec(memory_space=pl.ANY)
        scalar = name in inputs and inputs[name].ndim == 1
        return pl.BlockSpec(memory_space=pltpu.SMEM if scalar else pltpu.VMEM)

    results = pl.pallas_call(
        kernel,
        out_shape=[jax.ShapeDtypeStruct(*outputs[n]) for n in names_out],
        in_specs=[space(n) for n in names_in],
        out_specs=[space(n) for n in names_out],
        scratch_shapes=[pltpu.VMEM(*scratch[n]) for n in names_scratch]
        + [pltpu.SemaphoreType.DMA((sends,)), pltpu.SemaphoreType.DMA((arrivals,)), pltpu.SemaphoreType.DMA((len(carried),)), pltpu.SemaphoreType.DMA((4,))],
        compiler_params=pltpu.CompilerParams(
            collective_id=number, has_side_effects=True, vmem_limit_bytes=VMEM_BYTES
        ),
        name=body.__name__,
    )(*inputs.values())
    return dict(zip(names_out, results))


def reduce_scratch(s):
    return dict(
        stage=((3, s.rows, s.dim), BF16),
        from_sib=((2, s.rows, s.dim), BF16),
        from_across=((s.rows, s.dim), BF16),
        own_part=((s.rows, s.dim), F32),
        across_part=((s.rows, s.dim), F32),
    )


def forward_call(s, inputs):
    wide = s.here * s.head
    all_rows = 4 * s.rows
    outputs = dict(
        h_one=((4, s.rows, s.dim), BF16),
        q=((s.here, all_rows, 2 * s.head), BF16),
        keys=((s.here, all_rows, 2 * s.head), BF16),
        values=((s.here, all_rows, 2 * s.head), BF16),
        outs=((s.here, all_rows, 2 * s.head), F32),
        mixed_main=((4, s.rows, 2 * s.head), BF16),
        mixed_third=((4, s.pack, 2 * s.head), BF16),
        token_rows=((s.rows, s.dim), F32),
        after=((s.rows, s.dim), F32),
        h_two=((4, s.rows, s.dim), BF16),
        act=((4, s.rows, s.hidden), BF16),
        slope=((4, s.rows, s.hidden), BF16),
        final=((s.rows, s.dim), F32),
        patch_unit=((s.own + 2 * WP, s.dim), BF16),
        head_gain=((8, s.lanes), F32),
        class_unit=((s.lanes, s.dim), BF16),
        logit_unit=((s.own, s.lanes), F32),
        logit_scale=((s.own, 128), F32),
        cells=((s.own + 2 * WP, s.lanes), BF16),
        halo=((2 * EDGE, s.wide_pixels), jnp.int32),
        gains=((8, s.dim), F32),
    )
    scratch = dict(
        tokens=((4, s.own, s.dim), BF16),
        cls_rows=((s.lanes, s.dim), F32),
        mixed=((4, s.rows, wide), BF16),
        third_out=((4, s.pack, 2 * s.head), BF16),
        cls_units=((4, s.slot, s.dim), BF16),
        **reduce_scratch(s),
    )
    recv = dict(tokens=4, mixed=4, third=4, h_two=4, feed=6, units=4, rim=2, halo=2)
    sends = 3 + 6 + 3 + 6 + 3 + 2 + 2
    if s.img_comm:
        shard = s.dim // s.images
        outputs.update(w_joint=((s.images, shard, 3 * wide), BF16))
        outputs.update(w_project=((s.images, shard, s.dim), BF16))
        scratch.update(small=((s.lanes, 128), BF16), wq=((shard, 3 * wide), BF16))
        scratch.update(wi=((shard, s.hidden), BF16), w_in_near=((shard, 4 * s.hidden), BF16))
        outputs.update(w_expand=((s.images, shard, s.hidden), BF16))
        outputs.update(w_reduce=((s.images, shard, s.dim), BF16))
        scratch.update(smalls=((s.images, s.lanes, 128), BF16))
        n = s.images
        recv.update(small=n, joint0=n, joint1=n, w_project=n, w_shared=4)
        recv.update(expand0=n, expand1=n, reduce0=n, reduce1=n)
        sends += 2 * (n // PLANE) - 1 + 7 * (4 * (n // PLANE) - 3) + 3
    carried = [n for n in CARRIED if n in outputs]
    return run_kernel(forward_kernel, s, inputs, outputs, scratch, recv, sends, 1, carried)


def backward_call(s, inputs, carried):
    wide = s.here * s.head
    all_rows = 4 * s.rows
    outputs = dict(patch_grad=((1, s.own, s.dim), F32))
    scratch = dict(
        class_out=((4, s.slot, s.dim), BF16),
        class_in=((4, s.slot, s.dim), BF16),
        d_rows=((s.rows, s.dim), F32),
        d_branch=((4, s.rows, s.dim), BF16),
        d_pre=((4, s.rows, s.hidden), BF16),
        main_out=((4, s.rows, 2 * s.head), BF16),
        main_in=((4, s.rows, 2 * s.head), BF16),
        third_out=((4, s.pack, 2 * s.head), BF16),
        third_in=((4, s.pack, 2 * s.head), BF16),
        powers=((s.here, all_rows, all_rows), BF16),
        d_scores=((all_rows, all_rows), BF16),
        d_out=((all_rows, 2 * s.head), BF16),
        q_back=((s.here, all_rows, 2 * s.head), BF16),
        d_pair=((all_rows, 2 * s.head), F32),
        d_joint=((s.here, all_rows, 3 * s.head), BF16),
        **reduce_scratch(s),
    )
    recv = dict(class_=4, d_branch=4, d_first=4, d_class=4, feed=6, d_mixed=4, third=4, joint=6)
    sends = 3 + 3 + 3 + 3 + 6 + 6 + 6
    columns = [s.dim // 2] * 2 + [s.hidden // 2] * 2 + [3 * s.head * (s.here - 1), 3 * s.head]
    columns += [s.dim // 2] * s.img_comm
    planes, shard = s.images // PLANE, s.dim // s.images
    for n, cols in enumerate(columns):
        out, blocks, from_mate, from_line = [word + str(n) for word in GRAD_REFS]
        at_mate, at_line, at_out = [word + str(n) for word in GRAD_PLACES]
        if not s.img_comm:
            outputs[out] = ((s.dim, cols), BF16)
            continue
        rows = shard // 2 if n == PROJECT else shard
        outputs[out] = ((4, rows, cols), BF16)
        scratch[blocks] = ((PLANE, planes, rows, cols), BF16)
        for what in (from_mate, from_line):
            scratch[what] = ((planes, rows, cols), BF16)
        recv[at_mate] = 1
        recv[at_line] = planes
        recv[at_out] = 4
        sends += 1 + planes - 1 + 3
    if s.img_comm:
        outputs.update(small_sum=((4, s.slot, 128), F32))
        piece = (s.images, shard // 2, s.dim // 2)
        scratch.update(p_out=((4, *piece), BF16), p_sib=((2, *piece), BF16))
        scratch.update(p_across=(piece, BF16), p_stage=(piece, BF16))
        scratch.update(small_out=((s.images, s.slot, 128), BF16))
        scratch.update(small_in=((s.images, s.slot, 128), BF16))
        recv.update(project=3, small=s.images, small_sum=4)
        sends += 3 + s.images - 1 + 3
    else:
        outputs.update(d_project=((s.dim, s.dim), BF16))
        outputs.update(small_out=((s.slot, s.dim), F32))
        outputs.update(head_out=((s.slot, 128), F32))
    return run_kernel(backward_kernel, s, inputs, outputs, scratch, recv, sends, 2, carried, True)


def write_call(s, grads, pieces, raw):
    shard = s.dim // s.images
    outputs = dict(
        patch_grad=((1, s.own, s.dim), F32),
        d_w_back=((4 * shard, s.dim), F32),
        d_w_in=((shard, 4 * s.hidden), F32),
        d_w_qkv=((shard, 3 * s.dim), F32),
        d_w_out=((shard, s.dim), F32),
        d_cls=((s.classes, shard), F32),
        d_gain_one=((1, shard), F32),
        d_gain_two=((1, shard), F32),
        d_head=((1, s.classes), F32),
    )
    inputs = dict(patch_rows=grads.patch_grad, project=pieces[PROJECT], small_sum=grads.small_sum)
    inputs.update(back0=pieces[0], back1=pieces[1], into0=pieces[2], into1=pieces[3])
    inputs.update(pair=pieces[JOINT], last=pieces[LAST], **raw)

    def kernel(*refs):
        k = types.SimpleNamespace(s=s, **dict(zip(list(inputs) + list(outputs), refs)))
        k.back, k.into = (k.back0, k.back1), (k.into0, k.into1)
        write_kernel(k)

    whole = pl.BlockSpec(memory_space=pltpu.VMEM)
    results = pl.pallas_call(
        kernel,
        out_shape=[jax.ShapeDtypeStruct(*v) for v in outputs.values()],
        in_specs=[whole] * len(inputs),
        out_specs=[whole] * len(outputs),
        compiler_params=pltpu.CompilerParams(vmem_limit_bytes=VMEM_BYTES),
        name=write_kernel.__name__,
    )(*inputs.values())
    return types.SimpleNamespace(**dict(zip(outputs, results)))


def sizes(patches, cls_emb, w_joint, w_back, head_gain):
    images, tiles = lax.axis_size(IMG), lax.axis_size(TILE)
    s = types.SimpleNamespace(images=images, tiles=tiles)
    s.dim = patches.shape[2]
    s.own = patches.shape[1]
    s.grid = s.own // WP
    s.wide_pixels = WP * UP
    s.classes = head_gain.shape[0]
    s.step = -(-s.classes // (8 * tiles)) * 8
    s.slot = -(-s.step // 16) * 16
    s.lanes = s.step * tiles
    s.rows = s.own + s.slot
    s.pack = -(-s.rows // 32) * 16
    s.head = s.dim // HEADS
    s.here = HEADS // tiles
    s.hidden = w_back.shape[0] * images // tiles
    shard = w_joint.shape[0]
    s.img_comm = images == PLANE * tiles and shard % 16 == 0 and shard <= 128
    return s


def shards(
    patches, labels, heights, cls_emb, gain_one, w_qkv, w_out, gain_two, w_in, w_back, head_gain
):
    s = sizes(patches, cls_emb, w_qkv, w_back, head_gain)
    t = lax.axis_index(TILE)
    shard = w_qkv.shape[0]
    wide = s.here * s.head

    part = w_back.shape[0] // s.tiles
    w_back = w_back.reshape(s.tiles, part, s.dim)
    cls_emb, gain_one, gain_two = cls_emb, gain_one[None], gain_two[None]
    inputs = dict(patches=patches, labels=labels, height=heights, gain_row=head_gain[None])
    common = {}
    if s.img_comm:
        inputs.update(cls_emb=cls_emb, gain_one=gain_one, gain_two=gain_two)
        inputs.update(w_qkv=w_qkv, wo=w_out, w_in=w_in, wb=w_back)
    else:

        def gather(value, axis=0):
            return lax.all_gather(value, IMG, axis=axis, tiled=True)

        def pick(value, axis):
            return lax.dynamic_index_in_dim(value, t, axis, keepdims=False)

        joint = pick(w_qkv.reshape(shard, 3, s.tiles, s.here, s.head), 2)
        joint = joint.transpose(0, 2, 1, 3).reshape(shard, 3 * wide)
        expand = pick(w_in.reshape(shard, s.images, s.tiles, part), 2).reshape(shard, s.hidden)
        reduce = pick(w_back, 0)
        small = jnp.concatenate([cls_emb, gain_one, gain_two], axis=0)
        small = jnp.pad(small, ((0, s.lanes - small.shape[0]), (0, 0)))
        common.update(
            w_joint=gather(joint)[None],
            w_project=gather(w_out)[None],
            w_expand=gather(expand)[None],
            w_reduce=gather(reduce)[None],
        )
        inputs.update(small_full=gather(small, 1), **common)
    arrays = forward_call(s, inputs)
    cells, halo = arrays.pop(CELLS), arrays.pop(HALO)
    masks, cell_sums = upsampled_loss(cells, labels, halo, heights, s.classes)
    carried = [n for n in CARRIED if n in arrays]
    grads = backward_call(s, dict(**arrays, **common, cell_sums=cell_sums), carried)
    grads = types.SimpleNamespace(**grads)
    count = PROJECT + 1 if s.img_comm else PROJECT
    pieces = [getattr(grads, GRAD_REFS[0] + str(n)) for n in range(count)]
    if s.img_comm:
        raw = dict(w_qkv=w_qkv, w_in=w_in, gain_one=gain_one, gain_two=gain_two)
        written = write_call(s, grads, pieces, raw)
        return (
            masks[None],
            written.patch_grad,
            written.d_cls,
            written.d_gain_one[0],
            written.d_w_qkv,
            written.d_w_out,
            written.d_gain_two[0],
            written.d_w_in,
            written.d_w_back,
            written.d_head[0],
        )

    def across(value):
        return lax.all_gather(value, TILE, axis=0, tiled=False)

    def total(value, axis=0):
        return lax.psum_scatter(value, IMG, scatter_dimension=axis, tiled=True)

    pieces = [across(total(v)) for v in pieces]
    back, into = [jnp.concatenate(pieces[n : n + 2], axis=2) for n in (BACK, INTO)]
    project = total(lax.psum(grads.d_project, TILE))
    small = across(total(grads.small_out, 1))
    head_rows = across(lax.psum(grads.head_out, IMG))
    joint = jnp.concatenate(pieces[JOINT:], axis=2)
    joint = joint.reshape(s.tiles, shard, s.here, 3, s.head).transpose(1, 3, 0, 2, 4)
    joint = joint.reshape(shard, -1).astype(F32)
    expand = into.reshape(s.tiles, shard, s.images, part).transpose(1, 2, 0, 3)
    expand = expand.reshape(shard, -1).astype(F32)
    cls_grad = small[:, : s.step, :shard].reshape(s.lanes, shard)[: s.classes]
    head_grad = jnp.sum(head_rows[:, s.step : s.step + 2, :128], axis=0).reshape(-1)[: s.classes]
    return (
        masks[None],
        grads.patch_grad,
        cls_grad,
        gain_sums(w_qkv, joint)[:, 0] / gain_one[0].astype(F32),
        joint,
        project.astype(F32),
        gain_sums(w_in, expand)[:, 0] / gain_two[0].astype(F32),
        expand,
        back.reshape(-1, s.dim).astype(F32),
        head_grad,
    )


def solution(mesh):
    in_specs = (
        P(IMG, TILE, None),
        P(IMG, TILE, None),
        P(IMG),
        P(None, IMG),
        P(IMG),
        P(IMG, None),
        P(IMG, None),
        P(IMG),
        P(IMG, None),
        P(IMG, None),
        P(),
    )
    out_specs = (
        P(IMG, None, TILE, None),
        P(IMG, TILE, None),
        P(None, IMG),
        P(IMG),
        P(IMG, None),
        P(IMG, None),
        P(IMG),
        P(IMG, None),
        P(IMG, None),
        P(),
    )
    return jax.shard_map(shards, mesh=mesh, in_specs=in_specs, out_specs=out_specs, check_vma=False)
```

```python
import collections
import functools
import types

import jax
import jax.numpy as jnp
import numpy as np
from jax import lax
from jax.experimental import pallas as pl
from jax.experimental.pallas import tpu as pltpu
from jax.sharding import PartitionSpec as P

IMG = "img"
TILE = "tile"
HEADS = 12
WP = 16
UP = 16
BAND = 32
BAND_CELLS = 4
GROUP = 8
EDGE = UP // 2
MESH = pl.DeviceIdType.MESH
LOGIT_UNIT = "logit_unit"
LOGIT_SCALE = "logit_scale"
HEAD_GAIN = "head_gain"
PATCH_UNIT = "patch_unit"
CLASS_UNIT = "class_unit"
FINAL = "final"
W_REDUCE = "w_reduce"
SLOPE = "slope"
W_EXPAND = "w_expand"
ACT = "act"
H_TWO = "h_two"
AFTER = "after"
GAINS = "gains"
W_PROJECT = "w_project"
Q = "q"
KEYS = "keys"
OUTS = "outs"
VALUES = "values"
MIXED_MAIN = "mixed_main"
MIXED_THIRD = "mixed_third"
H_ONE = "h_one"
W_JOINT = "w_joint"
TOKEN_ROWS = "token_rows"
F32 = jnp.float32
BF16 = jnp.bfloat16
PLANE = 2
BACK, INTO, JOINT, LAST, PROJECT = 0, 2, 4, 5, 6
VMEM_BYTES = 62 << 20


def product(left, right):
    return jnp.dot(left, right, preferred_element_type=F32)


def times_transposed(left, right):
    return lax.dot_general(left, right, (((1,), (1,)), ((), ())), preferred_element_type=F32)


def transposed_times(left, right):
    return lax.dot_general(left, right, (((0,), (0,)), ((), ())), preferred_element_type=F32)


def layer_norm_parts(value):
    centre = jnp.mean(value, axis=-1, keepdims=True)
    centred = value - centre
    spread = jnp.mean(centred * centred, axis=-1, keepdims=True)
    scale = lax.rsqrt(spread + 1e-05)
    return centred * scale, scale


def layer_norm_back(unit, scale, gain, upstream):
    weighted = upstream * gain
    mean = jnp.mean(weighted, axis=-1, keepdims=True)
    along = jnp.mean(weighted * unit, axis=-1, keepdims=True)
    return scale * (weighted - mean - unit * along)


def gelu_pair(x):
    root = np.float32(np.sqrt(2.0 / np.pi))
    square = x * x
    turned = jnp.tanh(root * x * (1.0 + np.float32(0.044715) * square))
    half = 0.5 * (1.0 + turned)
    slope = half + 0.5 * x * (1.0 - turned * turned) * root * (
        1.0 + np.float32(3 * 0.044715) * square
    )
    return x * half, slope


def lane_iota(rows, lanes):
    return lax.broadcasted_iota(jnp.int32, (rows, lanes), 1)


def row_iota(rows, lanes):
    return lax.broadcasted_iota(jnp.int32, (rows, lanes), 0)


def carry_copy(k, name, back=False):
    near, far = getattr(k, name), k.far[name]
    n = list(k.far).index(name)
    ends = (far, near) if back else (near, far)
    return pltpu.make_async_copy(*ends, k.carry_sem.at[n])


def keep(k, name):
    if name in k.far:
        carry_copy(k, name).start()


def kept(k):
    for name in k.far:
        carry_copy(k, name).wait()


def fetch_all(k):
    for name in k.far:
        carry_copy(k, name, True).start()


def have(k, *names):
    for name in names:
        if name in k.far:
            carry_copy(k, name, True).wait()


class Net:
    def __init__(self, k):
        self.k = k
        self.sent = []
        self.stage_sends = []

    def send(self, source, target, base, slot, device, when=None):
        k = self.k
        copy = pltpu.make_async_remote_copy(
            src_ref=source,
            dst_ref=target,
            send_sem=k.send_sem.at[len(self.sent)],
            recv_sem=k.recv_sem.at[base + slot],
            device_id=device,
            device_id_type=MESH,
        )
        self.sent.append((copy, when))
        if when is None:
            copy.start()
        else:
            pl.when(when)(copy.start)
        return len(self.sent) - 1

    def arrived(self, target, base, slot):
        k = self.k
        pltpu.make_async_remote_copy(
            src_ref=target,
            dst_ref=target,
            send_sem=k.send_sem.at[0],
            recv_sem=k.recv_sem.at[base + slot],
            device_id=k.sibling,
            device_id_type=MESH,
        ).wait_recv()

    def gone(self, number):
        if self.sent[number] is None:
            return
        copy, when = self.sent[number]
        self.sent[number] = None
        if when is None:
            copy.wait_send()
        else:
            pl.when(when)(copy.wait_send)

    def drain(self):
        for number in range(len(self.sent)):
            self.gone(number)


def place(k):
    k.i = lax.axis_index(IMG)
    k.t = lax.axis_index(TILE)
    k.y = k.i % PLANE
    k.z = k.i // PLANE
    k.planes = k.s.images // PLANE
    k.ts = k.t + 1 - 2 * (k.t % 2)
    k.tx = (k.t + 2) % 4
    k.td = (k.ts + 2) % 4
    k.sibling = (k.i, k.ts)
    k.across = (k.i, k.tx)
    k.diagonal = (k.i, k.td)
    k.mate = (k.i + 1 - 2 * k.y, k.t)


def line_peer(k, step):
    z = (k.z + step) % k.planes
    return z, (PLANE * z + k.y, k.t)


def enter(k, beside):
    barrier = pltpu.get_barrier_semaphore()
    peers = [k.sibling, k.across, k.diagonal]
    if k.s.img_comm:
        peers += [k.mate] + [line_peer(k, step)[1] for step in range(1, k.planes)]
    for peer in peers:
        pl.semaphore_signal(barrier, inc=1, device_id=peer, device_id_type=MESH)
    done = beside()
    pl.semaphore_wait(barrier, len(peers))
    return done


def spread_start(k, own, slots, name):
    for step in range(1, k.planes):
        k.net.send(own, slots.at[k.i], name, k.i, line_peer(k, step)[1])
    k.net.send(own, slots.at[k.i], name, k.i, k.mate)


def spread_pass(k, slots, name):
    for step in range(1, k.planes):
        z = (k.z + k.planes - step) % k.planes
        i = PLANE * z + k.y
        k.net.arrived(slots.at[i], name, i)
        k.net.send(slots.at[i], slots.at[i], name, i, k.mate)


def spread_end(k, slots, name):
    for z in range(k.planes):
        i = PLANE * z + 1 - k.y
        k.net.arrived(slots.at[i], name, i)


def line_start(k, own, slots, base, cut):
    send = k.net.send
    own, there = own.at[cut], slots.at[(k.i, *cut)]
    send(own, there, base, k.i, line_peer(k, 1)[1], k.z < k.planes - 1)
    send(own, there, base, k.i, line_peer(k, k.planes - 1)[1], k.z > 0)
    send(own, there, base, k.i, k.mate)


def line_end(k, slots, base, cut):
    for z in range(k.planes):
        i = PLANE * z + 1 - k.y
        k.net.arrived(slots.at[(i, *cut)], base, i)


def line_hop(k, slots, base, far, cut):
    send = k.net.send
    for sign in (-1, 1):
        here = k.z >= far if sign < 0 else k.z < k.planes - far
        more = k.z < k.planes - 1 if sign < 0 else k.z > 0
        i = PLANE * ((k.z + sign * far + k.planes) % k.planes) + k.y
        there = slots.at[(i, *cut)]

        @pl.when(here)
        def _(i=i, there=there):
            k.net.arrived(there, base, i)

        if far < k.planes - 1:
            peer = line_peer(k, 1 if sign < 0 else k.planes - 1)[1]
            send(there, there, base, i, peer, here & more)
        send(there, there, base, i, k.mate, here)


def project_cut(k, tile):
    rows, columns = k.s.dim // k.s.images // 2, k.s.dim // 2
    return (
        pl.ds(pl.multiple_of(rows * (tile // 2), 16), rows),
        pl.ds(pl.multiple_of(columns * (tile % 2), 128), columns),
    )


def project_part(k, tile):
    rows, columns = project_cut(k, tile)
    return k.w_project.at[:, rows, columns]


def slot_part(slots, slot, rows):
    return slots.at[slot] if rows is None else slots.at[slot, rows]


def share_start(k, slots, base, rows=None):
    own = slot_part(slots, k.t, rows)
    k.net.send(own, own, base, k.t, k.across)
    k.net.send(own, own, base, k.t, k.sibling)


def share_pass(k, slots, base, rows=None):
    part = slot_part(slots, k.tx, rows)
    k.net.arrived(part, base, k.tx)
    k.net.send(part, part, base, k.tx, k.sibling)


def halves(s):
    return [pl.ds(n * s.dim // 2, s.dim // 2) for n in range(2)]


def edge_cuts(s):
    first, second = halves(s)
    return [
        (pl.ds(0, s.rows), first),
        (pl.ds(s.own - WP, WP + s.slot), second),
        (pl.ds(0, WP), second),
        (pl.ds(WP, s.own - 2 * WP), second),
    ]


def row_cuts(s):
    return [(pl.ds(s.own, s.slot), pl.ds(0, s.dim)), (pl.ds(0, s.own), pl.ds(0, s.dim))]


def reduce_over_tile(k, base, part, cuts, before=None, ready=None):
    sends = k.net.stage_sends
    for number in sends:
        k.net.gone(number)
    sends.clear()

    def to_sibling(n, kind, slot):
        at = (kind, *cuts[n])
        k.stage[at] = part(slot, *cuts[n]).astype(BF16)
        sends.append(k.net.send(k.stage.at[at], k.from_sib.at[at], base, 3 * n + kind, k.sibling))

    def near(n):
        if before:
            before(k.t, n)
        k.own_part[cuts[n]] = part(k.t, *cuts[n])
        if before:
            before(k.ts, n)
        to_sibling(n, 0, k.ts)

    if before:
        for n in range(len(cuts)):
            near(n)
    for n in range(len(cuts)):
        if ready:
            ready(n)
        if before:
            before(k.tx, n)
            before(k.td, n)
        to_sibling(n, 1, k.td)
        total = part(k.tx, *cuts[n])
        k.across_part[cuts[n]] = total
        k.net.arrived(k.from_sib.at[(1, *cuts[n])], base, 3 * n + 1)
        total = k.across_part[cuts[n]] + k.from_sib[(1, *cuts[n])].astype(F32)
        k.stage[(2, *cuts[n])] = total.astype(BF16)
        ends = k.stage.at[(2, *cuts[n])], k.from_across.at[cuts[n]]
        sends.append(k.net.send(*ends, base, 3 * n + 2, k.across))
        if not before:
            near(n)


def reduced_wait(k, base, cuts, which):
    for n in which:
        k.net.arrived(k.from_sib.at[(0, *cuts[n])], base, 3 * n)
        k.net.arrived(k.from_across.at[cuts[n]], base, 3 * n + 2)


def reduced(k, rows):
    return k.own_part[rows, :] + k.from_sib[0, rows, :].astype(F32) + k.from_across[rows, :].astype(F32)


def pack_third(s, value):
    return jnp.concatenate([value[: s.pack], value[s.rows - s.pack :]], axis=1)


def third_rows(s, packed):
    rest = 2 * s.pack - s.rows
    return jnp.concatenate([packed[:, : s.head], packed[rest:, s.head :]], axis=0)


def key_bias(k, slot, height):
    s = k.s
    rows = row_iota(s.rows, s.head)
    cls = rows - s.own
    patch_ok = (rows < s.own) & (rows < (height - slot * s.grid) * WP)
    class_ok = (cls >= 0) & (cls < s.step) & (slot * s.step + cls < s.classes)
    off = jnp.where(patch_ok | class_ok, 0.0, -1e30)
    lane = lane_iota(s.rows, s.head)
    return jnp.where(lane == 0, off, jnp.where(lane < 4, 1.0, 0.0))


def class_rows(k, slot):
    s = k.s
    rows = k.cls_rows[pl.ds(pl.multiple_of(slot * s.step, 8), s.step), :]
    return jnp.concatenate([rows, jnp.zeros((s.slot - s.step, s.dim), F32)], axis=0)


def slot_rows(k, slot):
    return pl.ds(pl.multiple_of(slot * k.s.rows, 16), k.s.rows)


def block_scores(k, head, slot):
    return times_transposed(k.q[head, slot_rows(k, slot), :], k.keys[head])


def local_copy(k, source, target, number):
    return pltpu.make_async_copy(source, target, k.local_sem.at[number])


def pick_columns(k):
    s = k.s
    wide = s.here * s.head
    for n in range(4):

        @pl.when(k.t == n)
        def _(n=n):
            cut = [
                k.w_qkv[:, s.dim * m + wide * n + s.head * h :][:, : s.head]
                for h in range(s.here)
                for m in range(3)
            ]
            k.wq[...] = jnp.concatenate(cut, axis=1)


def pick_hidden(k):
    part = k.s.hidden // k.s.images
    for n in range(4):

        @pl.when(k.t == n)
        def _(n=n):
            cut = [k.w_in_near[:, part * (4 * i + n) :][:, :part] for i in range(k.s.images)]
            k.wi[...] = jnp.concatenate(cut, axis=1)


def forward_kernel(k):
    s = k.s
    place(k)
    net = k.net
    i, t = k.i, k.t
    shard = s.dim // s.images

    def prepare():
        head_gain = k.gain_row[...].astype(F32).reshape(1, s.classes)
        head_gain = jnp.concatenate([head_gain, jnp.zeros((1, s.lanes - s.classes), F32)], axis=1)
        k.head_gain[...] = jnp.broadcast_to(head_gain, (8, s.lanes))
        if s.img_comm:
            rows = [ref[...].astype(F32) for ref in (k.cls_emb, k.gain_one, k.gain_two)]
            rows += [jnp.zeros((s.lanes - s.classes - 2, shard), F32)]
            table = jnp.concatenate(rows, axis=0)
            table = jnp.concatenate([table, jnp.zeros((s.lanes, 128 - shard), F32)], axis=1)
            k.small[...] = table.astype(BF16)
            pick_columns(k)

    patches, labels = k.patches.at[0], k.labels.at[0]
    tokens_in = local_copy(k, patches, k.tokens.at[t], 1)
    tokens_in.start()
    if s.img_comm:
        w_in_copy = local_copy(k, k.w_in, k.w_in_near, 2)
        w_in_copy.start()
        w_back_copy = local_copy(k, k.wb.at[t], k.w_reduce.at[i], 3)
        w_back_copy.start()
    enter(k, prepare)
    keep(k, HEAD_GAIN)
    comm = s.img_comm
    wide = s.here * s.head
    first, second = halves(s)
    early = pl.ds(0, 3 * s.head * (s.here - 1))
    late = pl.ds(3 * s.head * (s.here - 1), 3 * s.head)
    joint = expand = reduce = (None, None)
    project = None
    if comm:
        at = k.at
        every = pl.ds(0, shard)
        joint = ((k.wq, k.w_joint, at.joint0, early), (k.wq, k.w_joint, at.joint1, late))
        expand = ((k.wi, k.w_expand, at.expand0, first), (k.wi, k.w_expand, at.expand1, second))
        back = k.wb.at[t]
        reduce = ((back, k.w_reduce, at.reduce0, first), (back, k.w_reduce, at.reduce1, second))
        joint, expand, reduce = [
            [(*item[:3], (every, item[3])) for item in pair] for pair in (joint, expand, reduce)
        ]
        project = (k.wo, k.w_project, at.w_project, project_cut(k, t))
        wo_copy = local_copy(k, k.wo.at[project[3]], k.w_project.at[(i, *project[3])], 0)
        wo_copy.start()

    def start(item):
        if comm:
            line_start(k, *item)

    def hop(item, far):
        if comm:
            line_hop(k, *item[1:3], far, item[3])

    def end(item):
        if comm:
            line_end(k, *item[1:])

    if comm:
        spread_start(k, k.small, k.smalls, k.at.small)
        k.smalls[i] = k.small[...]
        start(joint[0])
        start(joint[1])
        start(project)
    net.send(patches, k.tokens.at[t], k.at.tokens, t, k.across)
    net.send(patches, k.tokens.at[t], k.at.tokens, t, k.sibling)
    top, bottom, last = pl.ds(0, EDGE), pl.ds(EDGE, EDGE), pl.ds(s.grid * UP - EDGE, EDGE)
    net.send(labels.at[top], k.halo.at[bottom], k.at.halo, 1, (i, (t + 3) % 4))
    net.send(labels.at[last], k.halo.at[top], k.at.halo, 0, (i, (t + 1) % 4))
    if comm:
        k.w_joint[i] = k.wq[...]
        spread_pass(k, k.smalls, k.at.small)
        hop(joint[0], 1)
        hop(joint[1], 1)
        hop(project, 1)
        w_in_copy.wait()
        pick_hidden(k)
        k.w_expand[i] = k.wi[...]
        hop(joint[0], 2)
        hop(joint[1], 2)
        hop(project, 2)
        start(expand[0])
        spread_end(k, k.smalls, k.at.small)
        pieces = [k.smalls[n].astype(F32)[:, :shard] for n in range(s.images)]
        full = jnp.concatenate(pieces, axis=1)
    else:
        full = k.small_full[...].astype(F32)
    k.gains[0:2] = full[s.classes : s.classes + 2]
    k.cls_rows[...] = jnp.where(row_iota(s.lanes, s.dim) < s.classes, full, 0.0)
    gain_one, gain_two = k.gains[0:1], k.gains[1:2]
    keep(k, GAINS)

    def normed_tokens(slot):
        value = jnp.concatenate([k.tokens[slot].astype(F32), class_rows(k, slot)], axis=0)
        k.h_one[slot] = (layer_norm_parts(value)[0] * gain_one).astype(BF16)

    tokens_in.wait()
    k.token_rows[0 : s.own] = k.tokens[t].astype(F32)
    k.token_rows[s.own : s.rows] = class_rows(k, t)
    keep(k, TOKEN_ROWS)
    normed_tokens(t)
    if comm:
        hop(joint[0], 3)
        hop(joint[1], 3)
        hop(project, 3)
        start(expand[1])
    net.arrived(k.tokens.at[k.ts], k.at.tokens, k.ts)
    normed_tokens(k.ts)
    net.arrived(k.tokens.at[k.tx], k.at.tokens, k.tx)
    net.send(k.tokens.at[k.tx], k.tokens.at[k.tx], k.at.tokens, k.tx, k.sibling)
    normed_tokens(k.tx)
    hop(expand[0], 1)
    net.arrived(k.tokens.at[k.td], k.at.tokens, k.td)
    normed_tokens(k.td)
    keep(k, H_ONE)
    if comm:
        end(joint[0])
        end(joint[1])
        keep(k, W_JOINT)
        end(project)
        wo_copy.wait()
        part = project_part(k, t)
        net.send(part, part, at.w_shared, t, k.across)
        net.send(part, part, at.w_shared, t, k.sibling)

    lane = lane_iota(s.rows, s.head)
    one = jnp.where(lane == 0, 1.0, 0.0)
    ones = jnp.where(lane < 2, 1.0, 0.0)
    height = k.height[0]

    def joint_rows(slot):
        value = product(k.h_one[slot], k.w_joint[...].reshape(s.dim, s.here * 3 * s.head))
        bias = key_bias(k, slot, height)
        rows = slot_rows(k, slot)
        for h in range(s.here):
            cut = [
                value[:, (3 * h + n) * s.head : (3 * h + n + 1) * s.head] for n in range(3)
            ]
            for ref, part, extra in zip(
                (k.q, k.keys, k.values), (cut[0] * s.head**-0.5, cut[1], cut[2]), (one, bias, ones)
            ):
                ref[h, rows, :] = jnp.concatenate([part, extra], axis=1).astype(BF16)

    joint_rows(0)
    hop(expand[0], 2)
    joint_rows(1)
    start(reduce[0])
    joint_rows(2)
    hop(expand[0], 3)
    joint_rows(3)
    keep(k, Q)
    keep(k, KEYS)
    keep(k, VALUES)
    hop(expand[1], 1)

    def attend(slot):
        rows = slot_rows(k, slot)
        wide_lane = lane_iota(s.rows, 2 * s.head)
        parts = []
        for h in range(s.here):
            scores = block_scores(k, h, slot)
            largest = jnp.max(scores, axis=-1, keepdims=True)
            powers = jnp.exp(scores - largest).astype(BF16)
            out = product(powers, k.values[h])
            parts.append(out[:, : s.head] / out[:, s.head : s.head + 1])
            k.outs[h, rows, :] = jnp.where(wide_lane == s.head + 1, largest, out)
        k.mixed[slot] = jnp.concatenate(parts, axis=1).astype(BF16)
        k.third_out[slot] = pack_third(s, parts[2]).astype(BF16)

    for step, slot in enumerate((k.tx, k.td, k.ts, t), 1):
        attend(slot)
        if step < 4:
            main = k.mixed.at[slot, :, pl.ds(0, 2 * s.head)]
            net.send(main, k.mixed_main.at[t], k.at.mixed, t, (i, slot))
            net.send(k.third_out.at[slot], k.mixed_third.at[t], k.at.third, t, (i, slot))
        if step == 1:
            hop(expand[1], 2)
            start(reduce[1])
        if step == 2:
            hop(expand[1], 3)
            if comm:
                part = project_part(k, k.tx)
                net.arrived(part, at.w_shared, k.tx)
                net.send(part, part, at.w_shared, k.tx, k.sibling)
        if step == 3:
            hop(reduce[0], 1)
    keep(k, OUTS)
    k.mixed_main[t] = k.mixed[t, :, pl.ds(0, 2 * s.head)]
    k.mixed_third[t] = k.third_out[t]
    hop(reduce[0], 2)
    hop(reduce[0], 3)
    if comm:
        for slot in (k.ts, k.td):
            net.arrived(project_part(k, slot), at.w_shared, slot)
        keep(k, W_PROJECT)
    after = k.token_rows[...]
    w_project = k.w_project[...].reshape(s.dim, s.dim)
    for step in range(1, 4):
        slot = (t + step) % 4
        net.arrived(k.mixed_main.at[slot], k.at.mixed, slot)
        net.arrived(k.mixed_third.at[slot], k.at.third, slot)
    for n in range(4):
        rows = third_rows(s, k.mixed_third[n].astype(F32)).astype(BF16)
        mixed = jnp.concatenate([k.mixed_main[n], rows], axis=1)
        after = after + product(mixed, w_project[wide * n : wide * (n + 1)])
    keep(k, MIXED_MAIN)
    keep(k, MIXED_THIRD)
    k.after[...] = after
    keep(k, AFTER)
    k.h_two[t] = (layer_norm_parts(after)[0] * gain_two).astype(BF16)
    share_start(k, k.h_two, k.at.h_two)
    hop(reduce[1], 1)
    if comm:
        end(expand[0])
        end(expand[1])
        keep(k, W_EXPAND)

    def hidden(slot):
        pre = product(k.h_two[slot], k.w_expand[...].reshape(s.dim, s.hidden))
        act, slope = gelu_pair(pre)
        k.act[slot] = act.astype(BF16)
        k.slope[slot] = slope.astype(BF16)

    hidden(t)
    hop(reduce[1], 2)
    net.arrived(k.h_two.at[k.ts], k.at.h_two, k.ts)
    hidden(k.ts)
    hop(reduce[1], 3)
    share_pass(k, k.h_two, k.at.h_two)
    hidden(k.tx)
    net.arrived(k.h_two.at[k.td], k.at.h_two, k.td)
    hidden(k.td)
    keep(k, H_TWO)
    keep(k, ACT)
    keep(k, SLOPE)

    def contract(slot, rows, columns):
        return product(k.act[slot, rows], k.w_reduce[:, :, columns].reshape(s.hidden, s.dim // 2))

    if comm:
        w_back_copy.wait()
    cuts = edge_cuts(s)

    def ready(n):
        if comm and n < 2:
            end(reduce[n])

    reduce_over_tile(k, k.at.feed, contract, cuts, ready=ready)
    if comm:
        keep(k, W_REDUCE)

    def finish(rows):
        final = k.after[rows, :] + reduced(k, rows)
        k.final[rows, :] = final
        square = jnp.sum(final * final, axis=-1, keepdims=True)
        return (final * lax.rsqrt(square + 1e-06)).astype(BF16)

    reduced_wait(k, k.at.feed, cuts, (0, 1, 2))
    last_rows = finish(cuts[1][0])
    k.cls_units[t] = last_rows[WP:]
    k.patch_unit[s.own : WP + s.own] = last_rows[:WP]
    k.patch_unit[WP : 2 * WP] = finish(cuts[2][0])
    above, below = pl.ds(0, WP), pl.ds(WP + s.own, WP)
    for slot in (k.tx, k.td, k.ts):
        net.send(k.cls_units.at[t], k.cls_units.at[t], k.at.units, t, (i, slot))
    net.send(k.patch_unit.at[pl.ds(WP, WP)], k.patch_unit.at[below], k.at.rim, 1, (i, (t + 3) % 4))
    net.send(k.patch_unit.at[pl.ds(s.own, WP)], k.patch_unit.at[above], k.at.rim, 0, (i, (t + 1) % 4))
    reduced_wait(k, k.at.feed, cuts, (3,))
    k.patch_unit[2 * WP : s.own] = finish(cuts[3][0])
    keep(k, FINAL)
    for slot in (k.ts, k.tx, k.td):
        net.arrived(k.cls_units.at[slot], k.at.units, slot)
    net.arrived(k.patch_unit.at[above], k.at.rim, 0)
    net.arrived(k.patch_unit.at[below], k.at.rim, 1)
    units = jnp.concatenate([k.cls_units[n].astype(F32)[: s.step] for n in range(4)], axis=0)
    units = jnp.where(row_iota(s.lanes, s.dim) < s.classes, units, 0.0).astype(BF16)
    k.class_unit[...] = units
    keep(k, CLASS_UNIT)
    keep(k, PATCH_UNIT)
    logits = times_transposed(k.patch_unit[...], units)
    unit_logits, scale = class_norm_parts(k, logits)
    k.logit_unit[...] = unit_logits[WP : WP + s.own]
    k.logit_scale[...] = jnp.broadcast_to(scale[WP : WP + s.own], (s.own, 128))
    keep(k, LOGIT_UNIT)
    keep(k, LOGIT_SCALE)
    normed = (unit_logits * k.head_gain[0:1]).astype(BF16)
    k.cells[WP : WP + s.own] = normed[WP : WP + s.own]
    k.cells[:WP] = jnp.where(t == 0, normed[WP : 2 * WP], normed[:WP])
    k.cells[WP + s.own :] = jnp.where(t == 3, normed[s.own : WP + s.own], normed[WP + s.own :])
    net.arrived(k.halo.at[pl.ds(0, EDGE)], k.at.halo, 0)
    net.arrived(k.halo.at[pl.ds(EDGE, EDGE)], k.at.halo, 1)
    kept(k)
    net.drain()


def class_norm_parts(k, value):
    s = k.s
    real = lane_iota(value.shape[0], s.lanes) < s.classes
    centre = jnp.sum(value, axis=-1, keepdims=True) / s.classes
    centred = jnp.where(real, value - centre, 0.0)
    spread = jnp.sum(centred * centred, axis=-1, keepdims=True) / s.classes
    scale = lax.rsqrt(spread + 1e-05)
    return centred * scale, scale


def sum_start(k, name):
    g = k.grads[name]
    k.net.send(g.blocks.at[1 - k.y], g.from_mate, g.at_mate, 0, k.mate)


def sum_pass(k, name):
    g = k.grads[name]
    k.net.arrived(g.from_mate, g.at_mate, 0)
    for step in range(k.planes):
        z = (k.z + step) % k.planes
        both = g.blocks[k.y, z].astype(F32) + g.from_mate[z].astype(F32)
        g.blocks[k.y, z] = both.astype(BF16)
        if step:
            k.net.send(g.blocks.at[k.y, z], g.from_line.at[k.z], g.at_line, k.z, line_peer(k, step)[1])


def sum_end(k, name):
    g = k.grads[name]
    total = g.blocks[k.y, k.z].astype(F32)
    for step in range(1, k.planes):
        z = (k.z + step) % k.planes
        k.net.arrived(g.from_line.at[z], g.at_line, z)
        total = total + g.from_line[z].astype(F32)
    g.out[k.t] = total.astype(BF16)
    if name != LAST:
        share_start(k, g.out, g.at_out)
        return
    for slot in (k.tx, k.td, k.ts):
        k.net.send(g.out.at[k.t], g.out.at[k.t], g.at_out, k.t, (k.i, slot))


def sum_share(k, name):
    g = k.grads[name]
    share_pass(k, g.out, g.at_out)


def sum_close(k, name):
    g = k.grads[name]
    if name == LAST:
        k.net.arrived(g.out.at[k.tx], g.at_out, k.tx)
    k.net.arrived(g.out.at[k.ts], g.at_out, k.ts)
    k.net.arrived(g.out.at[k.td], g.at_out, k.td)


def put_blocks(k, name, value):
    g = k.grads[name]
    if not k.s.img_comm:
        g.out[...] = value.astype(BF16)
        return
    rows = value.shape[0] // k.s.images
    for i in range(k.s.images):
        g.blocks[i % PLANE, i // PLANE] = value[rows * i : rows * (i + 1)].astype(BF16)


def head_powers(k, h):
    s = k.s
    out = k.outs[h]
    total = out[:, s.head + 1 : s.head + 2] + jnp.log(out[:, s.head : s.head + 1])
    first = total.astype(BF16).astype(F32)
    second = (total - first).astype(BF16).astype(F32)
    lane = lane_iota(4 * s.rows, 2 * s.head) - s.head
    value = jnp.where(lane == 1, -first, k.q[h].astype(F32))
    value = jnp.where(lane == 2, -second, value)
    k.q_back[h] = jnp.where(lane == 3, first + second - total, value).astype(BF16)

    def block(slot, carry):
        rows = slot_rows(k, slot)
        scores = times_transposed(k.keys[h, rows, :], k.q_back[h])
        k.powers[h, rows, :] = jnp.exp(scores).astype(BF16)
        return carry

    lax.fori_loop(0, 4, block, 0, unroll=True)


def head_back(k):
    s = k.s
    top = jnp.where(k.t == 0, k.cell_sums[:WP], 0.0)
    bottom = jnp.where(k.t == 3, k.cell_sums[WP + s.own :], 0.0)
    own = k.cell_sums[WP : WP + s.own]
    own = jnp.concatenate(
        [own[:WP] + top, own[WP : s.own - WP], own[s.own - WP :] + bottom], axis=0
    )
    upstream = own.astype(BF16).astype(F32)
    have(k, LOGIT_UNIT, LOGIT_SCALE, HEAD_GAIN, PATCH_UNIT, CLASS_UNIT, FINAL)
    unit, scale = k.logit_unit[...], k.logit_scale[:, :1]
    weighted = upstream * k.head_gain[0:1]
    mean = jnp.sum(weighted, axis=-1, keepdims=True) / s.classes
    along = jnp.sum(weighted * unit, axis=-1, keepdims=True) / s.classes
    head_row = jnp.sum(upstream * unit, axis=0, keepdims=True)
    d_logits = scale * (weighted - mean - unit * along)
    d_logits = jnp.where(lane_iota(s.own, s.lanes) < s.classes, d_logits, 0.0).astype(BF16)
    d_class = transposed_times(d_logits, k.patch_unit[WP : WP + s.own])
    for n in range(4):
        k.class_out[n] = jnp.concatenate(
            [d_class[s.step * n : s.step * (n + 1)], jnp.zeros((s.slot - s.step, s.dim), F32)], axis=0
        ).astype(BF16)
    return d_logits, head_row


def backward_kernel(k):
    s = k.s
    place(k)
    fetch_all(k)
    d_logits, head_row = enter(k, lambda: head_back(k))
    net = k.net
    i, t = k.i, k.t
    comm = s.img_comm
    split = s.own // 2
    first_part, patch_part = pl.ds(0, split), pl.ds(split, s.own - split)
    class_part = pl.ds(s.own, s.slot)

    for slot in (k.ts, k.tx, k.td):
        net.send(k.class_out.at[slot], k.class_in.at[t], k.at.class_, t, (i, slot))
    final = k.final[...]
    c = lax.rsqrt(jnp.sum(final * final, axis=-1, keepdims=True) + 1e-06)
    u = final * c

    def unit_back(rows, du):
        return c[rows] * (du - u[rows] * jnp.sum(u[rows] * du, axis=-1, keepdims=True))

    d_patch = unit_back(slice(0, s.own), product(d_logits, k.class_unit[...]))
    k.d_rows[: s.own] = d_patch
    k.d_branch[t, : s.own] = d_patch.astype(BF16)
    share_start(k, k.d_branch, k.at.d_first, first_part)
    share_start(k, k.d_branch, k.at.d_branch, patch_part)
    d_class_unit = k.class_out[t].astype(F32)
    for slot in (k.ts, k.tx, k.td):
        net.arrived(k.class_in.at[slot], k.at.class_, slot)
        d_class_unit = d_class_unit + k.class_in[slot].astype(F32)
    d_class = unit_back(slice(s.own, s.rows), d_class_unit)
    k.d_rows[s.own :] = d_class
    k.d_branch[t, s.own :] = d_class.astype(BF16)
    share_start(k, k.d_branch, k.at.d_class, class_part)

    have(k, W_REDUCE, SLOPE, W_EXPAND)

    every = pl.ds(0, s.dim)
    cuts = [(first_part, every), (pl.ds(split, s.rows - split), every)]

    def contract_back(slot, n):
        rows = cuts[n][0]
        d_act = times_transposed(k.d_branch[slot, rows], k.w_reduce[...].reshape(s.hidden, s.dim))
        k.d_pre[slot, rows] = (d_act * k.slope[slot, rows].astype(F32)).astype(BF16)

    def expand_back(slot, rows, columns):
        return times_transposed(k.d_pre[slot, rows], k.w_expand[...].reshape(s.dim, s.hidden))

    def before(slot, n):
        parts = ((first_part, k.at.d_first),)
        if n:
            parts = ((patch_part, k.at.d_branch), (class_part, k.at.d_class))
        if slot is k.tx and n == 0:
            have(k, Q, KEYS, OUTS)
            head_powers(k, 0)
        if slot is k.tx and n == 1:
            head_powers(k, 1)
        for rows, base in parts:
            if slot is k.tx:
                share_pass(k, k.d_branch, base, rows)
            elif slot is not t:
                net.arrived(k.d_branch.at[slot, rows], base, slot)
        contract_back(slot, n)

    reduce_over_tile(k, k.at.feed, expand_back, cuts, before)
    tall = 4 * s.rows
    have(k, ACT, H_TWO)
    for n, columns in enumerate(halves(s)):
        right = k.d_branch[:, :, columns].reshape(tall, s.dim // 2)
        put_blocks(k, BACK + n, transposed_times(k.act[...].reshape(tall, s.hidden), right))
        if comm:
            sum_start(k, BACK + n)
    for n, columns in enumerate(halves(s)):
        right = k.d_pre[:, :, columns].reshape(tall, s.hidden // 2)
        put_blocks(k, INTO + n, transposed_times(k.h_two[...].reshape(tall, s.dim), right))
        if comm:
            sum_start(k, INTO + n)
    head_powers(k, 2)

    have(k, AFTER, GAINS, W_PROJECT, VALUES, MIXED_MAIN, MIXED_THIRD, H_ONE, W_JOINT, TOKEN_ROWS)
    unit, scale = layer_norm_parts(k.after[...])
    reduced_wait(k, k.at.feed, cuts, (0, 1))
    part = layer_norm_back(unit, scale, k.gains[1:2], reduced(k, pl.ds(0, s.rows)))
    d_after = k.d_rows[...] + part
    k.d_rows[...] = d_after
    d_attn = d_after.astype(BF16)
    wide = s.here * s.head
    for slot in (k.tx, k.td, k.ts, t):
        if comm:
            rows = k.w_project[pl.ds(PLANE * slot, PLANE)].reshape(wide, s.dim)
        else:
            rows = k.w_project[0, pl.ds(pl.multiple_of(slot * wide, 16), wide), :]
        value = times_transposed(d_attn, rows)
        k.main_out[slot] = value[:, : 2 * s.head].astype(BF16)
        k.third_out[slot] = pack_third(s, value[:, 2 * s.head :]).astype(BF16)
        if slot is not t:
            net.send(k.main_out.at[slot], k.main_in.at[t], k.at.d_mixed, t, (i, slot))
    for slot in (k.tx, k.td, k.ts):
        net.send(k.third_out.at[slot], k.third_in.at[t], k.at.third, t, (i, slot))
    k.main_in[t] = k.main_out[t]
    k.third_in[t] = k.third_out[t]
    project_start(k, d_attn)
    if comm:
        sum_pass(k, BACK)
        project_across(k)
        sum_pass(k, BACK + 1)

    for slot in (k.ts, k.tx, k.td):
        net.arrived(k.main_in.at[slot], k.at.d_mixed, slot)

    for h in range(s.here):
        if comm and h == 2:
            sum_pass(k, INTO + 1)
        out = k.outs[h]
        if h < 2:
            d_mixed = k.main_in[...].reshape(tall, 2 * s.head)[:, s.head * h :][:, : s.head].astype(F32)
        else:
            for slot in (k.ts, k.tx, k.td):
                net.arrived(k.third_in.at[slot], k.at.third, slot)
            thirds = [third_rows(s, k.third_in[n].astype(F32)) for n in range(4)]
            d_mixed = jnp.concatenate(thirds, axis=0)
        along = jnp.sum(d_mixed * out[:, : s.head], axis=-1, keepdims=True)
        along = along / out[:, s.head : s.head + 1]
        high = along.astype(BF16).astype(F32)
        lane = lane_iota(tall, s.head)
        tail = jnp.where(lane == 0, -high, jnp.where(lane == 1, high - along, 0.0))
        k.d_out[...] = jnp.concatenate([d_mixed, tail], axis=1).astype(BF16)

        def block(slot, carry, h=h):
            rows = slot_rows(k, slot)
            powers = k.powers[h, rows, :]
            slopes = times_transposed(k.values[h, rows, :], k.d_out[...])
            d_scores = (powers.astype(F32) * slopes).astype(BF16)
            k.d_scores[rows, :] = d_scores
            d_k = product(d_scores, k.q_back[h])
            d_v = product(powers, k.d_out[...])
            both = jnp.concatenate([d_k[:, : s.head], d_v[:, : s.head]], axis=1)
            k.d_pair[rows, :] = both
            return carry

        lax.fori_loop(0, 4, block, 0)
        if comm and h == 0:
            project_end(k)
            sum_pass(k, INTO)
        if comm and h == 1:
            sum_end(k, BACK)
        if comm and h == 2:
            sum_share(k, BACK)
            sum_share(k, BACK + 1)
            sum_end(k, INTO)
            sum_pass(k, PROJECT)
        d_q = transposed_times(k.keys[h][:, : s.head], k.d_scores[...]).T * s.head**-0.5
        k.d_joint[h] = jnp.concatenate([d_q, k.d_pair[...]], axis=1).astype(BF16)
        if h == s.here - 2:
            pair = jnp.concatenate([k.d_joint[n] for n in range(h + 1)], axis=1)
            put_blocks(k, JOINT, transposed_times(k.h_one[...].reshape(tall, s.dim), pair))
        if h == s.here - 1:
            put_blocks(k, LAST, transposed_times(k.h_one[...].reshape(tall, s.dim), k.d_joint[h]))
        if comm and h >= s.here - 2:
            sum_start(k, JOINT if h == s.here - 2 else LAST)
        if comm and h == 1:
            sum_end(k, BACK + 1)

    w_joint = k.w_joint[...].reshape(s.dim, 3 * wide)

    def joint_back(slot, rows, columns):
        rows = pl.ds(pl.multiple_of(slot * s.rows + rows.start, 16), rows.size)
        left = jnp.concatenate([k.d_joint[h, rows, :] for h in range(s.here)], axis=1)
        return times_transposed(left, w_joint)

    cuts = row_cuts(s)
    reduce_over_tile(k, k.at.joint, joint_back, cuts)
    unit, scale = layer_norm_parts(k.token_rows[...])
    if comm:
        sum_pass(k, JOINT)
        sum_share(k, INTO)
        sum_end(k, INTO + 1)

    def norm_back(rows, upstream):
        return k.d_rows[rows] + layer_norm_back(unit[rows], scale[rows], k.gains[0:1], upstream)

    own_rows, cls_rows = slice(0, s.own), slice(s.own, s.rows)
    reduced_wait(k, k.at.joint, cuts, (0,))
    table = norm_back(cls_rows, reduced(k, cuts[0][0]))
    table = jnp.where(row_iota(s.slot, s.dim) < s.step, table, 0.0)
    rows = row_iota(s.slot, 128)
    head_rows = jnp.where(rows == s.step, head_row[:, :128], 0.0)
    rest = jnp.concatenate([head_row[:, 128:], jnp.zeros((1, 256 - s.lanes), F32)], axis=1)
    head_rows = jnp.where(rows == s.step + 1, rest, head_rows)
    if comm:
        small_start(k, table, head_rows)
        sum_pass(k, LAST)
        sum_end(k, PROJECT)
        small_end(k)
        sum_share(k, INTO + 1)
        sum_end(k, JOINT)
        sum_share(k, PROJECT)
    reduced_wait(k, k.at.joint, cuts, (1,))
    k.patch_grad[0] = norm_back(own_rows, reduced(k, cuts[1][0]))
    if not comm:
        k.small_out[...] = table
        k.head_out[...] = head_rows
        net.drain()
        return
    sum_end(k, LAST)
    sum_share(k, JOINT)
    for name in range(len(k.grads)):
        sum_close(k, name)
    for slot in (k.ts, k.tx, k.td):
        net.arrived(k.small_sum.at[slot], k.at.small_sum, slot)
    net.drain()


def project_start(k, d_attn):
    s = k.s
    shard = s.dim // s.images
    rows, columns = shard // 2, s.dim // 2
    for m in range(4):
        third = third_rows(s, k.mixed_third[m].astype(F32)).astype(BF16)
        mixed = jnp.concatenate([k.mixed_main[m], third], axis=1)
        value = transposed_times(mixed, d_attn).astype(BF16)
        if not s.img_comm:
            wide = s.here * s.head
            k.d_project[wide * m : wide * (m + 1)] = value
            continue
        for n in range(4):
            for y in range(PLANE):
                first = shard * y + rows * (n // 2)
                cut = value[first : first + rows, columns * (n % 2) :][:, :columns]
                k.p_out[n, PLANE * m + y] = cut
    if s.img_comm:
        k.net.send(k.p_out.at[k.td], k.p_sib.at[1], k.at.project, 1, k.sibling)
        k.net.send(k.p_out.at[k.ts], k.p_sib.at[0], k.at.project, 0, k.sibling)


def project_across(k):
    k.net.arrived(k.p_sib.at[1], k.at.project, 1)
    k.p_stage[...] = (k.p_out[k.tx].astype(F32) + k.p_sib[1].astype(F32)).astype(BF16)
    k.net.send(k.p_stage, k.p_across, k.at.project, 2, k.across)


def project_end(k):
    blocks = k.grads[PROJECT].blocks
    k.net.arrived(k.p_sib.at[0], k.at.project, 0)
    k.net.arrived(k.p_across, k.at.project, 2)
    total = k.p_out[k.t].astype(F32) + k.p_sib[0].astype(F32) + k.p_across[...].astype(F32)
    for i in range(k.s.images):
        blocks[i % PLANE, i // PLANE] = total[i].astype(BF16)
    sum_start(k, PROJECT)


def small_start(k, table, head_rows):
    s = k.s
    shard = s.dim // s.images
    pad = jnp.zeros((s.slot, 128 - shard), F32)
    for n in range(s.images):
        cut = jnp.concatenate([table[:, shard * n : shard * (n + 1)], pad], axis=1)
        k.small_out[n] = (cut + head_rows).astype(BF16)
    for step in range(1, s.images):
        n = (k.i + step) % s.images
        k.net.send(k.small_out.at[n], k.small_in.at[k.i], k.at.small, k.i, (n, k.t))


def small_end(k):
    s = k.s
    total = k.small_out[k.i].astype(F32)
    for step in range(1, s.images):
        n = (k.i + step) % s.images
        k.net.arrived(k.small_in.at[n], k.at.small, n)
        total = total + k.small_in[n].astype(F32)
    k.small_sum[k.t] = total
    for slot in (k.ts, k.tx, k.td):
        k.net.send(k.small_sum.at[k.t], k.small_sum.at[k.t], k.at.small_sum, k.t, (k.i, slot))


def gain_sums(weight, grad):
    return jnp.sum(weight.astype(F32) * grad, axis=1, keepdims=True)


def write_kernel(k):
    s = k.s
    shard = s.dim // s.images
    k.patch_grad[...] = k.patch_rows[...]
    half = s.dim // 2
    for n in range(2):
        k.d_w_back[:, half * n : half * (n + 1)] = k.back[n][...].astype(F32).reshape(4 * shard, half)
    part = s.hidden // s.images
    cut = [jnp.concatenate([ref[n].astype(F32) for ref in k.into], axis=1) for n in range(4)]
    cut = [cut[n][:, part * i : part * (i + 1)] for i in range(s.images) for n in range(4)]
    k.d_w_in[...] = jnp.concatenate(cut, axis=1)
    both = [[k.pair[n].astype(F32), k.last[n].astype(F32)] for n in range(4)]
    split = s.here - 1
    for m in range(3):
        cut = [
            both[n][h // split][:, s.head * (3 * (h % split) + m) :][:, : s.head]
            for n in range(4)
            for h in range(s.here)
        ]
        k.d_w_qkv[:, s.dim * m : s.dim * (m + 1)] = jnp.concatenate(cut, axis=1)
    for n in range(4):
        rows, columns = shard // 2 * (n // 2), half * (n % 2)
        k.d_w_out[rows : rows + shard // 2, columns : columns + half] = k.project[n].astype(F32)
    rows = jnp.concatenate([k.small_sum[n][: s.step] for n in range(4)], axis=0)
    k.d_cls[...] = rows[: s.classes, :shard]
    rest = k.small_sum[0] + k.small_sum[1] + k.small_sum[2] + k.small_sum[3]
    one = gain_sums(k.w_qkv[...], k.d_w_qkv[...])
    two = gain_sums(k.w_in[...], k.d_w_in[...])
    both = jnp.concatenate([one, two, jnp.zeros((shard, 126), F32)], axis=1).T
    k.d_gain_one[...] = both[0:1] / k.gain_one[...].astype(F32)
    k.d_gain_two[...] = both[1:2] / k.gain_two[...].astype(F32)
    head = jnp.concatenate([rest[s.step : s.step + 1], rest[s.step + 1 : s.step + 2]], axis=1)
    k.d_head[...] = head[:, : s.classes]


def tent(pixels, cells, first):
    place = (np.arange(pixels) + 0.5) / UP - 0.5 - first
    return np.maximum(0.0, 1.0 - np.abs(place[:, None] - np.arange(cells)[None, :]))


def band_tables():
    edge = tent(2 * UP, 2, 0)[EDGE : 3 * EDGE]
    edge = np.concatenate([edge[:EDGE], np.zeros((EDGE, 2)), np.zeros((EDGE, 2)), edge[EDGE:]], axis=0)
    edge = edge.reshape(2, 2 * EDGE, 2).transpose(1, 0, 2).reshape(2 * EDGE, BAND_CELLS)
    across = (np.clip((np.arange(WP * UP) + 0.5) / UP - 0.5, 0, WP - 1))[None, :]
    across = np.maximum(0.0, 1.0 - np.abs(across - np.arange(WP)[:, None]))
    down = tent(BAND, BAND_CELLS, -1)
    tables = [across]
    for table in (down, edge):
        rows = table.shape[0]
        up = np.zeros((GROUP, rows, 2, BAND_CELLS, GROUP), np.float32)
        back = np.zeros((BAND_CELLS, GROUP, GROUP, rows), np.float32)
        for c in range(GROUP):
            up[c, :, :, :, c] = table[:, None, :]
            back[:, c, c, :] = table.T
        tables.append(up.reshape(GROUP * rows, 2 * BAND_CELLS * GROUP))
        tables.append(back.reshape(BAND_CELLS * GROUP, GROUP * rows))
    return [jnp.asarray(t, BF16) for t in tables]


def two_parts(value):
    high = value.astype(BF16)
    return high, (value - high.astype(F32)).astype(BF16)


def upsample_kernel(
    classes, bands, height_ref, cell_ref, label_ref, halo_ref, across_ref, up_ref, back_ref,
    edge_up_ref, edge_back_ref, mask_ref, sum_ref, wide, wide_grad, powers,
):
    band = pl.program_id(0)
    groups = -(-classes // GROUP)
    tail = classes - GROUP * (groups - 1)
    cell_rows = cell_ref.shape[0] // WP
    pixels = label_ref.shape[2]
    tile = lax.axis_index(TILE)
    limit = (height_ref[0] - tile * (bands * BAND // UP)) * UP
    share = 1.0 / (UP * UP)
    counts = [GROUP] * (groups - 1) + [tail]

    @pl.when(band == 0)
    def _():
        for r in range(cell_rows):
            wide[r] = lax.dot_general(
                cell_ref[WP * r : WP * (r + 1), :], across_ref[...], (((0,), (0,)), ((), ())),
                preferred_element_type=F32,
            )
        wide_grad[...] = jnp.zeros_like(wide_grad)

    def pixel_rows(rows, label, first, second, up, back, masked):
        def forward(g, total, count):
            at = pl.ds(GROUP * g, GROUP)
            part = jnp.concatenate([wide[pl.ds(r, 2), at, :] for r in (first, second)], axis=0)
            both = jnp.concatenate(two_parts(part.reshape(BAND_CELLS * GROUP, pixels)), axis=0)
            upsampled = product(up[: count * rows, :], both).reshape(count, rows, pixels)
            if masked:
                mask_ref[pl.ds(GROUP * g, count)] = upsampled.astype(BF16)
            power = jnp.exp(upsampled)
            powers[pl.ds(GROUP * g, count), :rows] = power
            return total + jnp.sum(power, axis=0)

        total = jnp.zeros((rows, pixels), F32)
        for g, count in enumerate(counts):
            total = forward(g, total, count)
        inverse = jnp.where(label >= 0, share, 0.0) / total
        for g, count in enumerate(counts):
            parts = []
            for c in range(count):
                target = jnp.where(label == GROUP * g + c, share, 0.0)
                parts.append((powers[GROUP * g + c, :rows] * inverse - target).astype(BF16))
            summed = product(back[:, : count * rows], jnp.concatenate(parts, axis=0))
            summed = summed.reshape(BAND_CELLS, GROUP, pixels)
            at = pl.ds(GROUP * g, GROUP)
            wide_grad[pl.ds(first, 2), at, :] += summed[:2]
            wide_grad[pl.ds(second, 2), at, :] += summed[2:]

    @pl.when(band < bands)
    def _():
        rows = lax.broadcasted_iota(jnp.int32, (BAND, pixels), 0) + BAND * band
        label = jnp.where(rows < limit, label_ref[0], -1)
        first = BAND // UP * band
        pixel_rows(BAND, label, first, first + 2, up_ref, back_ref, True)

    @pl.when(band == bands)
    def _():
        rows = lax.broadcasted_iota(jnp.int32, (2 * EDGE, pixels), 0)
        below = rows >= EDGE
        rows = rows - EDGE + jnp.where(below, bands * BAND, 0)
        label = jnp.where((rows < limit) & (below | (tile > 0)), halo_ref[...], -1)
        pixel_rows(2 * EDGE, label, 0, cell_rows - 2, edge_up_ref, edge_back_ref, False)
        for r in range(cell_rows):
            high, low = two_parts(wide_grad[r])
            sum_ref[WP * r : WP * (r + 1), :] = times_transposed(
                across_ref[...], high
            ) + times_transposed(across_ref[...], low)


def upsampled_loss(cells, labels, halo, heights, classes):
    rows, lanes = cells.shape[0] // WP, cells.shape[1]
    tile_pixels, wide_pixels = labels.shape[1:]
    tables = band_tables()
    bands = tile_pixels // BAND

    def whole(shape):
        return pl.BlockSpec(shape, lambda i: (0,) * len(shape))

    return pl.pallas_call(
        functools.partial(upsample_kernel, classes, bands),
        grid=(bands + 1,),
        out_shape=(
            jax.ShapeDtypeStruct((classes, tile_pixels, wide_pixels), BF16),
            jax.ShapeDtypeStruct(cells.shape, F32),
        ),
        in_specs=[
            pl.BlockSpec(memory_space=pltpu.SMEM),
            whole(cells.shape),
            pl.BlockSpec((1, BAND, wide_pixels), lambda i: (0, jnp.minimum(i, bands - 1), 0)),
            whole(halo.shape),
        ]
        + [whole(t.shape) for t in tables],
        out_specs=(
            pl.BlockSpec((classes, BAND, wide_pixels), lambda i: (0, jnp.minimum(i, bands - 1), 0)),
            whole(cells.shape),
        ),
        scratch_shapes=[
            pltpu.VMEM((rows, lanes, wide_pixels), F32),
            pltpu.VMEM((rows, lanes, wide_pixels), F32),
            pltpu.VMEM((lanes, BAND, wide_pixels), F32),
        ],
        compiler_params=pltpu.CompilerParams(vmem_limit_bytes=56 << 20),
        name=upsample_kernel.__name__,
    )(heights, cells, labels, halo, *tables)


CELLS = "cells"
HALO = "halo"
FAR_INPUTS = ("patches", "labels", "wo", "w_in", "wb")
CARRIED = (
    LOGIT_UNIT,
    LOGIT_SCALE,
    HEAD_GAIN,
    PATCH_UNIT,
    CLASS_UNIT,
    FINAL,
    W_REDUCE,
    SLOPE,
    W_EXPAND,
    ACT,
    H_TWO,
    AFTER,
    GAINS,
    W_PROJECT,
    Q,
    KEYS,
    OUTS,
    VALUES,
    MIXED_MAIN,
    MIXED_THIRD,
    H_ONE,
    W_JOINT,
    TOKEN_ROWS,
)
GRAD_REFS = ("out", "blocks", "from_mate", "from_line")
GRAD_PLACES = ("at_mate", "at_line", "at_out")
Grad = collections.namedtuple("Grad", GRAD_REFS + GRAD_PLACES)


def run_kernel(body, s, inputs, outputs, scratch, recv, sends, number, carried, back=False):
    if back:
        inputs.update({n: inputs.pop(n) for n in carried})
        near = {n: (inputs[n].shape, inputs[n].dtype) for n in carried}
    else:
        near = {n: outputs.pop(n) for n in carried}
        outputs = {**near, **outputs}
    scratch = {**near, **scratch}
    names_in, names_out, names_scratch = list(inputs), list(outputs), list(scratch)

    places = types.SimpleNamespace()
    arrivals = 0
    for name, count in recv.items():
        setattr(places, name, arrivals)
        arrivals += count

    def kernel(*refs):
        k = types.SimpleNamespace(s=s, at=places)
        for name, ref in zip(names_in + names_out + names_scratch, refs):
            setattr(k, name, ref)
        k.far = {}
        for name, ref in zip(carried, refs[len(names_in) - len(carried) :] if back else refs[len(names_in) :]):
            k.far[name] = ref
        for name, ref in zip(carried, refs[len(names_in) + len(names_out) :]):
            setattr(k, name, ref)
        k.send_sem, k.recv_sem, k.carry_sem, k.local_sem = refs[-4:]
        k.net = Net(k)
        k.grads = []
        for n in range(PROJECT + 1):
            of = [getattr(k, word + str(n), None) for word in GRAD_REFS]
            at = [getattr(places, word + str(n), None) for word in GRAD_PLACES]
            k.grads.append(Grad(*of, *at))
        body(k)

    def space(name):
        if name in carried or name in FAR_INPUTS:
            return pl.BlockSpec(memory_space=pl.ANY)
        scalar = name in inputs and inputs[name].dtype == jnp.int32 and inputs[name].ndim == 1
        return pl.BlockSpec(memory_space=pltpu.SMEM if scalar else pltpu.VMEM)

    results = pl.pallas_call(
        kernel,
        out_shape=[jax.ShapeDtypeStruct(*outputs[n]) for n in names_out],
        in_specs=[space(n) for n in names_in],
        out_specs=[space(n) for n in names_out],
        scratch_shapes=[pltpu.VMEM(*scratch[n]) for n in names_scratch]
        + [pltpu.SemaphoreType.DMA((sends,)), pltpu.SemaphoreType.DMA((arrivals,)), pltpu.SemaphoreType.DMA((len(carried),)), pltpu.SemaphoreType.DMA((4,))],
        compiler_params=pltpu.CompilerParams(
            collective_id=number, has_side_effects=True, vmem_limit_bytes=VMEM_BYTES
        ),
        name=body.__name__,
    )(*inputs.values())
    return dict(zip(names_out, results))


def reduce_scratch(s):
    return dict(
        stage=((3, s.rows, s.dim), BF16),
        from_sib=((2, s.rows, s.dim), BF16),
        from_across=((s.rows, s.dim), BF16),
        own_part=((s.rows, s.dim), F32),
        across_part=((s.rows, s.dim), F32),
    )


def forward_call(s, inputs):
    wide = s.here * s.head
    all_rows = 4 * s.rows
    outputs = dict(
        h_one=((4, s.rows, s.dim), BF16),
        q=((s.here, all_rows, 2 * s.head), BF16),
        keys=((s.here, all_rows, 2 * s.head), BF16),
        values=((s.here, all_rows, 2 * s.head), BF16),
        outs=((s.here, all_rows, 2 * s.head), F32),
        mixed_main=((4, s.rows, 2 * s.head), BF16),
        mixed_third=((4, s.pack, 2 * s.head), BF16),
        token_rows=((s.rows, s.dim), F32),
        after=((s.rows, s.dim), F32),
        h_two=((4, s.rows, s.dim), BF16),
        act=((4, s.rows, s.hidden), BF16),
        slope=((4, s.rows, s.hidden), BF16),
        final=((s.rows, s.dim), F32),
        patch_unit=((s.own + 2 * WP, s.dim), BF16),
        head_gain=((8, s.lanes), F32),
        class_unit=((s.lanes, s.dim), BF16),
        logit_unit=((s.own, s.lanes), F32),
        logit_scale=((s.own, 128), F32),
        cells=((s.own + 2 * WP, s.lanes), BF16),
        halo=((2 * EDGE, s.wide_pixels), jnp.int32),
        gains=((8, s.dim), F32),
    )
    scratch = dict(
        tokens=((4, s.own, s.dim), BF16),
        cls_rows=((s.lanes, s.dim), F32),
        mixed=((4, s.rows, wide), BF16),
        third_out=((4, s.pack, 2 * s.head), BF16),
        cls_units=((4, s.slot, s.dim), BF16),
        **reduce_scratch(s),
    )
    recv = dict(tokens=4, mixed=4, third=4, h_two=4, feed=12, units=4, rim=2, halo=2)
    sends = 3 + 6 + 3 + 12 + 3 + 2 + 2
    if s.img_comm:
        shard = s.dim // s.images
        outputs.update(w_joint=((s.images, shard, 3 * wide), BF16))
        outputs.update(w_project=((s.images, shard, s.dim), BF16))
        scratch.update(small=((s.lanes, 128), BF16), wq=((shard, 3 * wide), BF16))
        scratch.update(wi=((shard, s.hidden), BF16), w_in_near=((shard, 4 * s.hidden), BF16))
        outputs.update(w_expand=((s.images, shard, s.hidden), BF16))
        outputs.update(w_reduce=((s.images, shard, s.dim), BF16))
        scratch.update(smalls=((s.images, s.lanes, 128), BF16))
        n = s.images
        recv.update(small=n, joint0=n, joint1=n, w_project=n, w_shared=4)
        recv.update(expand0=n, expand1=n, reduce0=n, reduce1=n)
        sends += 2 * (n // PLANE) - 1 + 7 * (4 * (n // PLANE) - 3) + 3
    carried = [n for n in CARRIED if n in outputs]
    return run_kernel(forward_kernel, s, inputs, outputs, scratch, recv, sends, 1, carried)


def backward_call(s, inputs, carried):
    wide = s.here * s.head
    all_rows = 4 * s.rows
    outputs = dict(patch_grad=((1, s.own, s.dim), F32))
    scratch = dict(
        class_out=((4, s.slot, s.dim), BF16),
        class_in=((4, s.slot, s.dim), BF16),
        d_rows=((s.rows, s.dim), F32),
        d_branch=((4, s.rows, s.dim), BF16),
        d_pre=((4, s.rows, s.hidden), BF16),
        main_out=((4, s.rows, 2 * s.head), BF16),
        main_in=((4, s.rows, 2 * s.head), BF16),
        third_out=((4, s.pack, 2 * s.head), BF16),
        third_in=((4, s.pack, 2 * s.head), BF16),
        powers=((s.here, all_rows, all_rows), BF16),
        d_scores=((all_rows, all_rows), BF16),
        d_out=((all_rows, 2 * s.head), BF16),
        q_back=((s.here, all_rows, 2 * s.head), BF16),
        d_pair=((all_rows, 2 * s.head), F32),
        d_joint=((s.here, all_rows, 3 * s.head), BF16),
        **reduce_scratch(s),
    )
    recv = dict(class_=4, d_branch=4, d_first=4, d_class=4, feed=6, d_mixed=4, third=4, joint=6)
    sends = 3 + 3 + 3 + 3 + 6 + 6 + 6
    columns = [s.dim // 2] * 2 + [s.hidden // 2] * 2 + [3 * s.head * (s.here - 1), 3 * s.head]
    columns += [s.dim // 2] * s.img_comm
    planes, shard = s.images // PLANE, s.dim // s.images
    for n, cols in enumerate(columns):
        out, blocks, from_mate, from_line = [word + str(n) for word in GRAD_REFS]
        at_mate, at_line, at_out = [word + str(n) for word in GRAD_PLACES]
        if not s.img_comm:
            outputs[out] = ((s.dim, cols), BF16)
            continue
        rows = shard // 2 if n == PROJECT else shard
        outputs[out] = ((4, rows, cols), BF16)
        scratch[blocks] = ((PLANE, planes, rows, cols), BF16)
        for what in (from_mate, from_line):
            scratch[what] = ((planes, rows, cols), BF16)
        recv[at_mate] = 1
        recv[at_line] = planes
        recv[at_out] = 4
        sends += 1 + planes - 1 + 3
    if s.img_comm:
        outputs.update(small_sum=((4, s.slot, 128), F32))
        piece = (s.images, shard // 2, s.dim // 2)
        scratch.update(p_out=((4, *piece), BF16), p_sib=((2, *piece), BF16))
        scratch.update(p_across=(piece, BF16), p_stage=(piece, BF16))
        scratch.update(small_out=((s.images, s.slot, 128), BF16))
        scratch.update(small_in=((s.images, s.slot, 128), BF16))
        recv.update(project=3, small=s.images, small_sum=4)
        sends += 3 + s.images - 1 + 3
    else:
        outputs.update(d_project=((s.dim, s.dim), BF16))
        outputs.update(small_out=((s.slot, s.dim), F32))
        outputs.update(head_out=((s.slot, 128), F32))
    return run_kernel(backward_kernel, s, inputs, outputs, scratch, recv, sends, 2, carried, True)


def write_call(s, grads, pieces, raw):
    shard = s.dim // s.images
    outputs = dict(
        patch_grad=((1, s.own, s.dim), F32),
        d_w_back=((4 * shard, s.dim), F32),
        d_w_in=((shard, 4 * s.hidden), F32),
        d_w_qkv=((shard, 3 * s.dim), F32),
        d_w_out=((shard, s.dim), F32),
        d_cls=((s.classes, shard), F32),
        d_gain_one=((1, shard), F32),
        d_gain_two=((1, shard), F32),
        d_head=((1, s.classes), F32),
    )
    inputs = dict(patch_rows=grads.patch_grad, project=pieces[PROJECT], small_sum=grads.small_sum)
    inputs.update(back0=pieces[0], back1=pieces[1], into0=pieces[2], into1=pieces[3])
    inputs.update(pair=pieces[JOINT], last=pieces[LAST], **raw)

    def kernel(*refs):
        k = types.SimpleNamespace(s=s, **dict(zip(list(inputs) + list(outputs), refs)))
        k.back, k.into = (k.back0, k.back1), (k.into0, k.into1)
        write_kernel(k)

    whole = pl.BlockSpec(memory_space=pltpu.VMEM)
    results = pl.pallas_call(
        kernel,
        out_shape=[jax.ShapeDtypeStruct(*v) for v in outputs.values()],
        in_specs=[whole] * len(inputs),
        out_specs=[whole] * len(outputs),
        compiler_params=pltpu.CompilerParams(vmem_limit_bytes=VMEM_BYTES),
        name=write_kernel.__name__,
    )(*inputs.values())
    return types.SimpleNamespace(**dict(zip(outputs, results)))


def sizes(patches, cls_emb, w_joint, w_back, head_gain):
    images, tiles = lax.axis_size(IMG), lax.axis_size(TILE)
    s = types.SimpleNamespace(images=images, tiles=tiles)
    s.dim = patches.shape[2]
    s.own = patches.shape[1]
    s.grid = s.own // WP
    s.wide_pixels = WP * UP
    s.classes = head_gain.shape[0]
    s.step = -(-s.classes // (8 * tiles)) * 8
    s.slot = -(-s.step // 16) * 16
    s.lanes = s.step * tiles
    s.rows = s.own + s.slot
    s.pack = -(-s.rows // 32) * 16
    s.head = s.dim // HEADS
    s.here = HEADS // tiles
    s.hidden = w_back.shape[0] * images // tiles
    shard = w_joint.shape[0]
    s.img_comm = images == PLANE * tiles and shard % 16 == 0 and shard <= 128
    return s


def shards(
    patches, labels, heights, cls_emb, gain_one, w_qkv, w_out, gain_two, w_in, w_back, head_gain
):
    s = sizes(patches, cls_emb, w_qkv, w_back, head_gain)
    t = lax.axis_index(TILE)
    shard = w_qkv.shape[0]
    wide = s.here * s.head

    part = w_back.shape[0] // s.tiles
    w_back = w_back.reshape(s.tiles, part, s.dim)
    cls_emb, gain_one, gain_two = cls_emb, gain_one[None], gain_two[None]
    inputs = dict(patches=patches, labels=labels, height=heights, gain_row=head_gain)
    common = {}
    if s.img_comm:
        inputs.update(cls_emb=cls_emb, gain_one=gain_one, gain_two=gain_two)
        inputs.update(w_qkv=w_qkv, wo=w_out, w_in=w_in, wb=w_back)
    else:

        def gather(value, axis=0):
            return lax.all_gather(value, IMG, axis=axis, tiled=True)

        def pick(value, axis):
            return lax.dynamic_index_in_dim(value, t, axis, keepdims=False)

        joint = pick(w_qkv.reshape(shard, 3, s.tiles, s.here, s.head), 2)
        joint = joint.transpose(0, 2, 1, 3).reshape(shard, 3 * wide)
        expand = pick(w_in.reshape(shard, s.images, s.tiles, part), 2).reshape(shard, s.hidden)
        reduce = pick(w_back, 0)
        small = jnp.concatenate([cls_emb, gain_one, gain_two], axis=0)
        small = jnp.pad(small, ((0, s.lanes - small.shape[0]), (0, 0)))
        common.update(
            w_joint=gather(joint)[None],
            w_project=gather(w_out)[None],
            w_expand=gather(expand)[None],
            w_reduce=gather(reduce)[None],
        )
        inputs.update(small_full=gather(small, 1), **common)
    arrays = forward_call(s, inputs)
    cells, halo = arrays.pop(CELLS), arrays.pop(HALO)
    masks, cell_sums = upsampled_loss(cells, labels, halo, heights, s.classes)
    carried = [n for n in CARRIED if n in arrays]
    grads = backward_call(s, dict(**arrays, **common, cell_sums=cell_sums), carried)
    grads = types.SimpleNamespace(**grads)
    count = PROJECT + 1 if s.img_comm else PROJECT
    pieces = [getattr(grads, GRAD_REFS[0] + str(n)) for n in range(count)]
    if s.img_comm:
        raw = dict(w_qkv=w_qkv, w_in=w_in, gain_one=gain_one, gain_two=gain_two)
        written = write_call(s, grads, pieces, raw)
        return (
            masks[None],
            written.patch_grad,
            written.d_cls,
            written.d_gain_one[0],
            written.d_w_qkv,
            written.d_w_out,
            written.d_gain_two[0],
            written.d_w_in,
            written.d_w_back,
            written.d_head[0],
        )

    def across(value):
        return lax.all_gather(value, TILE, axis=0, tiled=False)

    def total(value, axis=0):
        return lax.psum_scatter(value, IMG, scatter_dimension=axis, tiled=True)

    pieces = [across(total(v)) for v in pieces]
    back, into = [jnp.concatenate(pieces[n : n + 2], axis=2) for n in (BACK, INTO)]
    project = total(lax.psum(grads.d_project, TILE))
    small = across(total(grads.small_out, 1))
    head_rows = across(lax.psum(grads.head_out, IMG))
    joint = jnp.concatenate(pieces[JOINT:], axis=2)
    joint = joint.reshape(s.tiles, shard, s.here, 3, s.head).transpose(1, 3, 0, 2, 4)
    joint = joint.reshape(shard, -1).astype(F32)
    expand = into.reshape(s.tiles, shard, s.images, part).transpose(1, 2, 0, 3)
    expand = expand.reshape(shard, -1).astype(F32)
    cls_grad = small[:, : s.step, :shard].reshape(s.lanes, shard)[: s.classes]
    head_grad = jnp.sum(head_rows[:, s.step : s.step + 2, :128], axis=0).reshape(-1)[: s.classes]
    return (
        masks[None],
        grads.patch_grad,
        cls_grad,
        gain_sums(w_qkv, joint)[:, 0] / gain_one[0].astype(F32),
        joint,
        project.astype(F32),
        gain_sums(w_in, expand)[:, 0] / gain_two[0].astype(F32),
        expand,
        back.reshape(-1, s.dim).astype(F32),
        head_grad,
    )


def solution(mesh):
    in_specs = (
        P(IMG, TILE, None),
        P(IMG, TILE, None),
        P(IMG),
        P(None, IMG),
        P(IMG),
        P(IMG, None),
        P(IMG, None),
        P(IMG),
        P(IMG, None),
        P(IMG, None),
        P(),
    )
    out_specs = (
        P(IMG, None, TILE, None),
        P(IMG, TILE, None),
        P(None, IMG),
        P(IMG),
        P(IMG, None),
        P(IMG, None),
        P(IMG),
        P(IMG, None),
        P(IMG, None),
        P(),
    )
    return jax.shard_map(shards, mesh=mesh, in_specs=in_specs, out_specs=out_specs, check_vma=False)
```

```python
import collections
import functools
import types

import jax
import jax.numpy as jnp
import numpy as np
from jax import lax
from jax.experimental import pallas as pl
from jax.experimental.pallas import tpu as pltpu
from jax.sharding import PartitionSpec as P

IMG = "img"
TILE = "tile"
HEADS = 12
WP = 16
UP = 16
BAND = 32
BAND_CELLS = 4
GROUP = 8
EDGE = UP // 2
MESH = pl.DeviceIdType.MESH
LOGIT_UNIT = "logit_unit"
LOGIT_SCALE = "logit_scale"
HEAD_GAIN = "head_gain"
PATCH_UNIT = "patch_unit"
CLASS_UNIT = "class_unit"
FINAL = "final"
W_REDUCE = "w_reduce"
SLOPE = "slope"
W_EXPAND = "w_expand"
ACT = "act"
H_TWO = "h_two"
AFTER = "after"
GAINS = "gains"
W_PROJECT = "w_project"
Q = "q"
KEYS = "keys"
OUTS = "outs"
VALUES = "values"
MIXED_MAIN = "mixed_main"
MIXED_THIRD = "mixed_third"
H_ONE = "h_one"
W_JOINT = "w_joint"
TOKEN_ROWS = "token_rows"
F32 = jnp.float32
BF16 = jnp.bfloat16
PLANE = 2
BACK, INTO, JOINT, LAST, PROJECT = 0, 2, 4, 5, 6
VMEM_BYTES = 62 << 20


def product(left, right):
    return jnp.dot(left, right, preferred_element_type=F32)


def times_transposed(left, right):
    return lax.dot_general(left, right, (((1,), (1,)), ((), ())), preferred_element_type=F32)


def transposed_times(left, right):
    return lax.dot_general(left, right, (((0,), (0,)), ((), ())), preferred_element_type=F32)


def layer_norm_parts(value):
    centre = jnp.mean(value, axis=-1, keepdims=True)
    centred = value - centre
    spread = jnp.mean(centred * centred, axis=-1, keepdims=True)
    scale = lax.rsqrt(spread + 1e-05)
    return centred * scale, scale


def layer_norm_back(unit, scale, gain, upstream):
    weighted = upstream * gain
    mean = jnp.mean(weighted, axis=-1, keepdims=True)
    along = jnp.mean(weighted * unit, axis=-1, keepdims=True)
    return scale * (weighted - mean - unit * along)


def gelu_pair(x):
    root = np.float32(np.sqrt(2.0 / np.pi))
    square = x * x
    turned = jnp.tanh(root * x * (1.0 + np.float32(0.044715) * square))
    half = 0.5 * (1.0 + turned)
    slope = half + 0.5 * x * (1.0 - turned * turned) * root * (
        1.0 + np.float32(3 * 0.044715) * square
    )
    return x * half, slope


def lane_iota(rows, lanes):
    return lax.broadcasted_iota(jnp.int32, (rows, lanes), 1)


def row_iota(rows, lanes):
    return lax.broadcasted_iota(jnp.int32, (rows, lanes), 0)


def carry_copy(k, name, back=False):
    near, far = getattr(k, name), k.far[name]
    n = list(k.far).index(name)
    ends = (far, near) if back else (near, far)
    return pltpu.make_async_copy(*ends, k.carry_sem.at[n])


def keep(k, name):
    if name in k.far:
        carry_copy(k, name).start()


def kept(k):
    for name in k.far:
        carry_copy(k, name).wait()


def fetch_all(k):
    for name in k.far:
        carry_copy(k, name, True).start()


def have(k, *names):
    for name in names:
        if name in k.far:
            carry_copy(k, name, True).wait()


class Net:
    def __init__(self, k):
        self.k = k
        self.sent = []
        self.stage_sends = []

    def send(self, source, target, base, slot, device, when=None):
        k = self.k
        copy = pltpu.make_async_remote_copy(
            src_ref=source,
            dst_ref=target,
            send_sem=k.send_sem.at[len(self.sent)],
            recv_sem=k.recv_sem.at[base + slot],
            device_id=device,
            device_id_type=MESH,
        )
        self.sent.append((copy, when))
        if when is None:
            copy.start()
        else:
            pl.when(when)(copy.start)
        return len(self.sent) - 1

    def arrived(self, target, base, slot):
        k = self.k
        pltpu.make_async_remote_copy(
            src_ref=target,
            dst_ref=target,
            send_sem=k.send_sem.at[0],
            recv_sem=k.recv_sem.at[base + slot],
            device_id=k.sibling,
            device_id_type=MESH,
        ).wait_recv()

    def gone(self, number):
        if self.sent[number] is None:
            return
        copy, when = self.sent[number]
        self.sent[number] = None
        if when is None:
            copy.wait_send()
        else:
            pl.when(when)(copy.wait_send)

    def drain(self):
        for number in range(len(self.sent)):
            self.gone(number)


def place(k):
    k.i = lax.axis_index(IMG)
    k.t = lax.axis_index(TILE)
    k.y = k.i % PLANE
    k.z = k.i // PLANE
    k.planes = k.s.images // PLANE
    k.ts = k.t + 1 - 2 * (k.t % 2)
    k.tx = (k.t + 2) % 4
    k.td = (k.ts + 2) % 4
    k.sibling = (k.i, k.ts)
    k.across = (k.i, k.tx)
    k.diagonal = (k.i, k.td)
    k.mate = (k.i + 1 - 2 * k.y, k.t)


def line_peer(k, step):
    z = (k.z + step) % k.planes
    return z, (PLANE * z + k.y, k.t)


def enter(k, beside):
    barrier = pltpu.get_barrier_semaphore()
    peers = [k.sibling, k.across, k.diagonal]
    if k.s.img_comm:
        peers += [k.mate] + [line_peer(k, step)[1] for step in range(1, k.planes)]
    for peer in peers:
        pl.semaphore_signal(barrier, inc=1, device_id=peer, device_id_type=MESH)
    done = beside()
    pl.semaphore_wait(barrier, len(peers))
    return done


def spread_start(k, own, slots, name):
    for step in range(1, k.planes):
        k.net.send(own, slots.at[k.i], name, k.i, line_peer(k, step)[1])
    k.net.send(own, slots.at[k.i], name, k.i, k.mate)


def spread_pass(k, slots, name):
    for step in range(1, k.planes):
        z = (k.z + k.planes - step) % k.planes
        i = PLANE * z + k.y
        k.net.arrived(slots.at[i], name, i)
        k.net.send(slots.at[i], slots.at[i], name, i, k.mate)


def spread_end(k, slots, name):
    for z in range(k.planes):
        i = PLANE * z + 1 - k.y
        k.net.arrived(slots.at[i], name, i)


def line_start(k, own, slots, base, cut):
    send = k.net.send
    own, there = own.at[cut], slots.at[(k.i, *cut)]
    send(own, there, base, k.i, line_peer(k, 1)[1], k.z < k.planes - 1)
    send(own, there, base, k.i, line_peer(k, k.planes - 1)[1], k.z > 0)
    send(own, there, base, k.i, k.mate)


def line_end(k, slots, base, cut):
    for z in range(k.planes):
        i = PLANE * z + 1 - k.y
        k.net.arrived(slots.at[(i, *cut)], base, i)


def line_hop(k, slots, base, far, cut):
    send = k.net.send
    for sign in (-1, 1):
        here = k.z >= far if sign < 0 else k.z < k.planes - far
        more = k.z < k.planes - 1 if sign < 0 else k.z > 0
        i = PLANE * ((k.z + sign * far + k.planes) % k.planes) + k.y
        there = slots.at[(i, *cut)]

        @pl.when(here)
        def _(i=i, there=there):
            k.net.arrived(there, base, i)

        if far < k.planes - 1:
            peer = line_peer(k, 1 if sign < 0 else k.planes - 1)[1]
            send(there, there, base, i, peer, here & more)
        send(there, there, base, i, k.mate, here)


def project_cut(k, tile):
    rows, columns = k.s.dim // k.s.images // 2, k.s.dim // 2
    return (
        pl.ds(pl.multiple_of(rows * (tile // 2), 16), rows),
        pl.ds(pl.multiple_of(columns * (tile % 2), 128), columns),
    )


def project_part(k, tile):
    rows, columns = project_cut(k, tile)
    return k.w_project.at[:, rows, columns]


def slot_part(slots, slot, rows):
    return slots.at[slot] if rows is None else slots.at[slot, rows]


def share_start(k, slots, base, rows=None):
    own = slot_part(slots, k.t, rows)
    k.net.send(own, own, base, k.t, k.across)
    k.net.send(own, own, base, k.t, k.sibling)


def share_pass(k, slots, base, rows=None):
    part = slot_part(slots, k.tx, rows)
    k.net.arrived(part, base, k.tx)
    k.net.send(part, part, base, k.tx, k.sibling)


def halves(s):
    return [pl.ds(n * s.dim // 2, s.dim // 2) for n in range(2)]


def edge_cuts(s):
    first, second = halves(s)
    return [
        (pl.ds(0, s.rows), first),
        (pl.ds(s.own - WP, WP + s.slot), second),
        (pl.ds(0, WP), second),
        (pl.ds(WP, s.own - 2 * WP), second),
    ]


def row_cuts(s):
    return [(pl.ds(s.own, s.slot), pl.ds(0, s.dim)), (pl.ds(0, s.own), pl.ds(0, s.dim))]


def reduce_over_tile(k, base, part, cuts, before=None, ready=None):
    sends = k.net.stage_sends
    for number in sends:
        k.net.gone(number)
    sends.clear()

    def to_sibling(n, kind, slot):
        at = (kind, *cuts[n])
        k.stage[at] = part(slot, *cuts[n]).astype(BF16)
        sends.append(k.net.send(k.stage.at[at], k.from_sib.at[at], base, 3 * n + kind, k.sibling))

    def near(n):
        if before:
            before(k.t, n)
        k.own_part[cuts[n]] = part(k.t, *cuts[n])
        if before:
            before(k.ts, n)
        to_sibling(n, 0, k.ts)

    if before:
        for n in range(len(cuts)):
            near(n)
    for n in range(len(cuts)):
        if ready:
            ready(n)
        if before:
            before(k.tx, n)
            before(k.td, n)
        to_sibling(n, 1, k.td)
        total = part(k.tx, *cuts[n])
        k.across_part[cuts[n]] = total
        k.net.arrived(k.from_sib.at[(1, *cuts[n])], base, 3 * n + 1)
        total = k.across_part[cuts[n]] + k.from_sib[(1, *cuts[n])].astype(F32)
        k.stage[(2, *cuts[n])] = total.astype(BF16)
        ends = k.stage.at[(2, *cuts[n])], k.from_across.at[cuts[n]]
        sends.append(k.net.send(*ends, base, 3 * n + 2, k.across))
        if not before:
            near(n)


def reduced_wait(k, base, cuts, which):
    for n in which:
        k.net.arrived(k.from_sib.at[(0, *cuts[n])], base, 3 * n)
        k.net.arrived(k.from_across.at[cuts[n]], base, 3 * n + 2)


def reduced(k, rows):
    return k.own_part[rows, :] + k.from_sib[0, rows, :].astype(F32) + k.from_across[rows, :].astype(F32)


def pack_third(s, value):
    return jnp.concatenate([value[: s.pack], value[s.rows - s.pack :]], axis=1)


def third_rows(s, packed):
    rest = 2 * s.pack - s.rows
    return jnp.concatenate([packed[:, : s.head], packed[rest:, s.head :]], axis=0)


def key_bias(k, slot, height):
    s = k.s
    rows = row_iota(s.rows, s.head)
    cls = rows - s.own
    patch_ok = (rows < s.own) & (rows < (height - slot * s.grid) * WP)
    class_ok = (cls >= 0) & (cls < s.step) & (slot * s.step + cls < s.classes)
    off = jnp.where(patch_ok | class_ok, 0.0, -1e30)
    lane = lane_iota(s.rows, s.head)
    return jnp.where(lane == 0, off, jnp.where(lane < 4, 1.0, 0.0))


def class_rows(k, slot):
    s = k.s
    rows = k.cls_rows[pl.ds(pl.multiple_of(slot * s.step, 8), s.step), :]
    return jnp.concatenate([rows, jnp.zeros((s.slot - s.step, s.dim), F32)], axis=0)


def slot_rows(k, slot):
    return pl.ds(pl.multiple_of(slot * k.s.rows, 16), k.s.rows)


def block_scores(k, head, slot):
    return times_transposed(k.q[head, slot_rows(k, slot), :], k.keys[head])


def local_copy(k, source, target, number):
    return pltpu.make_async_copy(source, target, k.local_sem.at[number])


def pick_columns(k):
    s = k.s
    wide = s.here * s.head
    for n in range(4):

        @pl.when(k.t == n)
        def _(n=n):
            cut = [
                k.w_qkv[:, s.dim * m + wide * n + s.head * h :][:, : s.head]
                for h in range(s.here)
                for m in range(3)
            ]
            k.wq[...] = jnp.concatenate(cut, axis=1)


def pick_hidden(k):
    part = k.s.hidden // k.s.images
    for n in range(4):

        @pl.when(k.t == n)
        def _(n=n):
            cut = [k.w_in_near[:, part * (4 * i + n) :][:, :part] for i in range(k.s.images)]
            k.wi[...] = jnp.concatenate(cut, axis=1)


def forward_kernel(k):
    s = k.s
    place(k)
    net = k.net
    i, t = k.i, k.t
    shard = s.dim // s.images

    def prepare():
        head_gain = k.gain_row[...].astype(F32).reshape(1, s.classes)
        head_gain = jnp.concatenate([head_gain, jnp.zeros((1, s.lanes - s.classes), F32)], axis=1)
        k.head_gain[...] = jnp.broadcast_to(head_gain, (8, s.lanes))
        if s.img_comm:
            rows = [ref[...].astype(F32) for ref in (k.cls_emb, k.gain_one, k.gain_two)]
            rows += [jnp.zeros((s.lanes - s.classes - 2, shard), F32)]
            table = jnp.concatenate(rows, axis=0)
            table = jnp.concatenate([table, jnp.zeros((s.lanes, 128 - shard), F32)], axis=1)
            k.small[...] = table.astype(BF16)
            pick_columns(k)

    patches, labels = k.patches.at[0], k.labels.at[0]
    tokens_in = local_copy(k, patches, k.tokens.at[t], 1)
    tokens_in.start()
    if s.img_comm:
        w_in_copy = local_copy(k, k.w_in, k.w_in_near, 2)
        w_in_copy.start()
        w_back_copy = local_copy(k, k.wb.at[t], k.w_reduce.at[i], 3)
        w_back_copy.start()
    enter(k, prepare)
    keep(k, HEAD_GAIN)
    comm = s.img_comm
    wide = s.here * s.head
    first, second = halves(s)
    early = pl.ds(0, 3 * s.head * (s.here - 1))
    late = pl.ds(3 * s.head * (s.here - 1), 3 * s.head)
    joint = expand = reduce = (None, None)
    project = None
    if comm:
        at = k.at
        every = pl.ds(0, shard)
        joint = ((k.wq, k.w_joint, at.joint0, early), (k.wq, k.w_joint, at.joint1, late))
        expand = ((k.wi, k.w_expand, at.expand0, first), (k.wi, k.w_expand, at.expand1, second))
        back = k.wb.at[t]
        reduce = ((back, k.w_reduce, at.reduce0, first), (back, k.w_reduce, at.reduce1, second))
        joint, expand, reduce = [
            [(*item[:3], (every, item[3])) for item in pair] for pair in (joint, expand, reduce)
        ]
        project = (k.wo, k.w_project, at.w_project, project_cut(k, t))
        wo_copy = local_copy(k, k.wo.at[project[3]], k.w_project.at[(i, *project[3])], 0)
        wo_copy.start()

    def start(item):
        if comm:
            line_start(k, *item)

    def hop(item, far):
        if comm:
            line_hop(k, *item[1:3], far, item[3])

    def end(item):
        if comm:
            line_end(k, *item[1:])

    if comm:
        spread_start(k, k.small, k.smalls, k.at.small)
        k.smalls[i] = k.small[...]
        start(joint[0])
        start(joint[1])
        start(project)
    net.send(patches, k.tokens.at[t], k.at.tokens, t, k.across)
    net.send(patches, k.tokens.at[t], k.at.tokens, t, k.sibling)
    top, bottom, last = pl.ds(0, EDGE), pl.ds(EDGE, EDGE), pl.ds(s.grid * UP - EDGE, EDGE)
    net.send(labels.at[top], k.halo.at[bottom], k.at.halo, 1, (i, (t + 3) % 4))
    net.send(labels.at[last], k.halo.at[top], k.at.halo, 0, (i, (t + 1) % 4))
    if comm:
        k.w_joint[i] = k.wq[...]
        spread_pass(k, k.smalls, k.at.small)
        hop(joint[0], 1)
        hop(joint[1], 1)
        hop(project, 1)
        w_in_copy.wait()
        pick_hidden(k)
        k.w_expand[i] = k.wi[...]
        hop(joint[0], 2)
        hop(joint[1], 2)
        hop(project, 2)
        start(expand[0])
        spread_end(k, k.smalls, k.at.small)
        pieces = [k.smalls[n].astype(F32)[:, :shard] for n in range(s.images)]
        full = jnp.concatenate(pieces, axis=1)
    else:
        full = k.small_full[...].astype(F32)
    k.gains[0:2] = full[s.classes : s.classes + 2]
    k.cls_rows[...] = jnp.where(row_iota(s.lanes, s.dim) < s.classes, full, 0.0)
    gain_one, gain_two = k.gains[0:1], k.gains[1:2]
    keep(k, GAINS)

    def normed_tokens(slot):
        value = jnp.concatenate([k.tokens[slot].astype(F32), class_rows(k, slot)], axis=0)
        k.h_one[slot] = (layer_norm_parts(value)[0] * gain_one).astype(BF16)

    tokens_in.wait()
    k.token_rows[0 : s.own] = k.tokens[t].astype(F32)
    k.token_rows[s.own : s.rows] = class_rows(k, t)
    keep(k, TOKEN_ROWS)
    normed_tokens(t)
    if comm:
        hop(joint[0], 3)
        hop(joint[1], 3)
        hop(project, 3)
        start(expand[1])
    net.arrived(k.tokens.at[k.ts], k.at.tokens, k.ts)
    normed_tokens(k.ts)
    net.arrived(k.tokens.at[k.tx], k.at.tokens, k.tx)
    net.send(k.tokens.at[k.tx], k.tokens.at[k.tx], k.at.tokens, k.tx, k.sibling)
    normed_tokens(k.tx)
    hop(expand[0], 1)
    net.arrived(k.tokens.at[k.td], k.at.tokens, k.td)
    normed_tokens(k.td)
    keep(k, H_ONE)
    if comm:
        end(joint[0])
        end(joint[1])
        keep(k, W_JOINT)
        end(project)
        wo_copy.wait()
        part = project_part(k, t)
        net.send(part, part, at.w_shared, t, k.across)
        net.send(part, part, at.w_shared, t, k.sibling)

    lane = lane_iota(s.rows, s.head)
    one = jnp.where(lane == 0, 1.0, 0.0)
    ones = jnp.where(lane < 2, 1.0, 0.0)
    height = k.height[0]

    def joint_rows(slot):
        value = product(k.h_one[slot], k.w_joint[...].reshape(s.dim, s.here * 3 * s.head))
        bias = key_bias(k, slot, height)
        rows = slot_rows(k, slot)
        for h in range(s.here):
            cut = [
                value[:, (3 * h + n) * s.head : (3 * h + n + 1) * s.head] for n in range(3)
            ]
            for ref, part, extra in zip(
                (k.q, k.keys, k.values), (cut[0] * s.head**-0.5, cut[1], cut[2]), (one, bias, ones)
            ):
                ref[h, rows, :] = jnp.concatenate([part, extra], axis=1).astype(BF16)

    joint_rows(0)
    hop(expand[0], 2)
    joint_rows(1)
    start(reduce[0])
    joint_rows(2)
    hop(expand[0], 3)
    joint_rows(3)
    keep(k, Q)
    keep(k, KEYS)
    keep(k, VALUES)
    hop(expand[1], 1)

    def attend(slot):
        rows = slot_rows(k, slot)
        wide_lane = lane_iota(s.rows, 2 * s.head)
        parts = []
        for h in range(s.here):
            scores = block_scores(k, h, slot)
            largest = jnp.max(scores, axis=-1, keepdims=True)
            powers = jnp.exp(scores - largest).astype(BF16)
            out = product(powers, k.values[h])
            parts.append(out[:, : s.head] / out[:, s.head : s.head + 1])
            k.outs[h, rows, :] = jnp.where(wide_lane == s.head + 1, largest, out)
        k.mixed[slot] = jnp.concatenate(parts, axis=1).astype(BF16)
        k.third_out[slot] = pack_third(s, parts[2]).astype(BF16)

    for step, slot in enumerate((k.tx, k.td, k.ts, t), 1):
        attend(slot)
        if step < 4:
            main = k.mixed.at[slot, :, pl.ds(0, 2 * s.head)]
            net.send(main, k.mixed_main.at[t], k.at.mixed, t, (i, slot))
            net.send(k.third_out.at[slot], k.mixed_third.at[t], k.at.third, t, (i, slot))
        if step == 1:
            hop(expand[1], 2)
            start(reduce[1])
        if step == 2:
            hop(expand[1], 3)
            if comm:
                part = project_part(k, k.tx)
                net.arrived(part, at.w_shared, k.tx)
                net.send(part, part, at.w_shared, k.tx, k.sibling)
        if step == 3:
            hop(reduce[0], 1)
    keep(k, OUTS)
    k.mixed_main[t] = k.mixed[t, :, pl.ds(0, 2 * s.head)]
    k.mixed_third[t] = k.third_out[t]
    hop(reduce[0], 2)
    hop(reduce[0], 3)
    if comm:
        for slot in (k.ts, k.td):
            net.arrived(project_part(k, slot), at.w_shared, slot)
        keep(k, W_PROJECT)
    after = k.token_rows[...]
    w_project = k.w_project[...].reshape(s.dim, s.dim)
    for step in range(1, 4):
        slot = (t + step) % 4
        net.arrived(k.mixed_main.at[slot], k.at.mixed, slot)
        net.arrived(k.mixed_third.at[slot], k.at.third, slot)
    for n in range(4):
        rows = third_rows(s, k.mixed_third[n].astype(F32)).astype(BF16)
        mixed = jnp.concatenate([k.mixed_main[n], rows], axis=1)
        after = after + product(mixed, w_project[wide * n : wide * (n + 1)])
    keep(k, MIXED_MAIN)
    keep(k, MIXED_THIRD)
    k.after[...] = after
    keep(k, AFTER)
    k.h_two[t] = (layer_norm_parts(after)[0] * gain_two).astype(BF16)
    pieces = ((pl.ds(0, s.pack), k.at.h_two), (pl.ds(s.pack, s.rows - s.pack), k.at.h_second))
    for rows, base in pieces:
        share_start(k, k.h_two, base, rows)
    hop(reduce[1], 1)
    if comm:
        end(expand[0])
        end(expand[1])
        keep(k, W_EXPAND)

    def hidden(slot, rows=pl.ds(0, s.rows)):
        pre = product(k.h_two[slot, rows], k.w_expand[...].reshape(s.dim, s.hidden))
        act, slope = gelu_pair(pre)
        k.act[slot, rows] = act.astype(BF16)
        k.slope[slot, rows] = slope.astype(BF16)

    hidden(t)
    hop(reduce[1], 2)
    for rows, base in pieces:
        net.arrived(k.h_two.at[k.ts, rows], base, k.ts)
    hidden(k.ts)
    hop(reduce[1], 3)
    for rows, base in pieces:
        share_pass(k, k.h_two, base, rows)
        hidden(k.tx, rows)
        net.arrived(k.h_two.at[k.td, rows], base, k.td)
        hidden(k.td, rows)
    keep(k, H_TWO)
    keep(k, ACT)
    keep(k, SLOPE)

    def contract(slot, rows, columns):
        return product(k.act[slot, rows], k.w_reduce[:, :, columns].reshape(s.hidden, s.dim // 2))

    if comm:
        w_back_copy.wait()
    cuts = edge_cuts(s)

    def ready(n):
        if comm and n < 2:
            end(reduce[n])

    reduce_over_tile(k, k.at.feed, contract, cuts, ready=ready)
    if comm:
        keep(k, W_REDUCE)

    def finish(rows):
        final = k.after[rows, :] + reduced(k, rows)
        k.final[rows, :] = final
        square = jnp.sum(final * final, axis=-1, keepdims=True)
        return (final * lax.rsqrt(square + 1e-06)).astype(BF16)

    reduced_wait(k, k.at.feed, cuts, (0, 1, 2))
    last_rows = finish(cuts[1][0])
    k.cls_units[t] = last_rows[WP:]
    k.patch_unit[s.own : WP + s.own] = last_rows[:WP]
    k.patch_unit[WP : 2 * WP] = finish(cuts[2][0])
    above, below = pl.ds(0, WP), pl.ds(WP + s.own, WP)
    for slot in (k.tx, k.td, k.ts):
        net.send(k.cls_units.at[t], k.cls_units.at[t], k.at.units, t, (i, slot))
    net.send(k.patch_unit.at[pl.ds(WP, WP)], k.patch_unit.at[below], k.at.rim, 1, (i, (t + 3) % 4))
    net.send(k.patch_unit.at[pl.ds(s.own, WP)], k.patch_unit.at[above], k.at.rim, 0, (i, (t + 1) % 4))
    reduced_wait(k, k.at.feed, cuts, (3,))
    k.patch_unit[2 * WP : s.own] = finish(cuts[3][0])
    keep(k, FINAL)
    for slot in (k.ts, k.tx, k.td):
        net.arrived(k.cls_units.at[slot], k.at.units, slot)
    net.arrived(k.patch_unit.at[above], k.at.rim, 0)
    net.arrived(k.patch_unit.at[below], k.at.rim, 1)
    units = jnp.concatenate([k.cls_units[n].astype(F32)[: s.step] for n in range(4)], axis=0)
    units = jnp.where(row_iota(s.lanes, s.dim) < s.classes, units, 0.0).astype(BF16)
    k.class_unit[...] = units
    keep(k, CLASS_UNIT)
    keep(k, PATCH_UNIT)
    logits = times_transposed(k.patch_unit[...], units)
    unit_logits, scale = class_norm_parts(k, logits)
    k.logit_unit[...] = unit_logits[WP : WP + s.own]
    k.logit_scale[...] = jnp.broadcast_to(scale[WP : WP + s.own], (s.own, 128))
    keep(k, LOGIT_UNIT)
    keep(k, LOGIT_SCALE)
    normed = (unit_logits * k.head_gain[0:1]).astype(BF16)
    k.cells[WP : WP + s.own] = normed[WP : WP + s.own]
    k.cells[:WP] = jnp.where(t == 0, normed[WP : 2 * WP], normed[:WP])
    k.cells[WP + s.own :] = jnp.where(t == 3, normed[s.own : WP + s.own], normed[WP + s.own :])
    net.arrived(k.halo.at[pl.ds(0, EDGE)], k.at.halo, 0)
    net.arrived(k.halo.at[pl.ds(EDGE, EDGE)], k.at.halo, 1)
    kept(k)
    net.drain()


def class_norm_parts(k, value):
    s = k.s
    real = lane_iota(value.shape[0], s.lanes) < s.classes
    centre = jnp.sum(value, axis=-1, keepdims=True) / s.classes
    centred = jnp.where(real, value - centre, 0.0)
    spread = jnp.sum(centred * centred, axis=-1, keepdims=True) / s.classes
    scale = lax.rsqrt(spread + 1e-05)
    return centred * scale, scale


def sum_start(k, name):
    g = k.grads[name]
    k.net.send(g.blocks.at[1 - k.y], g.from_mate, g.at_mate, 0, k.mate)


def sum_pass(k, name):
    g = k.grads[name]
    k.net.arrived(g.from_mate, g.at_mate, 0)
    for step in range(k.planes):
        z = (k.z + step) % k.planes
        both = g.blocks[k.y, z].astype(F32) + g.from_mate[z].astype(F32)
        g.blocks[k.y, z] = both.astype(BF16)
        if step:
            k.net.send(g.blocks.at[k.y, z], g.from_line.at[k.z], g.at_line, k.z, line_peer(k, step)[1])


def sum_end(k, name):
    g = k.grads[name]
    total = g.blocks[k.y, k.z].astype(F32)
    for step in range(1, k.planes):
        z = (k.z + step) % k.planes
        k.net.arrived(g.from_line.at[z], g.at_line, z)
        total = total + g.from_line[z].astype(F32)
    g.out[k.t] = total.astype(BF16)
    if name != LAST:
        share_start(k, g.out, g.at_out)
        return
    for slot in (k.tx, k.td, k.ts):
        k.net.send(g.out.at[k.t], g.out.at[k.t], g.at_out, k.t, (k.i, slot))


def sum_share(k, name):
    g = k.grads[name]
    share_pass(k, g.out, g.at_out)


def sum_close(k, name):
    g = k.grads[name]
    if name == LAST:
        k.net.arrived(g.out.at[k.tx], g.at_out, k.tx)
    k.net.arrived(g.out.at[k.ts], g.at_out, k.ts)
    k.net.arrived(g.out.at[k.td], g.at_out, k.td)


def put_blocks(k, name, value):
    g = k.grads[name]
    if not k.s.img_comm:
        g.out[...] = value.astype(BF16)
        return
    rows = value.shape[0] // k.s.images
    for i in range(k.s.images):
        g.blocks[i % PLANE, i // PLANE] = value[rows * i : rows * (i + 1)].astype(BF16)


def head_powers(k, h):
    s = k.s
    out = k.outs[h]
    total = out[:, s.head + 1 : s.head + 2] + jnp.log(out[:, s.head : s.head + 1])
    first = total.astype(BF16).astype(F32)
    second = (total - first).astype(BF16).astype(F32)
    lane = lane_iota(4 * s.rows, 2 * s.head) - s.head
    value = jnp.where(lane == 1, -first, k.q[h].astype(F32))
    value = jnp.where(lane == 2, -second, value)
    k.q_back[h] = jnp.where(lane == 3, first + second - total, value).astype(BF16)

    def block(slot, carry):
        rows = slot_rows(k, slot)
        scores = times_transposed(k.keys[h, rows, :], k.q_back[h])
        k.powers[h, rows, :] = jnp.exp(scores).astype(BF16)
        return carry

    lax.fori_loop(0, 4, block, 0, unroll=True)


def head_back(k):
    s = k.s
    top = jnp.where(k.t == 0, k.cell_sums[:WP], 0.0)
    bottom = jnp.where(k.t == 3, k.cell_sums[WP + s.own :], 0.0)
    own = k.cell_sums[WP : WP + s.own]
    own = jnp.concatenate(
        [own[:WP] + top, own[WP : s.own - WP], own[s.own - WP :] + bottom], axis=0
    )
    upstream = own.astype(BF16).astype(F32)
    have(k, LOGIT_UNIT, LOGIT_SCALE, HEAD_GAIN, PATCH_UNIT, CLASS_UNIT, FINAL)
    unit, scale = k.logit_unit[...], k.logit_scale[:, :1]
    weighted = upstream * k.head_gain[0:1]
    mean = jnp.sum(weighted, axis=-1, keepdims=True) / s.classes
    along = jnp.sum(weighted * unit, axis=-1, keepdims=True) / s.classes
    head_row = jnp.sum(upstream * unit, axis=0, keepdims=True)
    d_logits = scale * (weighted - mean - unit * along)
    d_logits = jnp.where(lane_iota(s.own, s.lanes) < s.classes, d_logits, 0.0).astype(BF16)
    d_class = transposed_times(d_logits, k.patch_unit[WP : WP + s.own])
    for n in range(4):
        k.class_out[n] = jnp.concatenate(
            [d_class[s.step * n : s.step * (n + 1)], jnp.zeros((s.slot - s.step, s.dim), F32)], axis=0
        ).astype(BF16)
    return d_logits, head_row


def backward_kernel(k):
    s = k.s
    place(k)
    fetch_all(k)
    d_logits, head_row = enter(k, lambda: head_back(k))
    net = k.net
    i, t = k.i, k.t
    comm = s.img_comm
    split = s.own // 2
    first_part, patch_part = pl.ds(0, split), pl.ds(split, s.own - split)
    class_part = pl.ds(s.own, s.slot)

    for slot in (k.ts, k.tx, k.td):
        net.send(k.class_out.at[slot], k.class_in.at[t], k.at.class_, t, (i, slot))
    final = k.final[...]
    c = lax.rsqrt(jnp.sum(final * final, axis=-1, keepdims=True) + 1e-06)
    u = final * c

    def unit_back(rows, du):
        return c[rows] * (du - u[rows] * jnp.sum(u[rows] * du, axis=-1, keepdims=True))

    d_patch = unit_back(slice(0, s.own), product(d_logits, k.class_unit[...]))
    k.d_rows[: s.own] = d_patch
    k.d_branch[t, : s.own] = d_patch.astype(BF16)
    share_start(k, k.d_branch, k.at.d_first, first_part)
    share_start(k, k.d_branch, k.at.d_branch, patch_part)
    d_class_unit = k.class_out[t].astype(F32)
    for slot in (k.ts, k.tx, k.td):
        net.arrived(k.class_in.at[slot], k.at.class_, slot)
        d_class_unit = d_class_unit + k.class_in[slot].astype(F32)
    d_class = unit_back(slice(s.own, s.rows), d_class_unit)
    k.d_rows[s.own :] = d_class
    k.d_branch[t, s.own :] = d_class.astype(BF16)
    share_start(k, k.d_branch, k.at.d_class, class_part)

    have(k, W_REDUCE, SLOPE, W_EXPAND)

    every = pl.ds(0, s.dim)
    cuts = [(first_part, every), (pl.ds(split, s.rows - split), every)]

    def contract_back(slot, n):
        rows = cuts[n][0]
        d_act = times_transposed(k.d_branch[slot, rows], k.w_reduce[...].reshape(s.hidden, s.dim))
        k.d_pre[slot, rows] = (d_act * k.slope[slot, rows].astype(F32)).astype(BF16)

    def expand_back(slot, rows, columns):
        return times_transposed(k.d_pre[slot, rows], k.w_expand[...].reshape(s.dim, s.hidden))

    def before(slot, n):
        parts = ((first_part, k.at.d_first),)
        if n:
            parts = ((patch_part, k.at.d_branch), (class_part, k.at.d_class))
        if slot is k.tx and n == 0:
            have(k, Q, KEYS, OUTS)
            head_powers(k, 0)
        if slot is k.tx and n == 1:
            head_powers(k, 1)
        for rows, base in parts:
            if slot is k.tx:
                share_pass(k, k.d_branch, base, rows)
            elif slot is not t:
                net.arrived(k.d_branch.at[slot, rows], base, slot)
        contract_back(slot, n)

    reduce_over_tile(k, k.at.feed, expand_back, cuts, before)
    tall = 4 * s.rows
    have(k, ACT, H_TWO)
    for n, columns in enumerate(halves(s)):
        right = k.d_branch[:, :, columns].reshape(tall, s.dim // 2)
        put_blocks(k, BACK + n, transposed_times(k.act[...].reshape(tall, s.hidden), right))
        if comm:
            sum_start(k, BACK + n)
    for n, columns in enumerate(halves(s)):
        right = k.d_pre[:, :, columns].reshape(tall, s.hidden // 2)
        put_blocks(k, INTO + n, transposed_times(k.h_two[...].reshape(tall, s.dim), right))
        if comm:
            sum_start(k, INTO + n)
    head_powers(k, 2)

    have(k, AFTER, GAINS, W_PROJECT, VALUES, MIXED_MAIN, MIXED_THIRD, H_ONE, W_JOINT, TOKEN_ROWS)
    unit, scale = layer_norm_parts(k.after[...])
    reduced_wait(k, k.at.feed, cuts, (0, 1))
    part = layer_norm_back(unit, scale, k.gains[1:2], reduced(k, pl.ds(0, s.rows)))
    d_after = k.d_rows[...] + part
    k.d_rows[...] = d_after
    d_attn = d_after.astype(BF16)
    wide = s.here * s.head
    for slot in (k.tx, k.td, k.ts, t):
        if comm:
            rows = k.w_project[pl.ds(PLANE * slot, PLANE)].reshape(wide, s.dim)
        else:
            rows = k.w_project[0, pl.ds(pl.multiple_of(slot * wide, 16), wide), :]
        value = times_transposed(d_attn, rows)
        k.main_out[slot] = value[:, : 2 * s.head].astype(BF16)
        k.third_out[slot] = pack_third(s, value[:, 2 * s.head :]).astype(BF16)
        if slot is not t:
            net.send(k.main_out.at[slot], k.main_in.at[t], k.at.d_mixed, t, (i, slot))
    for slot in (k.tx, k.td, k.ts):
        net.send(k.third_out.at[slot], k.third_in.at[t], k.at.third, t, (i, slot))
    k.main_in[t] = k.main_out[t]
    k.third_in[t] = k.third_out[t]
    project_start(k, d_attn)
    if comm:
        sum_pass(k, BACK)
        project_across(k)
        sum_pass(k, BACK + 1)

    for slot in (k.ts, k.tx, k.td):
        net.arrived(k.main_in.at[slot], k.at.d_mixed, slot)

    for h in range(s.here):
        if comm and h == 2:
            sum_pass(k, INTO + 1)
        out = k.outs[h]
        if h < 2:
            d_mixed = k.main_in[...].reshape(tall, 2 * s.head)[:, s.head * h :][:, : s.head].astype(F32)
        else:
            for slot in (k.ts, k.tx, k.td):
                net.arrived(k.third_in.at[slot], k.at.third, slot)
            thirds = [third_rows(s, k.third_in[n].astype(F32)) for n in range(4)]
            d_mixed = jnp.concatenate(thirds, axis=0)
        along = jnp.sum(d_mixed * out[:, : s.head], axis=-1, keepdims=True)
        along = along / out[:, s.head : s.head + 1]
        high = along.astype(BF16).astype(F32)
        lane = lane_iota(tall, s.head)
        tail = jnp.where(lane == 0, -high, jnp.where(lane == 1, high - along, 0.0))
        k.d_out[...] = jnp.concatenate([d_mixed, tail], axis=1).astype(BF16)

        def block(slot, carry, h=h):
            rows = slot_rows(k, slot)
            powers = k.powers[h, rows, :]
            slopes = times_transposed(k.values[h, rows, :], k.d_out[...])
            d_scores = (powers.astype(F32) * slopes).astype(BF16)
            k.d_scores[rows, :] = d_scores
            d_k = product(d_scores, k.q_back[h])
            d_v = product(powers, k.d_out[...])
            both = jnp.concatenate([d_k[:, : s.head], d_v[:, : s.head]], axis=1)
            k.d_pair[rows, :] = both
            return carry

        lax.fori_loop(0, 4, block, 0)
        if comm and h == 0:
            project_end(k)
            sum_pass(k, INTO)
        if comm and h == 1:
            sum_end(k, BACK)
        if comm and h == 2:
            sum_share(k, BACK)
            sum_share(k, BACK + 1)
            sum_end(k, INTO)
            sum_pass(k, PROJECT)
        d_q = transposed_times(k.keys[h][:, : s.head], k.d_scores[...]).T * s.head**-0.5
        k.d_joint[h] = jnp.concatenate([d_q, k.d_pair[...]], axis=1).astype(BF16)
        if h == s.here - 2:
            pair = jnp.concatenate([k.d_joint[n] for n in range(h + 1)], axis=1)
            put_blocks(k, JOINT, transposed_times(k.h_one[...].reshape(tall, s.dim), pair))
        if h == s.here - 1:
            put_blocks(k, LAST, transposed_times(k.h_one[...].reshape(tall, s.dim), k.d_joint[h]))
        if comm and h >= s.here - 2:
            sum_start(k, JOINT if h == s.here - 2 else LAST)
        if comm and h == 1:
            sum_end(k, BACK + 1)

    w_joint = k.w_joint[...].reshape(s.dim, 3 * wide)

    def joint_back(slot, rows, columns):
        rows = pl.ds(pl.multiple_of(slot * s.rows + rows.start, 16), rows.size)
        left = jnp.concatenate([k.d_joint[h, rows, :] for h in range(s.here)], axis=1)
        return times_transposed(left, w_joint)

    cuts = row_cuts(s)
    reduce_over_tile(k, k.at.joint, joint_back, cuts)
    unit, scale = layer_norm_parts(k.token_rows[...])
    if comm:
        sum_pass(k, JOINT)
        sum_share(k, INTO)
        sum_end(k, INTO + 1)

    def norm_back(rows, upstream):
        return k.d_rows[rows] + layer_norm_back(unit[rows], scale[rows], k.gains[0:1], upstream)

    own_rows, cls_rows = slice(0, s.own), slice(s.own, s.rows)
    reduced_wait(k, k.at.joint, cuts, (0,))
    table = norm_back(cls_rows, reduced(k, cuts[0][0]))
    table = jnp.where(row_iota(s.slot, s.dim) < s.step, table, 0.0)
    rows = row_iota(s.slot, 128)
    head_rows = jnp.where(rows == s.step, head_row[:, :128], 0.0)
    rest = jnp.concatenate([head_row[:, 128:], jnp.zeros((1, 256 - s.lanes), F32)], axis=1)
    head_rows = jnp.where(rows == s.step + 1, rest, head_rows)
    if comm:
        small_start(k, table, head_rows)
        sum_pass(k, LAST)
        sum_end(k, PROJECT)
        small_end(k)
        sum_share(k, INTO + 1)
        sum_end(k, JOINT)
        sum_share(k, PROJECT)
    reduced_wait(k, k.at.joint, cuts, (1,))
    k.patch_grad[0] = norm_back(own_rows, reduced(k, cuts[1][0]))
    if not comm:
        k.small_out[...] = table
        k.head_out[...] = head_rows
        net.drain()
        return
    sum_end(k, LAST)
    sum_share(k, JOINT)
    for name in range(len(k.grads)):
        sum_close(k, name)
    for slot in (k.ts, k.tx, k.td):
        net.arrived(k.small_sum.at[slot], k.at.small_sum, slot)
    net.drain()


def project_start(k, d_attn):
    s = k.s
    shard = s.dim // s.images
    rows, columns = shard // 2, s.dim // 2
    for m in range(4):
        third = third_rows(s, k.mixed_third[m].astype(F32)).astype(BF16)
        mixed = jnp.concatenate([k.mixed_main[m], third], axis=1)
        value = transposed_times(mixed, d_attn).astype(BF16)
        if not s.img_comm:
            wide = s.here * s.head
            k.d_project[wide * m : wide * (m + 1)] = value
            continue
        for n in range(4):
            for y in range(PLANE):
                first = shard * y + rows * (n // 2)
                cut = value[first : first + rows, columns * (n % 2) :][:, :columns]
                k.p_out[n, PLANE * m + y] = cut
    if s.img_comm:
        k.net.send(k.p_out.at[k.td], k.p_sib.at[1], k.at.project, 1, k.sibling)
        k.net.send(k.p_out.at[k.ts], k.p_sib.at[0], k.at.project, 0, k.sibling)


def project_across(k):
    k.net.arrived(k.p_sib.at[1], k.at.project, 1)
    k.p_stage[...] = (k.p_out[k.tx].astype(F32) + k.p_sib[1].astype(F32)).astype(BF16)
    k.net.send(k.p_stage, k.p_across, k.at.project, 2, k.across)


def project_end(k):
    blocks = k.grads[PROJECT].blocks
    k.net.arrived(k.p_sib.at[0], k.at.project, 0)
    k.net.arrived(k.p_across, k.at.project, 2)
    total = k.p_out[k.t].astype(F32) + k.p_sib[0].astype(F32) + k.p_across[...].astype(F32)
    for i in range(k.s.images):
        blocks[i % PLANE, i // PLANE] = total[i].astype(BF16)
    sum_start(k, PROJECT)


def small_start(k, table, head_rows):
    s = k.s
    shard = s.dim // s.images
    pad = jnp.zeros((s.slot, 128 - shard), F32)
    for n in range(s.images):
        cut = jnp.concatenate([table[:, shard * n : shard * (n + 1)], pad], axis=1)
        k.small_out[n] = (cut + head_rows).astype(BF16)
    for step in range(1, s.images):
        n = (k.i + step) % s.images
        k.net.send(k.small_out.at[n], k.small_in.at[k.i], k.at.small, k.i, (n, k.t))


def small_end(k):
    s = k.s
    total = k.small_out[k.i].astype(F32)
    for step in range(1, s.images):
        n = (k.i + step) % s.images
        k.net.arrived(k.small_in.at[n], k.at.small, n)
        total = total + k.small_in[n].astype(F32)
    k.small_sum[k.t] = total
    for slot in (k.ts, k.tx, k.td):
        k.net.send(k.small_sum.at[k.t], k.small_sum.at[k.t], k.at.small_sum, k.t, (k.i, slot))


def gain_sums(weight, grad):
    return jnp.sum(weight.astype(F32) * grad, axis=1, keepdims=True)


def write_kernel(k):
    s = k.s
    shard = s.dim // s.images
    k.patch_grad[...] = k.patch_rows[...]
    half = s.dim // 2
    for n in range(2):
        k.d_w_back[:, half * n : half * (n + 1)] = k.back[n][...].astype(F32).reshape(4 * shard, half)
    part = s.hidden // s.images
    cut = [jnp.concatenate([ref[n].astype(F32) for ref in k.into], axis=1) for n in range(4)]
    cut = [cut[n][:, part * i : part * (i + 1)] for i in range(s.images) for n in range(4)]
    k.d_w_in[...] = jnp.concatenate(cut, axis=1)
    both = [[k.pair[n].astype(F32), k.last[n].astype(F32)] for n in range(4)]
    split = s.here - 1
    for m in range(3):
        cut = [
            both[n][h // split][:, s.head * (3 * (h % split) + m) :][:, : s.head]
            for n in range(4)
            for h in range(s.here)
        ]
        k.d_w_qkv[:, s.dim * m : s.dim * (m + 1)] = jnp.concatenate(cut, axis=1)
    for n in range(4):
        rows, columns = shard // 2 * (n // 2), half * (n % 2)
        k.d_w_out[rows : rows + shard // 2, columns : columns + half] = k.project[n].astype(F32)
    rows = jnp.concatenate([k.small_sum[n][: s.step] for n in range(4)], axis=0)
    k.d_cls[...] = rows[: s.classes, :shard]
    rest = k.small_sum[0] + k.small_sum[1] + k.small_sum[2] + k.small_sum[3]
    one = gain_sums(k.w_qkv[...], k.d_w_qkv[...])
    two = gain_sums(k.w_in[...], k.d_w_in[...])
    both = jnp.concatenate([one, two, jnp.zeros((shard, 126), F32)], axis=1).T
    k.d_gain_one[...] = both[0:1] / k.gain_one[...].astype(F32)
    k.d_gain_two[...] = both[1:2] / k.gain_two[...].astype(F32)
    head = jnp.concatenate([rest[s.step : s.step + 1], rest[s.step + 1 : s.step + 2]], axis=1)
    k.d_head[...] = head[:, : s.classes]


def tent(pixels, cells, first):
    place = (np.arange(pixels) + 0.5) / UP - 0.5 - first
    return np.maximum(0.0, 1.0 - np.abs(place[:, None] - np.arange(cells)[None, :]))


def band_tables():
    edge = tent(2 * UP, 2, 0)[EDGE : 3 * EDGE]
    edge = np.concatenate([edge[:EDGE], np.zeros((EDGE, 2)), np.zeros((EDGE, 2)), edge[EDGE:]], axis=0)
    edge = edge.reshape(2, 2 * EDGE, 2).transpose(1, 0, 2).reshape(2 * EDGE, BAND_CELLS)
    across = (np.clip((np.arange(WP * UP) + 0.5) / UP - 0.5, 0, WP - 1))[None, :]
    across = np.maximum(0.0, 1.0 - np.abs(across - np.arange(WP)[:, None]))
    down = tent(BAND, BAND_CELLS, -1)
    tables = [across]
    for table in (down, edge):
        rows = table.shape[0]
        up = np.zeros((GROUP, rows, 2, BAND_CELLS, GROUP), np.float32)
        back = np.zeros((BAND_CELLS, GROUP, GROUP, rows), np.float32)
        for c in range(GROUP):
            up[c, :, :, :, c] = table[:, None, :]
            back[:, c, c, :] = table.T
        tables.append(up.reshape(GROUP * rows, 2 * BAND_CELLS * GROUP))
        tables.append(back.reshape(BAND_CELLS * GROUP, GROUP * rows))
    return [jnp.asarray(t, BF16) for t in tables]


def two_parts(value):
    high = value.astype(BF16)
    return high, (value - high.astype(F32)).astype(BF16)


def upsample_kernel(
    classes, bands, height_ref, cell_ref, label_ref, halo_ref, across_ref, up_ref, back_ref,
    edge_up_ref, edge_back_ref, mask_ref, sum_ref, wide, wide_grad, powers,
):
    band = pl.program_id(0)
    groups = -(-classes // GROUP)
    tail = classes - GROUP * (groups - 1)
    cell_rows = cell_ref.shape[0] // WP
    pixels = label_ref.shape[2]
    tile = lax.axis_index(TILE)
    limit = (height_ref[0] - tile * (bands * BAND // UP)) * UP
    share = 1.0 / (UP * UP)
    counts = [GROUP] * (groups - 1) + [tail]

    @pl.when(band == 0)
    def _():
        for r in range(cell_rows):
            wide[r] = lax.dot_general(
                cell_ref[WP * r : WP * (r + 1), :], across_ref[...], (((0,), (0,)), ((), ())),
                preferred_element_type=F32,
            )
        wide_grad[...] = jnp.zeros_like(wide_grad)

    def pixel_rows(rows, label, first, second, up, back, masked):
        def forward(g, total, count):
            at = pl.ds(GROUP * g, GROUP)
            part = jnp.concatenate([wide[pl.ds(r, 2), at, :] for r in (first, second)], axis=0)
            both = jnp.concatenate(two_parts(part.reshape(BAND_CELLS * GROUP, pixels)), axis=0)
            upsampled = product(up[: count * rows, :], both).reshape(count, rows, pixels)
            if masked:
                mask_ref[pl.ds(GROUP * g, count)] = upsampled.astype(BF16)
            power = jnp.exp(upsampled)
            powers[pl.ds(GROUP * g, count), :rows] = power
            return total + jnp.sum(power, axis=0)

        total = jnp.zeros((rows, pixels), F32)
        for g, count in enumerate(counts):
            total = forward(g, total, count)
        inverse = jnp.where(label >= 0, share, 0.0) / total
        for g, count in enumerate(counts):
            parts = []
            for c in range(count):
                target = jnp.where(label == GROUP * g + c, share, 0.0)
                parts.append((powers[GROUP * g + c, :rows] * inverse - target).astype(BF16))
            summed = product(back[:, : count * rows], jnp.concatenate(parts, axis=0))
            summed = summed.reshape(BAND_CELLS, GROUP, pixels)
            at = pl.ds(GROUP * g, GROUP)
            wide_grad[pl.ds(first, 2), at, :] += summed[:2]
            wide_grad[pl.ds(second, 2), at, :] += summed[2:]

    @pl.when(band < bands)
    def _():
        rows = lax.broadcasted_iota(jnp.int32, (BAND, pixels), 0) + BAND * band
        label = jnp.where(rows < limit, label_ref[0], -1)
        first = BAND // UP * band
        pixel_rows(BAND, label, first, first + 2, up_ref, back_ref, True)

    @pl.when(band == bands)
    def _():
        rows = lax.broadcasted_iota(jnp.int32, (2 * EDGE, pixels), 0)
        below = rows >= EDGE
        rows = rows - EDGE + jnp.where(below, bands * BAND, 0)
        label = jnp.where((rows < limit) & (below | (tile > 0)), halo_ref[...], -1)
        pixel_rows(2 * EDGE, label, 0, cell_rows - 2, edge_up_ref, edge_back_ref, False)
        for r in range(cell_rows):
            high, low = two_parts(wide_grad[r])
            sum_ref[WP * r : WP * (r + 1), :] = times_transposed(
                across_ref[...], high
            ) + times_transposed(across_ref[...], low)


def upsampled_loss(cells, labels, halo, heights, classes):
    rows, lanes = cells.shape[0] // WP, cells.shape[1]
    tile_pixels, wide_pixels = labels.shape[1:]
    tables = band_tables()
    bands = tile_pixels // BAND

    def whole(shape):
        return pl.BlockSpec(shape, lambda i: (0,) * len(shape))

    return pl.pallas_call(
        functools.partial(upsample_kernel, classes, bands),
        grid=(bands + 1,),
        out_shape=(
            jax.ShapeDtypeStruct((classes, tile_pixels, wide_pixels), BF16),
            jax.ShapeDtypeStruct(cells.shape, F32),
        ),
        in_specs=[
            pl.BlockSpec(memory_space=pltpu.SMEM),
            whole(cells.shape),
            pl.BlockSpec((1, BAND, wide_pixels), lambda i: (0, jnp.minimum(i, bands - 1), 0)),
            whole(halo.shape),
        ]
        + [whole(t.shape) for t in tables],
        out_specs=(
            pl.BlockSpec((classes, BAND, wide_pixels), lambda i: (0, jnp.minimum(i, bands - 1), 0)),
            whole(cells.shape),
        ),
        scratch_shapes=[
            pltpu.VMEM((rows, lanes, wide_pixels), F32),
            pltpu.VMEM((rows, lanes, wide_pixels), F32),
            pltpu.VMEM((lanes, BAND, wide_pixels), F32),
        ],
        compiler_params=pltpu.CompilerParams(vmem_limit_bytes=56 << 20),
        name=upsample_kernel.__name__,
    )(heights, cells, labels, halo, *tables)


CELLS = "cells"
HALO = "halo"
FAR_INPUTS = ("patches", "labels", "wo", "w_in", "wb")
CARRIED = (
    LOGIT_UNIT,
    LOGIT_SCALE,
    HEAD_GAIN,
    PATCH_UNIT,
    CLASS_UNIT,
    FINAL,
    W_REDUCE,
    SLOPE,
    W_EXPAND,
    ACT,
    H_TWO,
    AFTER,
    GAINS,
    W_PROJECT,
    Q,
    KEYS,
    OUTS,
    VALUES,
    MIXED_MAIN,
    MIXED_THIRD,
    H_ONE,
    W_JOINT,
    TOKEN_ROWS,
)
GRAD_REFS = ("out", "blocks", "from_mate", "from_line")
GRAD_PLACES = ("at_mate", "at_line", "at_out")
Grad = collections.namedtuple("Grad", GRAD_REFS + GRAD_PLACES)


def run_kernel(body, s, inputs, outputs, scratch, recv, sends, number, carried, back=False):
    if back:
        inputs.update({n: inputs.pop(n) for n in carried})
        near = {n: (inputs[n].shape, inputs[n].dtype) for n in carried}
    else:
        near = {n: outputs.pop(n) for n in carried}
        outputs = {**near, **outputs}
    scratch = {**near, **scratch}
    names_in, names_out, names_scratch = list(inputs), list(outputs), list(scratch)

    places = types.SimpleNamespace()
    arrivals = 0
    for name, count in recv.items():
        setattr(places, name, arrivals)
        arrivals += count

    def kernel(*refs):
        k = types.SimpleNamespace(s=s, at=places)
        for name, ref in zip(names_in + names_out + names_scratch, refs):
            setattr(k, name, ref)
        k.far = {}
        for name, ref in zip(carried, refs[len(names_in) - len(carried) :] if back else refs[len(names_in) :]):
            k.far[name] = ref
        for name, ref in zip(carried, refs[len(names_in) + len(names_out) :]):
            setattr(k, name, ref)
        k.send_sem, k.recv_sem, k.carry_sem, k.local_sem = refs[-4:]
        k.net = Net(k)
        k.grads = []
        for n in range(PROJECT + 1):
            of = [getattr(k, word + str(n), None) for word in GRAD_REFS]
            at = [getattr(places, word + str(n), None) for word in GRAD_PLACES]
            k.grads.append(Grad(*of, *at))
        body(k)

    def space(name):
        if name in carried or name in FAR_INPUTS:
            return pl.BlockSpec(memory_space=pl.ANY)
        scalar = name in inputs and inputs[name].dtype == jnp.int32 and inputs[name].ndim == 1
        return pl.BlockSpec(memory_space=pltpu.SMEM if scalar else pltpu.VMEM)

    results = pl.pallas_call(
        kernel,
        out_shape=[jax.ShapeDtypeStruct(*outputs[n]) for n in names_out],
        in_specs=[space(n) for n in names_in],
        out_specs=[space(n) for n in names_out],
        scratch_shapes=[pltpu.VMEM(*scratch[n]) for n in names_scratch]
        + [pltpu.SemaphoreType.DMA((sends,)), pltpu.SemaphoreType.DMA((arrivals,)), pltpu.SemaphoreType.DMA((len(carried),)), pltpu.SemaphoreType.DMA((4,))],
        compiler_params=pltpu.CompilerParams(
            collective_id=number, has_side_effects=True, vmem_limit_bytes=VMEM_BYTES
        ),
        name=body.__name__,
    )(*inputs.values())
    return dict(zip(names_out, results))


def reduce_scratch(s):
    return dict(
        stage=((3, s.rows, s.dim), BF16),
        from_sib=((2, s.rows, s.dim), BF16),
        from_across=((s.rows, s.dim), BF16),
        own_part=((s.rows, s.dim), F32),
        across_part=((s.rows, s.dim), F32),
    )


def forward_call(s, inputs):
    wide = s.here * s.head
    all_rows = 4 * s.rows
    outputs = dict(
        h_one=((4, s.rows, s.dim), BF16),
        q=((s.here, all_rows, 2 * s.head), BF16),
        keys=((s.here, all_rows, 2 * s.head), BF16),
        values=((s.here, all_rows, 2 * s.head), BF16),
        outs=((s.here, all_rows, 2 * s.head), F32),
        mixed_main=((4, s.rows, 2 * s.head), BF16),
        mixed_third=((4, s.pack, 2 * s.head), BF16),
        token_rows=((s.rows, s.dim), F32),
        after=((s.rows, s.dim), F32),
        h_two=((4, s.rows, s.dim), BF16),
        act=((4, s.rows, s.hidden), BF16),
        slope=((4, s.rows, s.hidden), BF16),
        final=((s.rows, s.dim), F32),
        patch_unit=((s.own + 2 * WP, s.dim), BF16),
        head_gain=((8, s.lanes), F32),
        class_unit=((s.lanes, s.dim), BF16),
        logit_unit=((s.own, s.lanes), F32),
        logit_scale=((s.own, 128), F32),
        cells=((s.own + 2 * WP, s.lanes), BF16),
        halo=((2 * EDGE, s.wide_pixels), jnp.int32),
        gains=((8, s.dim), F32),
    )
    scratch = dict(
        tokens=((4, s.own, s.dim), BF16),
        cls_rows=((s.lanes, s.dim), F32),
        mixed=((4, s.rows, wide), BF16),
        third_out=((4, s.pack, 2 * s.head), BF16),
        cls_units=((4, s.slot, s.dim), BF16),
        **reduce_scratch(s),
    )
    recv = dict(tokens=4, mixed=4, third=4, h_two=4, h_second=4, feed=12, units=4, rim=2, halo=2)
    sends = 3 + 6 + 6 + 12 + 3 + 2 + 2
    if s.img_comm:
        shard = s.dim // s.images
        outputs.update(w_joint=((s.images, shard, 3 * wide), BF16))
        outputs.update(w_project=((s.images, shard, s.dim), BF16))
        scratch.update(small=((s.lanes, 128), BF16), wq=((shard, 3 * wide), BF16))
        scratch.update(wi=((shard, s.hidden), BF16), w_in_near=((shard, 4 * s.hidden), BF16))
        outputs.update(w_expand=((s.images, shard, s.hidden), BF16))
        outputs.update(w_reduce=((s.images, shard, s.dim), BF16))
        scratch.update(smalls=((s.images, s.lanes, 128), BF16))
        n = s.images
        recv.update(small=n, joint0=n, joint1=n, w_project=n, w_shared=4)
        recv.update(expand0=n, expand1=n, reduce0=n, reduce1=n)
        sends += 2 * (n // PLANE) - 1 + 7 * (4 * (n // PLANE) - 3) + 3
    carried = [n for n in CARRIED if n in outputs]
    return run_kernel(forward_kernel, s, inputs, outputs, scratch, recv, sends, 1, carried)


def backward_call(s, inputs, carried):
    wide = s.here * s.head
    all_rows = 4 * s.rows
    outputs = dict(patch_grad=((1, s.own, s.dim), F32))
    scratch = dict(
        class_out=((4, s.slot, s.dim), BF16),
        class_in=((4, s.slot, s.dim), BF16),
        d_rows=((s.rows, s.dim), F32),
        d_branch=((4, s.rows, s.dim), BF16),
        d_pre=((4, s.rows, s.hidden), BF16),
        main_out=((4, s.rows, 2 * s.head), BF16),
        main_in=((4, s.rows, 2 * s.head), BF16),
        third_out=((4, s.pack, 2 * s.head), BF16),
        third_in=((4, s.pack, 2 * s.head), BF16),
        powers=((s.here, all_rows, all_rows), BF16),
        d_scores=((all_rows, all_rows), BF16),
        d_out=((all_rows, 2 * s.head), BF16),
        q_back=((s.here, all_rows, 2 * s.head), BF16),
        d_pair=((all_rows, 2 * s.head), F32),
        d_joint=((s.here, all_rows, 3 * s.head), BF16),
        **reduce_scratch(s),
    )
    recv = dict(class_=4, d_branch=4, d_first=4, d_class=4, feed=6, d_mixed=4, third=4, joint=6)
    sends = 3 + 3 + 3 + 3 + 6 + 6 + 6
    columns = [s.dim // 2] * 2 + [s.hidden // 2] * 2 + [3 * s.head * (s.here - 1), 3 * s.head]
    columns += [s.dim // 2] * s.img_comm
    planes, shard = s.images // PLANE, s.dim // s.images
    for n, cols in enumerate(columns):
        out, blocks, from_mate, from_line = [word + str(n) for word in GRAD_REFS]
        at_mate, at_line, at_out = [word + str(n) for word in GRAD_PLACES]
        if not s.img_comm:
            outputs[out] = ((s.dim, cols), BF16)
            continue
        rows = shard // 2 if n == PROJECT else shard
        outputs[out] = ((4, rows, cols), BF16)
        scratch[blocks] = ((PLANE, planes, rows, cols), BF16)
        for what in (from_mate, from_line):
            scratch[what] = ((planes, rows, cols), BF16)
        recv[at_mate] = 1
        recv[at_line] = planes
        recv[at_out] = 4
        sends += 1 + planes - 1 + 3
    if s.img_comm:
        outputs.update(small_sum=((4, s.slot, 128), F32))
        piece = (s.images, shard // 2, s.dim // 2)
        scratch.update(p_out=((4, *piece), BF16), p_sib=((2, *piece), BF16))
        scratch.update(p_across=(piece, BF16), p_stage=(piece, BF16))
        scratch.update(small_out=((s.images, s.slot, 128), BF16))
        scratch.update(small_in=((s.images, s.slot, 128), BF16))
        recv.update(project=3, small=s.images, small_sum=4)
        sends += 3 + s.images - 1 + 3
    else:
        outputs.update(d_project=((s.dim, s.dim), BF16))
        outputs.update(small_out=((s.slot, s.dim), F32))
        outputs.update(head_out=((s.slot, 128), F32))
    return run_kernel(backward_kernel, s, inputs, outputs, scratch, recv, sends, 2, carried, True)


def write_call(s, grads, pieces, raw):
    shard = s.dim // s.images
    outputs = dict(
        patch_grad=((1, s.own, s.dim), F32),
        d_w_back=((4 * shard, s.dim), F32),
        d_w_in=((shard, 4 * s.hidden), F32),
        d_w_qkv=((shard, 3 * s.dim), F32),
        d_w_out=((shard, s.dim), F32),
        d_cls=((s.classes, shard), F32),
        d_gain_one=((1, shard), F32),
        d_gain_two=((1, shard), F32),
        d_head=((1, s.classes), F32),
    )
    inputs = dict(patch_rows=grads.patch_grad, project=pieces[PROJECT], small_sum=grads.small_sum)
    inputs.update(back0=pieces[0], back1=pieces[1], into0=pieces[2], into1=pieces[3])
    inputs.update(pair=pieces[JOINT], last=pieces[LAST], **raw)

    def kernel(*refs):
        k = types.SimpleNamespace(s=s, **dict(zip(list(inputs) + list(outputs), refs)))
        k.back, k.into = (k.back0, k.back1), (k.into0, k.into1)
        write_kernel(k)

    whole = pl.BlockSpec(memory_space=pltpu.VMEM)
    results = pl.pallas_call(
        kernel,
        out_shape=[jax.ShapeDtypeStruct(*v) for v in outputs.values()],
        in_specs=[whole] * len(inputs),
        out_specs=[whole] * len(outputs),
        compiler_params=pltpu.CompilerParams(vmem_limit_bytes=VMEM_BYTES),
        name=write_kernel.__name__,
    )(*inputs.values())
    return types.SimpleNamespace(**dict(zip(outputs, results)))


def sizes(patches, cls_emb, w_joint, w_back, head_gain):
    images, tiles = lax.axis_size(IMG), lax.axis_size(TILE)
    s = types.SimpleNamespace(images=images, tiles=tiles)
    s.dim = patches.shape[2]
    s.own = patches.shape[1]
    s.grid = s.own // WP
    s.wide_pixels = WP * UP
    s.classes = head_gain.shape[0]
    s.step = -(-s.classes // (8 * tiles)) * 8
    s.slot = -(-s.step // 16) * 16
    s.lanes = s.step * tiles
    s.rows = s.own + s.slot
    s.pack = -(-s.rows // 32) * 16
    s.head = s.dim // HEADS
    s.here = HEADS // tiles
    s.hidden = w_back.shape[0] * images // tiles
    shard = w_joint.shape[0]
    s.img_comm = images == PLANE * tiles and shard % 16 == 0 and shard <= 128
    return s


def shards(
    patches, labels, heights, cls_emb, gain_one, w_qkv, w_out, gain_two, w_in, w_back, head_gain
):
    s = sizes(patches, cls_emb, w_qkv, w_back, head_gain)
    t = lax.axis_index(TILE)
    shard = w_qkv.shape[0]
    wide = s.here * s.head

    part = w_back.shape[0] // s.tiles
    w_back = w_back.reshape(s.tiles, part, s.dim)
    cls_emb, gain_one, gain_two = cls_emb, gain_one[None], gain_two[None]
    inputs = dict(patches=patches, labels=labels, height=heights, gain_row=head_gain)
    common = {}
    if s.img_comm:
        inputs.update(cls_emb=cls_emb, gain_one=gain_one, gain_two=gain_two)
        inputs.update(w_qkv=w_qkv, wo=w_out, w_in=w_in, wb=w_back)
    else:

        def gather(value, axis=0):
            return lax.all_gather(value, IMG, axis=axis, tiled=True)

        def pick(value, axis):
            return lax.dynamic_index_in_dim(value, t, axis, keepdims=False)

        joint = pick(w_qkv.reshape(shard, 3, s.tiles, s.here, s.head), 2)
        joint = joint.transpose(0, 2, 1, 3).reshape(shard, 3 * wide)
        expand = pick(w_in.reshape(shard, s.images, s.tiles, part), 2).reshape(shard, s.hidden)
        reduce = pick(w_back, 0)
        small = jnp.concatenate([cls_emb, gain_one, gain_two], axis=0)
        small = jnp.pad(small, ((0, s.lanes - small.shape[0]), (0, 0)))
        common.update(
            w_joint=gather(joint)[None],
            w_project=gather(w_out)[None],
            w_expand=gather(expand)[None],
            w_reduce=gather(reduce)[None],
        )
        inputs.update(small_full=gather(small, 1), **common)
    arrays = forward_call(s, inputs)
    cells, halo = arrays.pop(CELLS), arrays.pop(HALO)
    masks, cell_sums = upsampled_loss(cells, labels, halo, heights, s.classes)
    carried = [n for n in CARRIED if n in arrays]
    grads = backward_call(s, dict(**arrays, **common, cell_sums=cell_sums), carried)
    grads = types.SimpleNamespace(**grads)
    count = PROJECT + 1 if s.img_comm else PROJECT
    pieces = [getattr(grads, GRAD_REFS[0] + str(n)) for n in range(count)]
    if s.img_comm:
        raw = dict(w_qkv=w_qkv, w_in=w_in, gain_one=gain_one, gain_two=gain_two)
        written = write_call(s, grads, pieces, raw)
        return (
            masks[None],
            written.patch_grad,
            written.d_cls,
            written.d_gain_one[0],
            written.d_w_qkv,
            written.d_w_out,
            written.d_gain_two[0],
            written.d_w_in,
            written.d_w_back,
            written.d_head[0],
        )

    def across(value):
        return lax.all_gather(value, TILE, axis=0, tiled=False)

    def total(value, axis=0):
        return lax.psum_scatter(value, IMG, scatter_dimension=axis, tiled=True)

    pieces = [across(total(v)) for v in pieces]
    back, into = [jnp.concatenate(pieces[n : n + 2], axis=2) for n in (BACK, INTO)]
    project = total(lax.psum(grads.d_project, TILE))
    small = across(total(grads.small_out, 1))
    head_rows = across(lax.psum(grads.head_out, IMG))
    joint = jnp.concatenate(pieces[JOINT:], axis=2)
    joint = joint.reshape(s.tiles, shard, s.here, 3, s.head).transpose(1, 3, 0, 2, 4)
    joint = joint.reshape(shard, -1).astype(F32)
    expand = into.reshape(s.tiles, shard, s.images, part).transpose(1, 2, 0, 3)
    expand = expand.reshape(shard, -1).astype(F32)
    cls_grad = small[:, : s.step, :shard].reshape(s.lanes, shard)[: s.classes]
    head_grad = jnp.sum(head_rows[:, s.step : s.step + 2, :128], axis=0).reshape(-1)[: s.classes]
    return (
        masks[None],
        grads.patch_grad,
        cls_grad,
        gain_sums(w_qkv, joint)[:, 0] / gain_one[0].astype(F32),
        joint,
        project.astype(F32),
        gain_sums(w_in, expand)[:, 0] / gain_two[0].astype(F32),
        expand,
        back.reshape(-1, s.dim).astype(F32),
        head_grad,
    )


def solution(mesh):
    in_specs = (
        P(IMG, TILE, None),
        P(IMG, TILE, None),
        P(IMG),
        P(None, IMG),
        P(IMG),
        P(IMG, None),
        P(IMG, None),
        P(IMG),
        P(IMG, None),
        P(IMG, None),
        P(),
    )
    out_specs = (
        P(IMG, None, TILE, None),
        P(IMG, TILE, None),
        P(None, IMG),
        P(IMG),
        P(IMG, None),
        P(IMG, None),
        P(IMG),
        P(IMG, None),
        P(IMG, None),
        P(),
    )
    return jax.shard_map(shards, mesh=mesh, in_specs=in_specs, out_specs=out_specs, check_vma=False)
```
